32 devices in a mesh: dp: 4 (over y, x), seq: 8 (over z, core).
Axes of the slice: x: 2, y: 2, z: 4, core: 2. Of those that a mesh axis runs over, the one named last changes fastest.
Arguments:
- queries: bfloat16 [4, 192, 2048], P('dp', 'seq'), may hold values from -18 to 18
- keys: bfloat16 [4, 2048, 2048], P('dp', 'seq'), may hold values from -18 to 18
- values: bfloat16 [4, 2048, 2048], P('dp', 'seq'), may hold values from -6 to 6
- attn_out: bfloat16 [4, 192, 2048], P('dp', 'seq'), may hold values from -3 to 3
- out_grad: bfloat16 [4, 192, 2048], P('dp', 'seq'), may hold values from -12 to 12
- loss_mask: int32 [4, 192], P('dp', 'seq'), may hold values from 0 to 1, as said below
- input_lengths: int32 [4, 1, 4], P('dp'), may hold values from 1 to 1024, 2048 in all within a row
- target_lengths: int32 [4, 1, 4], P('dp'), may hold values from 1 to 96, 192 in all within a row
Outputs:
- grad_queries: bfloat16 [4, 192, 2048], P('dp', 'seq')
- grad_keys: bfloat16 [4, 2048, 2048], P('dp', 'seq')
- grad_values: bfloat16 [4, 2048, 2048], P('dp', 'seq')
The draws below stay inside these ranges and needn't reach their ends.
Inputs may be any that keep to these rules, and one draw needn't show every extreme that they name: `loss_mask`: the first of each device's 24 target rows carries loss.
All inputs are finite; a program needn't handle non-finite values.
Results may differ from the reference program's by a relative error of at most 0.0095.
Values may be sent and summed in bfloat16 or wider, within the bound.
No kernel may reach another device: no remote copies, remote signals or barrier semaphores. Data moves between devices by JAX's collectives and lax.ppermute only.
A program may use at most 128 MiB of HBM per device.

```python
import math
import jax
import jax.numpy as jnp
import numpy as np
from jax import lax

HEADS = 8
HEAD_SIZE = 256
FEATURES = 2048
ENC_DEV = 256
DEC_DEV = 24
BLOCK = 8
DOCS = 4
BLOCKS = 1
ENC_ROWS = 2048
DEC_ROWS = 192
MOST_IN = 1024
MOST_OUT = 96
N_DP = 4


def draw_queries(key, part):
    key = jax.random.fold_in(key, 11)
    full_shape = (N_DP, DEC_ROWS, HEADS * HEAD_SIZE)
    drawn_values = jnp.clip(jax.random.normal(key, full_shape, jnp.float32), -6.0, 6.0)
    return drawn_values.astype(jnp.bfloat16)


def draw_keys(key, part):
    key = jax.random.fold_in(key, 13)
    full_shape = (N_DP, ENC_ROWS, HEADS * HEAD_SIZE)
    drawn_values = jnp.clip(jax.random.normal(key, full_shape, jnp.float32), -6.0, 6.0)
    return drawn_values.astype(jnp.bfloat16)


def draw_loss_mask(key, part):
    key = jax.random.fold_in(key, 23)
    per_group = DEC_ROWS // DEC_DEV
    device_count = N_DP * per_group
    row_index = lax.broadcasted_iota(jnp.int32, (N_DP, DEC_ROWS), 1)
    group_index = lax.broadcasted_iota(jnp.int32, (N_DP, DEC_ROWS), 0)
    device_index = group_index * per_group + row_index // DEC_DEV
    threshold = 250 + 500 * device_index // max(device_count - 1, 1)
    drawn_values = jax.random.randint(key, (N_DP, DEC_ROWS), 0, 1000)
    carries = (drawn_values < threshold) | (row_index % DEC_DEV == 0)
    return jnp.where(carries, 1, 0).astype(jnp.int32)


def block_levels(own_key, dims, cuts, smallest, high):
    loudness, own = 1.0, jax.random.fold_in(own_key, 6)
    for position, shards_of in cuts:
        heights = jnp.exp(jax.random.uniform(jax.random.fold_in(own, position), (shards_of,), jnp.float32, smallest / len(cuts), high / len(cuts)))
        loudness = loudness * jnp.repeat(heights, dims[position] // shards_of).reshape([-1 if axis == position else 1 for axis in range(len(dims))])
    return loudness


def split_up(count, total, limit, skew):
    portions = [(1 << 20) // math.isqrt(standing ** skew) + 1 for standing in range(2, count + 1)]
    rest, given = total - limit - (count - 1), [1] * (count - 1)
    while rest > 0:
        candidates = [i for i in range(count - 1) if given[i] < limit]
        whole, remaining = sum([portions[i] for i in candidates]), rest
        for i in candidates:
            addition = min(limit - given[i], max(1, remaining * portions[i] // whole), rest)
            given[i] = given[i] + addition
            rest = rest - addition
    return np.array([limit] + given)


def uneven_parts(rng, number_of, total, most, lean):
    if number_of == 2:
        one = jax.random.randint(rng, (), max(1, total - most), min(most, total - 1) + 1)
        return jnp.stack([one, total - one])
    sizes = jnp.asarray(split_up(number_of, total, most, lean), jnp.int32)
    couples = (number_of - 1) // 2
    donor, receiver = sizes[1:1 + 2 * couples:2], sizes[2:2 + 2 * couples:2]
    room = jnp.minimum(donor - 1, most - receiver)
    moved = jax.random.randint(jax.random.fold_in(rng, 1), (couples,), 0, 1 << 20) % (room + 1)
    sizes = sizes.at[1:1 + 2 * couples:2].set(donor - moved).at[2:2 + 2 * couples:2].set(receiver + moved)
    return sizes[jax.random.permutation(jax.random.fold_in(rng, 2), number_of)]


def normal_values(stream_key, shape, deviation, most, pieces=(), held_as=jnp.bfloat16):
    array = jax.random.normal(stream_key, shape, jnp.float32) * deviation
    if len(pieces) > 0:
        array = block_levels(stream_key, shape, pieces, -0.22, 0.18) * array
    return jnp.clip(array, min=-most, max=most).astype(held_as)


def setup_inputs(seed: int = 0) -> dict:
    streams_of = jax.random.split(jax.random.key(seed), 9)
    queries = draw_queries(jax.random.fold_in(streams_of[8], 71), 0)
    keys = draw_keys(jax.random.fold_in(streams_of[8], 71), 0)
    values = normal_values(streams_of[2], (N_DP, ENC_ROWS, FEATURES), 1.0, 6.0, ((0, 4), (1, 8)))
    attn_out = normal_values(streams_of[3], (N_DP, DEC_ROWS, FEATURES), 0.5, 3.0, ((0, 4), (1, 8)))
    out_grad = normal_values(streams_of[4], (N_DP, DEC_ROWS, FEATURES), 2.0, 12.0, ((0, 4), (1, 8)))
    loss_mask = draw_loss_mask(jax.random.fold_in(streams_of[8], 71), 0)
    input_lengths = jax.vmap(lambda own: uneven_parts(own, DOCS, BLOCK * ENC_DEV, MOST_IN, 2))(jax.random.split(streams_of[6], N_DP * BLOCKS)).reshape((N_DP, BLOCKS, DOCS)).astype(jnp.int32)
    target_lengths = jax.vmap(lambda own: uneven_parts(own, DOCS, BLOCK * DEC_DEV, MOST_OUT, 2))(jax.random.split(streams_of[7], N_DP * BLOCKS)).reshape((N_DP, BLOCKS, DOCS)).astype(jnp.int32)
    return {"queries": queries, "keys": keys, "values": values, "attn_out": attn_out, "out_grad": out_grad, "loss_mask": loss_mask, "input_lengths": input_lengths, "target_lengths": target_lengths}


def document_ids(lengths, positions):
    doc_ends = jnp.cumsum(lengths)
    return jnp.sum((positions[:, None] >= doc_ends[None, :]).astype(jnp.int32), axis=1)


def block_grads(block_inputs):
    query_rows, key_rows, value_rows, grad_rows, delta_rows, input_lens, target_lens = block_inputs
    dec_count = query_rows.shape[0]
    enc_count = key_rows.shape[0]
    enc_doc = document_ids(input_lens, jnp.arange(enc_count, dtype=jnp.int32))
    dec_doc = document_ids(target_lens, jnp.arange(dec_count, dtype=jnp.int32))
    allowed = dec_doc[:, None] == enc_doc[None, :]
    inverse_root = HEAD_SIZE ** -0.5
    query_heads = query_rows.astype(jnp.float32).reshape(dec_count, HEADS, HEAD_SIZE)
    key_heads = key_rows.astype(jnp.float32).reshape(enc_count, HEADS, HEAD_SIZE)
    value_heads = value_rows.astype(jnp.float32).reshape(enc_count, HEADS, HEAD_SIZE)
    grad_heads = grad_rows.astype(jnp.float32).reshape(dec_count, HEADS, HEAD_SIZE)
    scores = jnp.einsum('rhd,ehd->hre', query_heads, key_heads) * inverse_root
    masked_scores = jnp.where(allowed[None], scores, -1e30)
    row_top = jnp.max(masked_scores, axis=2)
    row_total = jnp.sum(jnp.where(allowed[None], jnp.exp(scores - row_top[:, :, None]), 0.0), axis=2)
    log_total = row_top + jnp.log(row_total)
    probs = jnp.where(allowed[None], jnp.exp(scores - log_total[:, :, None]), 0.0)
    dprob = jnp.einsum('rhd,ehd->hre', grad_heads, value_heads)
    dscore = probs * (dprob - delta_rows.astype(jnp.float32).T[:, :, None])
    probs_low = probs.astype(jnp.bfloat16).astype(jnp.float32)
    dscore_low = dscore.astype(jnp.bfloat16).astype(jnp.float32)
    dvalue = jnp.einsum('hre,rhd->ehd', probs_low, grad_heads).reshape(enc_count, HEADS * HEAD_SIZE)
    dkey = jnp.einsum('hre,rhd->ehd', dscore_low, query_heads).reshape(enc_count, HEADS * HEAD_SIZE) * inverse_root
    dquery = jnp.einsum('hre,ehd->rhd', dscore_low, key_heads).reshape(dec_count, HEADS * HEAD_SIZE) * inverse_root
    return dquery, dkey, dvalue


def reference(queries, keys, values, attn_out, out_grad, loss_mask, input_lengths, target_lengths):
    features = HEADS * HEAD_SIZE
    masked = out_grad * loss_mask[:, :, None].astype(jnp.bfloat16)
    delta = jnp.sum((masked.astype(jnp.float32) * attn_out.astype(jnp.float32)).reshape(N_DP, DEC_ROWS, HEADS, HEAD_SIZE), axis=3).astype(jnp.bfloat16)
    count = jnp.sum(loss_mask).astype(jnp.float32)
    factor = jnp.float32(N_DP * DEC_ROWS) / count
    block_count = N_DP * BLOCKS
    dec_block = BLOCK * DEC_DEV
    enc_block = BLOCK * ENC_DEV
    stacked = (queries.reshape(block_count, dec_block, features),
               keys.reshape(block_count, enc_block, features),
               values.reshape(block_count, enc_block, features),
               masked.reshape(block_count, dec_block, features),
               delta.reshape(block_count, dec_block, HEADS),
               input_lengths.reshape(block_count, DOCS),
               target_lengths.reshape(block_count, DOCS))
    dquery, dkey, dvalue = lax.map(block_grads, stacked)
    grad_queries = (factor * dquery).astype(jnp.bfloat16).reshape(N_DP, DEC_ROWS, features)
    grad_keys = (factor * dkey).astype(jnp.bfloat16).reshape(N_DP, ENC_ROWS, features)
    grad_values = (factor * dvalue).astype(jnp.bfloat16).reshape(N_DP, ENC_ROWS, features)
    return grad_queries, grad_keys, grad_values
```

```python
import functools
import jax
import jax.numpy as jnp
from jax import lax
from jax.experimental import pallas as pl
from jax.experimental.pallas import tpu as pltpu
from jax.sharding import PartitionSpec as P

HEADS = 8
HEAD_SIZE = 256
HALF_HEADS = HEADS // 2
HALF = HALF_HEADS * HEAD_SIZE
EXTRA = 128
ROOT = HEAD_SIZE**-0.5
NEVER = -1e30
VMEM_LIMIT = 24 * 1024 * 1024
F32 = jnp.float32
BF16 = jnp.bfloat16
ANY = pl.BlockSpec(memory_space=pl.ANY)
VMEM = pl.BlockSpec(memory_space=pltpu.VMEM)
SMEM = pl.BlockSpec(memory_space=pltpu.SMEM)
NT = (((1,), (1,)), ((), ()))
TN = (((0,), (0,)), ((), ()))
NN = (((1,), (0,)), ((), ()))


def dot(a, b, dims):
    return lax.dot_general(a, b, dims, preferred_element_type=F32)


def position():
    me = lax.axis_index("seq")
    return me >> 1, me & 1


def to_sibling(block):
    count = lax.axis_size("seq")
    return lax.ppermute(block, "seq", [(i, i ^ 1) for i in range(count)])


def across(block, apart):
    count = lax.axis_size("seq")
    return lax.ppermute(block, "seq", [(i, i ^ (2 * apart)) for i in range(count)])


def after(block, *others):
    return lax.optimization_barrier((block, *others))


def kernel_call(
    body, out_shape, in_specs, out_specs, scratch, flops, moved, name, vmem_limit=VMEM_LIMIT
):
    return pl.pallas_call(
        body,
        out_shape=out_shape,
        in_specs=in_specs,
        out_specs=out_specs,
        scratch_shapes=scratch,
        compiler_params=pltpu.CompilerParams(vmem_limit_bytes=vmem_limit),
        cost_estimate=pl.CostEstimate(flops=flops, bytes_accessed=moved, transcendentals=0),
        name=name,
    )


def prepare_kernel(
    grad_ref, out_ref, mask_ref, send_ref, keep_ref, grad_held, out_held, mask_held, sems
):
    _, core = position()
    rows = grad_ref.shape[0]
    copies = start_all(
        [(mask_ref, mask_held), (grad_ref, grad_held), (out_ref, out_held)], sems
    )
    copies[0].wait()
    mask_row = mask_held[...].astype(F32)
    here = lax.broadcasted_iota(jnp.int32, (rows, rows), 0) == lax.broadcasted_iota(
        jnp.int32, (rows, rows), 1
    )
    mask = jnp.sum(jnp.where(here, mask_row, 0.0), axis=1, keepdims=True)
    lane = lax.broadcasted_iota(jnp.int32, (rows, EXTRA), 1)
    for copy in copies[1:]:
        copy.wait()
    masked = grad_held[...].astype(F32) * mask
    products = masked * out_held[...].astype(F32)
    grad_held[...] = masked.astype(BF16)
    halves = []
    for half in range(2):
        extra = jnp.where(lane == HALF_HEADS, mask, 0.0)
        for head in range(HALF_HEADS):
            first = half * HALF + head * HEAD_SIZE
            delta = jnp.sum(products[:, first : first + HEAD_SIZE], axis=1, keepdims=True)
            extra = jnp.where(lane == head, delta, extra)
        halves.append(extra)
    for ref, half in ((send_ref, 1 - core), (keep_ref, core)):
        ref[:, :HALF] = grad_held[:, pl.ds(pl.multiple_of(half * HALF, HALF), HALF)]
        ref[:, HALF:] = jnp.where(half == 0, halves[0], halves[1]).astype(BF16)


def in_core_order(own, other, core):
    own, other = own.astype(F32), other.astype(F32)
    joined = jnp.where(
        core == 0, jnp.concatenate([own, other], 0), jnp.concatenate([other, own], 0)
    )
    return joined.astype(BF16)


def join_queries_kernel(own_ref, other_ref, joined_ref):
    _, core = position()
    mine = pl.ds(pl.multiple_of(core * HALF, HALF), HALF)
    joined_ref[...] = in_core_order(own_ref[:, mine], other_ref[:, mine], core)


def join_cotangents_kernel(own_ref, other_ref, joined_ref, delta_ref, count_ref):
    _, core = position()
    joined_ref[...] = in_core_order(own_ref[:, :HALF], other_ref[:, :HALF], core)
    extra = jnp.transpose(in_core_order(own_ref[:, HALF:], other_ref[:, HALF:], core).astype(F32))
    delta_ref[...] = extra[: delta_ref.shape[0]]
    count = jnp.sum(extra[HALF_HEADS : HALF_HEADS + 1], axis=1, keepdims=True)
    count_ref[...] = jnp.broadcast_to(count, count_ref.shape)


def document_of(positions, lengths_ref):
    end = 0
    document = jnp.zeros_like(positions)
    for i in range(lengths_ref.shape[1]):
        end = end + lengths_ref[0, i]
        document += (positions >= end).astype(jnp.int32)
    return document


def setup_kernel(offsets, in_ref, target_ref, key_ref, k_ref, bias_own, bias_other):
    chip, core = position()
    mine = pl.ds(pl.multiple_of(core * HALF, HALF), HALF)
    k_ref[...] = key_ref[:, mine]
    enc_rows, dec_rows = bias_own.shape
    block = dec_rows // len(offsets)
    lane = lax.broadcasted_iota(jnp.int32, (1, dec_rows), 1)
    dec = lane + chip * block
    for j, offset in enumerate(offsets[1:], 1):
        dec = jnp.where(lane >= j * block, lane + ((chip ^ offset) - j) * block, dec)
    dec = document_of(dec, target_ref)
    for ref, side in ((bias_own, core), (bias_other, 1 - core)):
        enc = lax.broadcasted_iota(jnp.int32, (enc_rows, 1), 0) + (2 * chip + side) * enc_rows
        ref[...] = jnp.where(document_of(enc, in_ref) == dec, 0.0, NEVER)


def start_all(pairs, sems):
    copies = [pltpu.make_async_copy(a, b, sems.at[i]) for i, (a, b) in enumerate(pairs)]
    for copy in copies:
        copy.start()
    return copies


def rows_of(blocks, head):
    columns = slice(head * HEAD_SIZE, (head + 1) * HEAD_SIZE)
    return jnp.concatenate([block[:, columns] for block in blocks], 0)


def tile_of(ref, head):
    first = head * HEAD_SIZE
    if ref.shape[1] == HALF:
        return ref[:, first : first + HEAD_SIZE]
    _, core = position()
    return ref[:, pl.ds(pl.multiple_of(core * HALF + first, HEAD_SIZE), HEAD_SIZE)]


def scores_kernel(offsets, delta_ref, bias_own, bias_other, key_ref, other_ref, *refs):
    count_ref, refs = refs[0], refs[1:]
    blocks, (stats_ref,) = refs[: len(offsets)], refs[len(offsets) :]
    rows = blocks[0].shape[0]
    dec_rows = rows * len(offsets)
    stats_ref[...] = jnp.broadcast_to(count_ref[0:1, 0:1], stats_ref.shape)
    stats_ref[HALF_HEADS:, :rows] = delta_ref[:HALF_HEADS]
    for head in range(HALF_HEADS):
        q = rows_of(blocks, head)
        scores = [
            dot(tile_of(k, head), q, NT) * ROOT + bias[...]
            for k, bias in ((key_ref, bias_own), (other_ref, bias_other))
        ]
        top = functools.reduce(jnp.maximum, [jnp.max(s, axis=0, keepdims=True) for s in scores])
        top = jnp.maximum(top, -1e20)
        total = sum(jnp.sum(jnp.exp(s - top), axis=0, keepdims=True) for s in scores)
        stats_ref[head : head + 1, :dec_rows] = jnp.where(
            total > 0, top + jnp.log(jnp.maximum(total, 1e-30)), NEVER
        )


def gathered_stats(offsets, stats, rows):
    logs = []
    for sender, ref in zip(offsets, stats):
        order = [offsets.index(offset ^ sender) for offset in offsets]
        logs.append(
            jnp.concatenate([ref[:HALF_HEADS, j * rows : (j + 1) * rows] for j in order], 1)
        )
    top = functools.reduce(jnp.maximum, logs)
    log_total = top + jnp.log(sum(jnp.exp(log - top) for log in logs))
    delta = jnp.concatenate([ref[HALF_HEADS:, :rows] for ref in stats], 1)
    last = stats[0].shape[1] - 1
    return log_total, delta, sum(ref[0:1, last:] for ref in stats)


def grads_kernel(offsets, bias_own, bias_other, *refs):
    chips = len(offsets)
    stats, refs = refs[:chips], refs[chips:]
    q_blocks, refs = refs[:chips], refs[chips:]
    g_blocks, refs = refs[:chips], refs[chips:]
    (key_ref, key_other, value_ref, value_other), refs = refs[:4], refs[4:]
    dq_blocks, (keep_ref, send_ref, count_ref) = refs[:chips], refs[chips:]
    rows = q_blocks[0].shape[0]
    log_total, delta, count = gathered_stats(offsets, stats, rows)
    count_ref[...] = jnp.broadcast_to(count, count_ref.shape)
    for head in range(HALF_HEADS):
        columns = slice(head * HEAD_SIZE, (head + 1) * HEAD_SIZE)
        value_columns = slice(HALF + columns.start, HALF + columns.stop)
        line = slice(head, head + 1)
        q, g = rows_of(q_blocks, head), rows_of(g_blocks, head)
        dq = 0.0
        for key, value, bias, out_ref in (
            (key_ref, value_ref, bias_own, keep_ref),
            (key_other, value_other, bias_other, send_ref),
        ):
            k, v = tile_of(key, head), tile_of(value, head)
            probs = jnp.exp(dot(k, q, NT) * ROOT + bias[...] - log_total[line])
            dscore = (probs * (dot(v, g, NT) - delta[line])).astype(BF16)
            dq += dot(dscore, k, TN)
            out_ref[:, columns] = (dot(dscore, q, NN) * ROOT).astype(BF16)
            out_ref[:, value_columns] = dot(probs.astype(BF16), g, NN).astype(BF16)
        dq = (dq * ROOT).astype(BF16)
        for j, block in enumerate(dq_blocks):
            block[:, columns] = dq[j * rows : (j + 1) * rows]


def key_end_kernel(rows_in_all, keep_ref, other_ref, *refs):
    counts, (dk_ref, dv_ref, factor_ref) = refs[:2], refs[2:]
    _, core = position()
    factor = rows_in_all / (counts[0][0:1, 0:1] + counts[1][0:1, 0:1])
    factor_ref[...] = jnp.broadcast_to(factor, factor_ref.shape)
    for ref, side in ((keep_ref, core), (other_ref, 1 - core)):
        columns = pl.ds(pl.multiple_of(side * HALF, HALF), HALF)
        dk_ref[:, columns] = (ref[:, :HALF].astype(F32) * factor).astype(BF16)
        dv_ref[:, columns] = (ref[:, HALF:].astype(F32) * factor).astype(BF16)


def query_end_kernel(factor_ref, *refs):
    parts, (send_ref, keep_ref) = refs[:-2], refs[-2:]
    _, core = position()
    summed = factor_ref[0:1, 0:1] * sum(part[...].astype(F32) for part in parts)
    half = summed.shape[0] // 2
    low, high = summed[:half], summed[half:]
    send_ref[...] = jnp.where(core == 0, high, low).astype(BF16)
    keep_ref[...] = jnp.where(core == 0, low, high).astype(BF16)


def in_order(own, other, core, axis):
    return jnp.where(
        core == 0, jnp.concatenate([own, other], axis), jnp.concatenate([other, own], axis)
    )


def local(queries, keys, values, attn_out, out_grad, loss_mask, input_lengths, target_lengths):
    query_rows, key_rows, value_rows = queries[0], keys[0], values[0]
    dec_local, enc_local = query_rows.shape[0], key_rows.shape[0]
    chips = lax.axis_size("seq") // 2
    data_groups = lax.axis_size("dp")
    _, core = position()
    dec_rows = 2 * chips * dec_local
    enc_rows = 2 * enc_local
    block = (2 * dec_local, HALF)
    lengths = (input_lengths[0], target_lengths[0])

    def shaped(*shape, dtype=BF16):
        return jax.ShapeDtypeStruct(shape, dtype)

    def gather(block):
        blocks = [block]
        apart = chips // 2
        while apart > 1:
            blocks += [across(one, apart) for one in blocks]
            apart //= 2
        return blocks, across(block, 1)

    def forwarded(blocks):
        return [across(one, 1) for one in blocks[1:]]

    offsets = [0]
    apart = chips // 2
    while apart:
        offsets += [offset ^ apart for offset in offsets]
        apart //= 2

    features = HEADS * HEAD_SIZE
    sent = shaped(dec_local, HALF + EXTRA)
    block = shaped(2 * dec_local, HALF)

    with jax.named_scope("sibling_exchange"):
        q_recv = to_sibling(query_rows)
        g_send, g_keep = kernel_call(
            prepare_kernel,
            (sent, sent),
            [ANY] * 3,
            (VMEM, VMEM),
            [
                pltpu.VMEM((dec_local, features), BF16),
                pltpu.VMEM((dec_local, features), BF16),
                pltpu.VMEM((1, dec_local), jnp.int32),
                pltpu.SemaphoreType.DMA((3,)),
            ],
            10**5,
            10**6,
            "prepare",
            60 * 1024 * 1024,
        )(out_grad[0], attn_out[0], loss_mask)
        g_recv = to_sibling(g_send)

    with jax.named_scope("query_gather"):
        q_recv, _ = after(q_recv, g_keep)
        q_block = kernel_call(
            join_queries_kernel, block, [VMEM, VMEM], VMEM, [], 10**5, 10**5, "join_queries"
        )(query_rows, q_recv)
        q_far, q_near = gather(q_block)

    with jax.named_scope("key_exchange"):
        k_recv = to_sibling(after(key_rows, q_block)[0])
        v_recv = to_sibling(after(value_rows, q_block)[0])

    with jax.named_scope("setup"):
        half_rows = shaped(enc_local, HALF)
        bias = shaped(enc_local, dec_rows, dtype=F32)
        k_own, bias_own, bias_other = kernel_call(
            functools.partial(setup_kernel, offsets),
            (half_rows, bias, bias),
            [SMEM] * 2 + [VMEM],
            (VMEM,) * 3,
            [],
            10**6,
            2**22,
            "setup",
        )(*lengths, after(key_rows, q_block)[0])

    with jax.named_scope("cotangent_gather"):
        small = shaped(8, 2 * dec_local, dtype=F32)
        g_block, delta, count = kernel_call(
            join_cotangents_kernel,
            (block, small, shaped(8, EXTRA, dtype=F32)),
            [VMEM, VMEM],
            (VMEM,) * 3,
            [],
            10**5,
            10**5,
            "join_cotangents",
        )(g_keep, g_recv)

    def over_groups(count, apart):
        return lax.ppermute(count, "dp", [(i, i ^ apart) for i in range(data_groups)])

    with jax.named_scope("mask_count"):
        apart = 1
        while apart < data_groups // 2:
            count = count + after(over_groups(count, apart), bias_own)[0]
            apart *= 2
        rows_in_all = float(data_groups * dec_rows)

    with jax.named_scope("query_forward"):
        q_far = [q_far[0], *(after(one, bias_own, count)[0] for one in q_far[1:])]
        q_blocks = [*q_far, q_near, *forwarded(q_far)]

    with jax.named_scope("cotangent_gather"):
        g_far, g_near = gather(after(g_block, *q_far, q_near)[0])

    with jax.named_scope("scores"):
        width = (dec_rows // 128 + 1) * 128
        stats = kernel_call(
            functools.partial(scores_kernel, offsets),
            shaped(2 * HALF_HEADS, width, dtype=F32),
            [VMEM] * (chips + 6),
            VMEM,
            [],
            2 * dec_rows * enc_rows * HALF,
            2 * (dec_rows + enc_rows) * HALF,
            "scores",
        )(delta, bias_own, bias_other, k_own, k_recv, count, *q_blocks)

    with jax.named_scope("cotangent_forward"):
        g_far = [g_far[0], *(after(one, stats)[0] for one in g_far[1:])]
        g_blocks = [*g_far, g_near, *forwarded(g_far)]

    with jax.named_scope("stats_exchange"):
        all_stats = [stats] + [across(stats, offset) for offset in offsets[1:]]

    with jax.named_scope("grads"):
        both = shaped(enc_local, 2 * HALF)
        *dq_blocks, dkv_keep, dkv_send, count = kernel_call(
            functools.partial(grads_kernel, offsets),
            (block,) * chips + (both, both, shaped(8, EXTRA, dtype=F32)),
            [VMEM] * (3 * chips + 6),
            (VMEM,) * (chips + 3),
            [],
            10 * dec_rows * enc_rows * HALF,
            4 * (dec_rows + 2 * enc_rows) * HALF,
            "grads",
        )(bias_own, bias_other, *all_stats, *q_blocks, *g_blocks, k_own, k_recv, value_rows, v_recv)

    with jax.named_scope("query_grad_sum"):
        parts = [dq_blocks[0]]
        for j in sorted(range(1, chips), key=lambda j: -offsets[j]):
            parts.append(across(dq_blocks[j], offsets[j]))

    with jax.named_scope("key_grad_end"):
        dkv_recv = to_sibling(dkv_send)
        counts = (count, over_groups(count, data_groups // 2))
        whole = shaped(enc_local, features)
        grad_keys, grad_values, factor = kernel_call(
            functools.partial(key_end_kernel, rows_in_all),
            (whole, whole, shaped(8, EXTRA, dtype=F32)),
            [VMEM] * 4,
            (VMEM, VMEM, VMEM),
            [],
            10**6,
            2**22,
            "key_end",
        )(dkv_keep, dkv_recv, *counts)

    with jax.named_scope("query_grad_end"):
        half = shaped(dec_local, HALF)
        dq_send, dq_keep = kernel_call(
            query_end_kernel,
            (half, half),
            [VMEM] * (chips + 1),
            (VMEM, VMEM),
            [],
            10**5,
            10**6,
            "query_end",
        )(factor, *parts)
        grad_queries = in_order(dq_keep, to_sibling(dq_send), core, 1)

    return grad_queries[None], grad_keys[None], grad_values[None]


def solution(mesh):
    return jax.shard_map(
        local,
        mesh=mesh,
        in_specs=(
            P("dp", "seq", None),
            P("dp", "seq", None),
            P("dp", "seq", None),
            P("dp", "seq", None),
            P("dp", "seq", None),
            P("dp", "seq"),
            P("dp", None, None),
            P("dp", None, None),
        ),
        out_specs=(P("dp", "seq", None), P("dp", "seq", None), P("dp", "seq", None)),
        check_vma=False,
    )
```

```python
import functools
import jax
import jax.numpy as jnp
from jax import lax
from jax.experimental import pallas as pl
from jax.experimental.pallas import tpu as pltpu
from jax.sharding import PartitionSpec as P

HEADS = 8
HEAD_SIZE = 256
HALF_HEADS = HEADS // 2
HALF = HALF_HEADS * HEAD_SIZE
EXTRA = 128
ROOT = HEAD_SIZE**-0.5
NEVER = -1e30
VMEM_LIMIT = 24 * 1024 * 1024
F32 = jnp.float32
BF16 = jnp.bfloat16
ANY = pl.BlockSpec(memory_space=pl.ANY)
VMEM = pl.BlockSpec(memory_space=pltpu.VMEM)
SMEM = pl.BlockSpec(memory_space=pltpu.SMEM)
NT = (((1,), (1,)), ((), ()))
TN = (((0,), (0,)), ((), ()))
NN = (((1,), (0,)), ((), ()))


def dot(a, b, dims):
    return lax.dot_general(a, b, dims, preferred_element_type=F32)


def position():
    me = lax.axis_index("seq")
    return me >> 1, me & 1


def to_sibling(block):
    count = lax.axis_size("seq")
    return lax.ppermute(block, "seq", [(i, i ^ 1) for i in range(count)])


def across(block, apart):
    count = lax.axis_size("seq")
    return lax.ppermute(block, "seq", [(i, i ^ (2 * apart)) for i in range(count)])


def after(block, *others):
    return lax.optimization_barrier((block, *others))


def kernel_call(
    body, out_shape, in_specs, out_specs, scratch, flops, moved, name, vmem_limit=VMEM_LIMIT
):
    return pl.pallas_call(
        body,
        out_shape=out_shape,
        in_specs=in_specs,
        out_specs=out_specs,
        scratch_shapes=scratch,
        compiler_params=pltpu.CompilerParams(vmem_limit_bytes=vmem_limit),
        cost_estimate=pl.CostEstimate(flops=flops, bytes_accessed=moved, transcendentals=0),
        name=name,
    )


def prepare_kernel(
    grad_ref, out_ref, mask_ref, send_ref, keep_ref, grad_held, out_held, mask_held, sems
):
    _, core = position()
    rows = grad_ref.shape[0]
    copies = start_all(
        [(mask_ref, mask_held), (grad_ref, grad_held), (out_ref, out_held)], sems
    )
    copies[0].wait()
    mask_row = mask_held[...].astype(F32)
    here = lax.broadcasted_iota(jnp.int32, (rows, rows), 0) == lax.broadcasted_iota(
        jnp.int32, (rows, rows), 1
    )
    mask = jnp.sum(jnp.where(here, mask_row, 0.0), axis=1, keepdims=True)
    lane = lax.broadcasted_iota(jnp.int32, (rows, EXTRA), 1)
    for copy in copies[1:]:
        copy.wait()
    masked = grad_held[...].astype(F32) * mask
    products = masked * out_held[...].astype(F32)
    grad_held[...] = masked.astype(BF16)
    halves = []
    for half in range(2):
        extra = jnp.where(lane == HALF_HEADS, mask, 0.0)
        for head in range(HALF_HEADS):
            first = half * HALF + head * HEAD_SIZE
            delta = jnp.sum(products[:, first : first + HEAD_SIZE], axis=1, keepdims=True)
            extra = jnp.where(lane == head, delta, extra)
        halves.append(extra)
    for ref, half in ((send_ref, 1 - core), (keep_ref, core)):
        ref[:, :HALF] = grad_held[:, pl.ds(pl.multiple_of(half * HALF, HALF), HALF)]
        ref[:, HALF:] = jnp.where(half == 0, halves[0], halves[1]).astype(BF16)


def in_core_order(own, other, core):
    own, other = own.astype(F32), other.astype(F32)
    joined = jnp.where(
        core == 0, jnp.concatenate([own, other], 0), jnp.concatenate([other, own], 0)
    )
    return joined.astype(BF16)


def join_queries_kernel(own_ref, other_ref, joined_ref):
    _, core = position()
    mine = pl.ds(pl.multiple_of(core * HALF, HALF), HALF)
    joined_ref[...] = in_core_order(own_ref[:, mine], other_ref[:, mine], core)


def join_cotangents_kernel(own_ref, other_ref, joined_ref, delta_ref, count_ref):
    _, core = position()
    joined_ref[...] = in_core_order(own_ref[:, :HALF], other_ref[:, :HALF], core)
    extra = jnp.transpose(in_core_order(own_ref[:, HALF:], other_ref[:, HALF:], core).astype(F32))
    delta_ref[...] = extra[: delta_ref.shape[0]]
    count = jnp.sum(extra[HALF_HEADS : HALF_HEADS + 1], axis=1, keepdims=True)
    count_ref[...] = jnp.broadcast_to(count, count_ref.shape)


def split_kernel(rows_ref, own_ref, send_ref):
    _, core = position()
    for ref, half in ((own_ref, core), (send_ref, 1 - core)):
        ref[...] = rows_ref[:, pl.ds(pl.multiple_of(half * HALF, HALF), HALF)]


def document_of(positions, lengths_ref):
    end = 0
    document = jnp.zeros_like(positions)
    for i in range(lengths_ref.shape[1]):
        end = end + lengths_ref[0, i]
        document += (positions >= end).astype(jnp.int32)
    return document


def setup_kernel(offsets, in_ref, target_ref, key_ref, k_ref, send_ref, bias_own, bias_other):
    chip, core = position()
    split_kernel(key_ref, k_ref, send_ref)
    enc_rows, dec_rows = bias_own.shape
    block = dec_rows // len(offsets)
    lane = lax.broadcasted_iota(jnp.int32, (1, dec_rows), 1)
    dec = lane + chip * block
    for j, offset in enumerate(offsets[1:], 1):
        dec = jnp.where(lane >= j * block, lane + ((chip ^ offset) - j) * block, dec)
    dec = document_of(dec, target_ref)
    for ref, side in ((bias_own, core), (bias_other, 1 - core)):
        enc = lax.broadcasted_iota(jnp.int32, (enc_rows, 1), 0) + (2 * chip + side) * enc_rows
        ref[...] = jnp.where(document_of(enc, in_ref) == dec, 0.0, NEVER)


def start_all(pairs, sems):
    copies = [pltpu.make_async_copy(a, b, sems.at[i]) for i, (a, b) in enumerate(pairs)]
    for copy in copies:
        copy.start()
    return copies


def rows_of(blocks, head):
    columns = slice(head * HEAD_SIZE, (head + 1) * HEAD_SIZE)
    return jnp.concatenate([block[:, columns] for block in blocks], 0)


def value_columns_of(head):
    _, core = position()
    first = core * HALF + head * HEAD_SIZE
    return pl.ds(pl.multiple_of(first, HEAD_SIZE), HEAD_SIZE)


def columns_of(head):
    return slice(head * HEAD_SIZE, (head + 1) * HEAD_SIZE)


def scores_kernel(offsets, delta_ref, bias_own, bias_other, key_ref, other_ref, *refs):
    count_ref, refs = refs[0], refs[1:]
    blocks, (stats_ref,) = refs[: len(offsets)], refs[len(offsets) :]
    rows = blocks[0].shape[0]
    dec_rows = rows * len(offsets)
    stats_ref[...] = jnp.broadcast_to(count_ref[0:1, 0:1], stats_ref.shape)
    stats_ref[HALF_HEADS:, :rows] = delta_ref[:HALF_HEADS]
    for head in range(HALF_HEADS):
        q = rows_of(blocks, head)
        scores = [
            dot(k[:, columns_of(head)], q, NT) * ROOT + bias[...]
            for k, bias in ((key_ref, bias_own), (other_ref, bias_other))
        ]
        top = functools.reduce(jnp.maximum, [jnp.max(s, axis=0, keepdims=True) for s in scores])
        top = jnp.maximum(top, -1e20)
        total = sum(jnp.sum(jnp.exp(s - top), axis=0, keepdims=True) for s in scores)
        stats_ref[head : head + 1, :dec_rows] = jnp.where(
            total > 0, top + jnp.log(jnp.maximum(total, 1e-30)), NEVER
        )


def gathered_stats(offsets, stats, rows):
    logs = []
    for sender, ref in zip(offsets, stats):
        order = [offsets.index(offset ^ sender) for offset in offsets]
        logs.append(
            jnp.concatenate([ref[:HALF_HEADS, j * rows : (j + 1) * rows] for j in order], 1)
        )
    top = functools.reduce(jnp.maximum, logs)
    log_total = top + jnp.log(sum(jnp.exp(log - top) for log in logs))
    delta = jnp.concatenate([ref[HALF_HEADS:, :rows] for ref in stats], 1)
    last = stats[0].shape[1] - 1
    return log_total, delta, sum(ref[0:1, last:] for ref in stats)


def grads_kernel(offsets, bias_own, bias_other, *refs):
    chips = len(offsets)
    stats, refs = refs[:chips], refs[chips:]
    q_blocks, refs = refs[:chips], refs[chips:]
    g_blocks, refs = refs[:chips], refs[chips:]
    (key_ref, key_other, value_ref, value_other), refs = refs[:4], refs[4:]
    dq_blocks, (keep_ref, send_ref, count_ref) = refs[:chips], refs[chips:]
    rows = q_blocks[0].shape[0]
    log_total, delta, count = gathered_stats(offsets, stats, rows)
    count_ref[...] = jnp.broadcast_to(count, count_ref.shape)
    for head in range(HALF_HEADS):
        columns = slice(head * HEAD_SIZE, (head + 1) * HEAD_SIZE)
        value_columns = slice(HALF + columns.start, HALF + columns.stop)
        line = slice(head, head + 1)
        q, g = rows_of(q_blocks, head), rows_of(g_blocks, head)
        dq = 0.0
        for key, value, bias, out_ref in (
            (key_ref, value_ref, bias_own, keep_ref),
            (key_other, value_other, bias_other, send_ref),
        ):
            k, v = key[:, columns], value[:, value_columns_of(head)]
            probs = jnp.exp(dot(k, q, NT) * ROOT + bias[...] - log_total[line])
            dscore = (probs * (dot(v, g, NT) - delta[line])).astype(BF16)
            dq += dot(dscore, k, TN)
            out_ref[:, columns] = (dot(dscore, q, NN) * ROOT).astype(BF16)
            out_ref[:, value_columns] = dot(probs.astype(BF16), g, NN).astype(BF16)
        dq = (dq * ROOT).astype(BF16)
        for j, block in enumerate(dq_blocks):
            block[:, columns] = dq[j * rows : (j + 1) * rows]


def key_end_kernel(rows_in_all, keep_ref, other_ref, *refs):
    counts, (dk_ref, dv_ref, factor_ref) = refs[:2], refs[2:]
    _, core = position()
    factor = rows_in_all / (counts[0][0:1, 0:1] + counts[1][0:1, 0:1])
    factor_ref[...] = jnp.broadcast_to(factor, factor_ref.shape)
    for ref, side in ((keep_ref, core), (other_ref, 1 - core)):
        columns = pl.ds(pl.multiple_of(side * HALF, HALF), HALF)
        dk_ref[:, columns] = (ref[:, :HALF].astype(F32) * factor).astype(BF16)
        dv_ref[:, columns] = (ref[:, HALF:].astype(F32) * factor).astype(BF16)


def query_end_kernel(factor_ref, *refs):
    parts, (send_ref, keep_ref) = refs[:-2], refs[-2:]
    _, core = position()
    summed = factor_ref[0:1, 0:1] * sum(part[...].astype(F32) for part in parts)
    half = summed.shape[0] // 2
    low, high = summed[:half], summed[half:]
    send_ref[...] = jnp.where(core == 0, high, low).astype(BF16)
    keep_ref[...] = jnp.where(core == 0, low, high).astype(BF16)


def in_order(own, other, core, axis):
    return jnp.where(
        core == 0, jnp.concatenate([own, other], axis), jnp.concatenate([other, own], axis)
    )


def local(queries, keys, values, attn_out, out_grad, loss_mask, input_lengths, target_lengths):
    query_rows, key_rows, value_rows = queries[0], keys[0], values[0]
    dec_local, enc_local = query_rows.shape[0], key_rows.shape[0]
    chips = lax.axis_size("seq") // 2
    data_groups = lax.axis_size("dp")
    _, core = position()
    dec_rows = 2 * chips * dec_local
    enc_rows = 2 * enc_local
    block = (2 * dec_local, HALF)
    lengths = (input_lengths[0], target_lengths[0])

    def shaped(*shape, dtype=BF16):
        return jax.ShapeDtypeStruct(shape, dtype)

    def gather(block):
        blocks = [block]
        apart = chips // 2
        while apart > 1:
            blocks += [across(one, apart) for one in blocks]
            apart //= 2
        return blocks, across(block, 1)

    def forwarded(blocks):
        return [across(one, 1) for one in blocks[1:]]

    offsets = [0]
    apart = chips // 2
    while apart:
        offsets += [offset ^ apart for offset in offsets]
        apart //= 2

    features = HEADS * HEAD_SIZE
    sent = shaped(dec_local, HALF + EXTRA)
    block = shaped(2 * dec_local, HALF)

    with jax.named_scope("sibling_exchange"):
        q_recv = to_sibling(query_rows)
        g_send, g_keep = kernel_call(
            prepare_kernel,
            (sent, sent),
            [ANY] * 3,
            (VMEM, VMEM),
            [
                pltpu.VMEM((dec_local, features), BF16),
                pltpu.VMEM((dec_local, features), BF16),
                pltpu.VMEM((1, dec_local), jnp.int32),
                pltpu.SemaphoreType.DMA((3,)),
            ],
            10**5,
            10**6,
            "prepare",
            60 * 1024 * 1024,
        )(out_grad[0], attn_out[0], loss_mask)
        g_recv = to_sibling(g_send)

    with jax.named_scope("query_gather"):
        q_recv, _ = after(q_recv, g_keep)
        q_block = kernel_call(
            join_queries_kernel, block, [VMEM, VMEM], VMEM, [], 10**5, 10**5, "join_queries"
        )(query_rows, q_recv)
        q_far, q_near = gather(q_block)

    with jax.named_scope("setup"):
        half_rows = shaped(enc_local, HALF)
        bias = shaped(enc_local, dec_rows, dtype=F32)
        k_own, k_send, bias_own, bias_other = kernel_call(
            functools.partial(setup_kernel, offsets),
            (half_rows, half_rows, bias, bias),
            [SMEM] * 2 + [VMEM],
            (VMEM,) * 4,
            [],
            10**6,
            2**22,
            "setup",
        )(*lengths, after(key_rows, q_block)[0])

    with jax.named_scope("cotangent_gather"):
        small = shaped(8, 2 * dec_local, dtype=F32)
        g_block, delta, count = kernel_call(
            join_cotangents_kernel,
            (block, small, shaped(8, EXTRA, dtype=F32)),
            [VMEM, VMEM],
            (VMEM,) * 3,
            [],
            10**5,
            10**5,
            "join_cotangents",
        )(g_keep, g_recv)

    def over_groups(count, apart):
        return lax.ppermute(count, "dp", [(i, i ^ apart) for i in range(data_groups)])

    with jax.named_scope("mask_count"):
        apart = 1
        while apart < data_groups // 2:
            count = count + after(over_groups(count, apart), bias_own)[0]
            apart *= 2
        rows_in_all = float(data_groups * dec_rows)

    with jax.named_scope("query_forward"):
        q_far = [q_far[0], *(after(one, bias_own, count, q_near)[0] for one in q_far[1:])]
        q_blocks = [*q_far, q_near, *forwarded(q_far)]

    with jax.named_scope("cotangent_gather"):
        sent = after(g_block, *q_far, q_near)[0]
        g_blocks = [g_block] + [across(sent, offset) for offset in offsets[1:]]

    with jax.named_scope("key_exchange"):
        v_recv = to_sibling(value_rows)
        k_send, v_recv, *_ = after(k_send, v_recv, *q_far, q_near)
        k_recv = to_sibling(k_send)

    with jax.named_scope("scores"):
        width = (dec_rows // 128 + 1) * 128
        stats = kernel_call(
            functools.partial(scores_kernel, offsets),
            shaped(2 * HALF_HEADS, width, dtype=F32),
            [VMEM] * (chips + 6),
            VMEM,
            [],
            2 * dec_rows * enc_rows * HALF,
            2 * (dec_rows + enc_rows) * HALF,
            "scores",
        )(delta, bias_own, bias_other, k_own, k_recv, count, *q_blocks)

    with jax.named_scope("stats_exchange"):
        all_stats = [stats] + [across(stats, offset) for offset in offsets[1:]]

    with jax.named_scope("grads"):
        both = shaped(enc_local, 2 * HALF)
        *dq_blocks, dkv_keep, dkv_send, count = kernel_call(
            functools.partial(grads_kernel, offsets),
            (block,) * chips + (both, both, shaped(8, EXTRA, dtype=F32)),
            [VMEM] * (3 * chips + 6),
            (VMEM,) * (chips + 3),
            [],
            10 * dec_rows * enc_rows * HALF,
            4 * (dec_rows + 2 * enc_rows) * HALF,
            "grads",
        )(bias_own, bias_other, *all_stats, *q_blocks, *g_blocks, k_own, k_recv, value_rows, v_recv)

    with jax.named_scope("query_grad_sum"):
        parts = [dq_blocks[0]]
        for j in sorted(range(1, chips), key=lambda j: -offsets[j]):
            parts.append(across(dq_blocks[j], offsets[j]))

    with jax.named_scope("key_grad_end"):
        dkv_recv = to_sibling(dkv_send)
        counts = (count, over_groups(count, data_groups // 2))
        whole = shaped(enc_local, features)
        grad_keys, grad_values, factor = kernel_call(
            functools.partial(key_end_kernel, rows_in_all),
            (whole, whole, shaped(8, EXTRA, dtype=F32)),
            [VMEM] * 4,
            (VMEM, VMEM, VMEM),
            [],
            10**6,
            2**22,
            "key_end",
        )(dkv_keep, dkv_recv, *counts)

    with jax.named_scope("query_grad_end"):
        half = shaped(dec_local, HALF)
        dq_send, dq_keep = kernel_call(
            query_end_kernel,
            (half, half),
            [VMEM] * (chips + 1),
            (VMEM, VMEM),
            [],
            10**5,
            10**6,
            "query_end",
        )(factor, *parts)
        grad_queries = in_order(dq_keep, to_sibling(dq_send), core, 1)

    return grad_queries[None], grad_keys[None], grad_values[None]


def solution(mesh):
    return jax.shard_map(
        local,
        mesh=mesh,
        in_specs=(
            P("dp", "seq", None),
            P("dp", "seq", None),
            P("dp", "seq", None),
            P("dp", "seq", None),
            P("dp", "seq", None),
            P("dp", "seq"),
            P("dp", None, None),
            P("dp", None, None),
        ),
        out_specs=(P("dp", "seq", None), P("dp", "seq", None), P("dp", "seq", None)),
        check_vma=False,
    )
```

```python
import functools
import jax
import jax.numpy as jnp
from jax import lax
from jax.experimental import pallas as pl
from jax.experimental.pallas import tpu as pltpu
from jax.sharding import PartitionSpec as P

HEADS = 8
HEAD_SIZE = 256
HALF_HEADS = HEADS // 2
HALF = HALF_HEADS * HEAD_SIZE
EXTRA = 128
ROOT = HEAD_SIZE**-0.5
NEVER = -1e30
VMEM_LIMIT = 24 * 1024 * 1024
F32 = jnp.float32
BF16 = jnp.bfloat16
ANY = pl.BlockSpec(memory_space=pl.ANY)
VMEM = pl.BlockSpec(memory_space=pltpu.VMEM)
SMEM = pl.BlockSpec(memory_space=pltpu.SMEM)
NT = (((1,), (1,)), ((), ()))
TN = (((0,), (0,)), ((), ()))
NN = (((1,), (0,)), ((), ()))


def dot(a, b, dims):
    return lax.dot_general(a, b, dims, preferred_element_type=F32)


def position():
    me = lax.axis_index("seq")
    return me >> 1, me & 1


def to_sibling(block):
    count = lax.axis_size("seq")
    return lax.ppermute(block, "seq", [(i, i ^ 1) for i in range(count)])


def across(block, apart):
    count = lax.axis_size("seq")
    return lax.ppermute(block, "seq", [(i, i ^ (2 * apart)) for i in range(count)])


def after(block, *others):
    return lax.optimization_barrier((block, *others))


def kernel_call(
    body, out_shape, in_specs, out_specs, scratch, flops, moved, name, vmem_limit=VMEM_LIMIT
):
    return pl.pallas_call(
        body,
        out_shape=out_shape,
        in_specs=in_specs,
        out_specs=out_specs,
        scratch_shapes=scratch,
        compiler_params=pltpu.CompilerParams(vmem_limit_bytes=vmem_limit),
        cost_estimate=pl.CostEstimate(flops=flops, bytes_accessed=moved, transcendentals=0),
        name=name,
    )


def prepare_kernel(
    grad_ref, out_ref, mask_ref, send_ref, keep_ref, grad_held, out_held, mask_held, sems
):
    _, core = position()
    rows = grad_ref.shape[0]
    copies = start_all(
        [(mask_ref, mask_held), (grad_ref, grad_held), (out_ref, out_held)], sems
    )
    copies[0].wait()
    mask_row = mask_held[...].astype(F32)
    here = lax.broadcasted_iota(jnp.int32, (rows, rows), 0) == lax.broadcasted_iota(
        jnp.int32, (rows, rows), 1
    )
    mask = jnp.sum(jnp.where(here, mask_row, 0.0), axis=1, keepdims=True)
    lane = lax.broadcasted_iota(jnp.int32, (rows, EXTRA), 1)
    for copy in copies[1:]:
        copy.wait()
    masked = grad_held[...].astype(F32) * mask
    products = masked * out_held[...].astype(F32)
    grad_held[...] = masked.astype(BF16)
    halves = []
    for half in range(2):
        extra = jnp.where(lane == HALF_HEADS, mask, 0.0)
        for head in range(HALF_HEADS):
            first = half * HALF + head * HEAD_SIZE
            delta = jnp.sum(products[:, first : first + HEAD_SIZE], axis=1, keepdims=True)
            extra = jnp.where(lane == head, delta, extra)
        halves.append(extra)
    for ref, half in ((send_ref, 1 - core), (keep_ref, core)):
        ref[:, :HALF] = grad_held[:, pl.ds(pl.multiple_of(half * HALF, HALF), HALF)]
        ref[:, HALF:] = jnp.where(half == 0, halves[0], halves[1]).astype(BF16)


def in_core_order(own, other, core):
    own, other = own.astype(F32), other.astype(F32)
    joined = jnp.where(
        core == 0, jnp.concatenate([own, other], 0), jnp.concatenate([other, own], 0)
    )
    return joined.astype(BF16)


def join_queries_kernel(own_ref, other_ref, joined_ref):
    _, core = position()
    mine = pl.ds(pl.multiple_of(core * HALF, HALF), HALF)
    joined_ref[...] = in_core_order(own_ref[:, mine], other_ref[:, mine], core)


def join_cotangents_kernel(own_ref, other_ref, joined_ref, delta_ref, count_ref):
    _, core = position()
    joined_ref[...] = in_core_order(own_ref[:, :HALF], other_ref[:, :HALF], core)
    extra = jnp.transpose(in_core_order(own_ref[:, HALF:], other_ref[:, HALF:], core).astype(F32))
    delta_ref[...] = extra[: delta_ref.shape[0]]
    count = jnp.sum(extra[HALF_HEADS : HALF_HEADS + 1], axis=1, keepdims=True)
    count_ref[...] = jnp.broadcast_to(count, count_ref.shape)


def split_kernel(rows_ref, own_ref, send_ref):
    _, core = position()
    for ref, half in ((own_ref, core), (send_ref, 1 - core)):
        ref[...] = rows_ref[:, pl.ds(pl.multiple_of(half * HALF, HALF), HALF)]


def document_of(positions, lengths_ref):
    end = 0
    document = jnp.zeros_like(positions)
    for i in range(lengths_ref.shape[1]):
        end = end + lengths_ref[0, i]
        document += (positions >= end).astype(jnp.int32)
    return document


def setup_kernel(offsets, in_ref, target_ref, key_ref, k_ref, send_ref, bias_own, bias_other):
    chip, core = position()
    split_kernel(key_ref, k_ref, send_ref)
    enc_rows, dec_rows = bias_own.shape
    block = dec_rows // len(offsets)
    lane = lax.broadcasted_iota(jnp.int32, (1, dec_rows), 1)
    dec = lane + chip * block
    for j, offset in enumerate(offsets[1:], 1):
        dec = jnp.where(lane >= j * block, lane + ((chip ^ offset) - j) * block, dec)
    dec = document_of(dec, target_ref)
    for ref, side in ((bias_own, core), (bias_other, 1 - core)):
        enc = lax.broadcasted_iota(jnp.int32, (enc_rows, 1), 0) + (2 * chip + side) * enc_rows
        ref[...] = jnp.where(document_of(enc, in_ref) == dec, 0.0, NEVER)


def start_all(pairs, sems):
    copies = [pltpu.make_async_copy(a, b, sems.at[i]) for i, (a, b) in enumerate(pairs)]
    for copy in copies:
        copy.start()
    return copies


def rows_of(blocks, head):
    columns = slice(head * HEAD_SIZE, (head + 1) * HEAD_SIZE)
    return jnp.concatenate([block[:, columns] for block in blocks], 0)


def value_columns_of(head):
    _, core = position()
    first = core * HALF + head * HEAD_SIZE
    return pl.ds(pl.multiple_of(first, HEAD_SIZE), HEAD_SIZE)


def columns_of(head):
    return slice(head * HEAD_SIZE, (head + 1) * HEAD_SIZE)


def scores_kernel(offsets, delta_ref, bias_own, bias_other, key_ref, other_ref, *refs):
    count_ref, refs = refs[0], refs[1:]
    blocks, (stats_ref,) = refs[: len(offsets)], refs[len(offsets) :]
    rows = blocks[0].shape[0]
    dec_rows = rows * len(offsets)
    stats_ref[...] = jnp.broadcast_to(count_ref[0:1, 0:1], stats_ref.shape)
    stats_ref[HALF_HEADS:, :rows] = delta_ref[:HALF_HEADS]
    for head in range(HALF_HEADS):
        q = rows_of(blocks, head)
        scores = [
            dot(k[:, columns_of(head)], q, NT) * ROOT + bias[...]
            for k, bias in ((key_ref, bias_own), (other_ref, bias_other))
        ]
        top = functools.reduce(jnp.maximum, [jnp.max(s, axis=0, keepdims=True) for s in scores])
        top = jnp.maximum(top, -1e20)
        total = sum(jnp.sum(jnp.exp(s - top), axis=0, keepdims=True) for s in scores)
        stats_ref[head : head + 1, :dec_rows] = jnp.where(
            total > 0, top + jnp.log(jnp.maximum(total, 1e-30)), NEVER
        )


def gathered_stats(offsets, stats, rows):
    logs = []
    for sender, ref in zip(offsets, stats):
        order = [offsets.index(offset ^ sender) for offset in offsets]
        logs.append(
            jnp.concatenate([ref[:HALF_HEADS, j * rows : (j + 1) * rows] for j in order], 1)
        )
    top = functools.reduce(jnp.maximum, logs)
    log_total = top + jnp.log(sum(jnp.exp(log - top) for log in logs))
    delta = jnp.concatenate([ref[HALF_HEADS:, :rows] for ref in stats], 1)
    last = stats[0].shape[1] - 1
    return log_total, delta, sum(ref[0:1, last:] for ref in stats)


def grads_kernel(offsets, bias_own, bias_other, *refs):
    chips = len(offsets)
    stats, refs = refs[:chips], refs[chips:]
    q_blocks, refs = refs[:chips], refs[chips:]
    g_blocks, refs = refs[:chips], refs[chips:]
    (key_ref, key_other, value_ref, value_other), refs = refs[:4], refs[4:]
    dq_blocks, (keep_ref, send_ref, count_ref) = refs[:chips], refs[chips:]
    rows = q_blocks[0].shape[0]
    log_total, delta, count = gathered_stats(offsets, stats, rows)
    count_ref[...] = jnp.broadcast_to(count, count_ref.shape)
    for head in range(HALF_HEADS):
        columns = slice(head * HEAD_SIZE, (head + 1) * HEAD_SIZE)
        value_columns = slice(HALF + columns.start, HALF + columns.stop)
        line = slice(head, head + 1)
        q, g = rows_of(q_blocks, head), rows_of(g_blocks, head)
        dq = 0.0
        for key, value, bias, out_ref in (
            (key_ref, value_ref, bias_own, keep_ref),
            (key_other, value_other, bias_other, send_ref),
        ):
            k, v = key[:, columns], value[:, value_columns_of(head)]
            probs = jnp.exp(dot(k, q, NT) * ROOT + bias[...] - log_total[line])
            dscore = (probs * (dot(v, g, NT) - delta[line])).astype(BF16)
            dq += dot(dscore, k, TN)
            out_ref[:, columns] = (dot(dscore, q, NN) * ROOT).astype(BF16)
            out_ref[:, value_columns] = dot(probs.astype(BF16), g, NN).astype(BF16)
        dq = (dq * ROOT).astype(BF16)
        for j, block in enumerate(dq_blocks):
            block[:, columns] = dq[j * rows : (j + 1) * rows]


def key_end_kernel(rows_in_all, keep_ref, other_ref, *refs):
    counts, (dk_ref, dv_ref, factor_ref) = refs[:2], refs[2:]
    _, core = position()
    factor = rows_in_all / (counts[0][0:1, 0:1] + counts[1][0:1, 0:1])
    factor_ref[...] = jnp.broadcast_to(factor, factor_ref.shape)
    for ref, side in ((keep_ref, core), (other_ref, 1 - core)):
        columns = pl.ds(pl.multiple_of(side * HALF, HALF), HALF)
        dk_ref[:, columns] = (ref[:, :HALF].astype(F32) * factor).astype(BF16)
        dv_ref[:, columns] = (ref[:, HALF:].astype(F32) * factor).astype(BF16)


def query_end_kernel(factor_ref, *refs):
    parts, (send_ref, keep_ref) = refs[:-2], refs[-2:]
    _, core = position()
    summed = factor_ref[0:1, 0:1] * sum(part[...].astype(F32) for part in parts)
    half = summed.shape[0] // 2
    low, high = summed[:half], summed[half:]
    send_ref[...] = jnp.where(core == 0, high, low).astype(BF16)
    keep_ref[...] = jnp.where(core == 0, low, high).astype(BF16)


def in_order(own, other, core, axis):
    return jnp.where(
        core == 0, jnp.concatenate([own, other], axis), jnp.concatenate([other, own], axis)
    )


def local(queries, keys, values, attn_out, out_grad, loss_mask, input_lengths, target_lengths):
    query_rows, key_rows, value_rows = queries[0], keys[0], values[0]
    dec_local, enc_local = query_rows.shape[0], key_rows.shape[0]
    chips = lax.axis_size("seq") // 2
    data_groups = lax.axis_size("dp")
    _, core = position()
    dec_rows = 2 * chips * dec_local
    enc_rows = 2 * enc_local
    block = (2 * dec_local, HALF)
    lengths = (input_lengths[0], target_lengths[0])

    def shaped(*shape, dtype=BF16):
        return jax.ShapeDtypeStruct(shape, dtype)

    def gather(block):
        blocks = [block]
        apart = chips // 2
        while apart > 1:
            blocks += [across(one, apart) for one in blocks]
            apart //= 2
        return blocks, across(block, 1)

    def forwarded(blocks):
        return [across(one, 1) for one in blocks[1:]]

    offsets = [0]
    apart = chips // 2
    while apart:
        offsets += [offset ^ apart for offset in offsets]
        apart //= 2

    features = HEADS * HEAD_SIZE
    sent = shaped(dec_local, HALF + EXTRA)
    block = shaped(2 * dec_local, HALF)

    with jax.named_scope("sibling_exchange"):
        q_recv = to_sibling(query_rows)
        g_send, g_keep = kernel_call(
            prepare_kernel,
            (sent, sent),
            [ANY] * 3,
            (VMEM, VMEM),
            [
                pltpu.VMEM((dec_local, features), BF16),
                pltpu.VMEM((dec_local, features), BF16),
                pltpu.VMEM((1, dec_local), jnp.int32),
                pltpu.SemaphoreType.DMA((3,)),
            ],
            10**5,
            10**6,
            "prepare",
            60 * 1024 * 1024,
        )(out_grad[0], attn_out[0], loss_mask)
        g_recv = to_sibling(g_send)

    with jax.named_scope("query_gather"):
        v_recv = to_sibling(value_rows)
        q_recv, _, v_recv = after(q_recv, g_keep, v_recv)
        q_block = kernel_call(
            join_queries_kernel, block, [VMEM, VMEM], VMEM, [], 10**5, 10**5, "join_queries"
        )(query_rows, q_recv)
        q_far, q_near = gather(q_block)

    with jax.named_scope("setup"):
        half_rows = shaped(enc_local, HALF)
        bias = shaped(enc_local, dec_rows, dtype=F32)
        k_own, k_send, bias_own, bias_other = kernel_call(
            functools.partial(setup_kernel, offsets),
            (half_rows, half_rows, bias, bias),
            [SMEM] * 2 + [VMEM],
            (VMEM,) * 4,
            [],
            10**6,
            2**22,
            "setup",
        )(*lengths, after(key_rows, q_block)[0])

    with jax.named_scope("cotangent_gather"):
        small = shaped(8, 2 * dec_local, dtype=F32)
        g_block, delta, count = kernel_call(
            join_cotangents_kernel,
            (block, small, shaped(8, EXTRA, dtype=F32)),
            [VMEM, VMEM],
            (VMEM,) * 3,
            [],
            10**5,
            10**5,
            "join_cotangents",
        )(g_keep, after(g_recv, q_block)[0])

    def over_groups(count, apart):
        return lax.ppermute(count, "dp", [(i, i ^ apart) for i in range(data_groups)])

    with jax.named_scope("mask_count"):
        apart = 1
        while apart < data_groups // 2:
            count = after(count, q_block)[0]
            count = count + after(over_groups(count, apart), bias_own)[0]
            apart *= 2
        rows_in_all = float(data_groups * dec_rows)

    with jax.named_scope("cotangent_gather"):
        g_far, g_near = gather(g_block)

    with jax.named_scope("forward"):
        held = (bias_own, count, q_near, g_near, *g_far[1:])
        q_far = [q_far[0], *(after(one, *held)[0] for one in q_far[1:])]
        q_blocks = [*q_far, q_near, *forwarded(q_far)]
        g_blocks = [*g_far, g_near, *forwarded(g_far)]

    with jax.named_scope("key_exchange"):
        k_recv = to_sibling(after(k_send, *q_far, q_near)[0])

    with jax.named_scope("scores"):
        width = (dec_rows // 128 + 1) * 128
        stats = kernel_call(
            functools.partial(scores_kernel, offsets),
            shaped(2 * HALF_HEADS, width, dtype=F32),
            [VMEM] * (chips + 6),
            VMEM,
            [],
            2 * dec_rows * enc_rows * HALF,
            2 * (dec_rows + enc_rows) * HALF,
            "scores",
        )(delta, bias_own, bias_other, k_own, k_recv, count, *q_blocks)

    with jax.named_scope("stats_exchange"):
        all_stats = [stats] + [across(stats, offset) for offset in offsets[1:]]

    with jax.named_scope("grads"):
        both = shaped(enc_local, 2 * HALF)
        *dq_blocks, dkv_keep, dkv_send, count = kernel_call(
            functools.partial(grads_kernel, offsets),
            (block,) * chips + (both, both, shaped(8, EXTRA, dtype=F32)),
            [VMEM] * (3 * chips + 6),
            (VMEM,) * (chips + 3),
            [],
            10 * dec_rows * enc_rows * HALF,
            4 * (dec_rows + 2 * enc_rows) * HALF,
            "grads",
        )(bias_own, bias_other, *all_stats, *q_blocks, *g_blocks, k_own, k_recv, value_rows, v_recv)

    with jax.named_scope("query_grad_sum"):
        parts = [dq_blocks[0]]
        for j in sorted(range(1, chips), key=lambda j: -offsets[j]):
            parts.append(across(dq_blocks[j], offsets[j]))

    with jax.named_scope("key_grad_end"):
        dkv_recv = to_sibling(dkv_send)
        counts = (count, over_groups(count, data_groups // 2))
        whole = shaped(enc_local, features)
        grad_keys, grad_values, factor = kernel_call(
            functools.partial(key_end_kernel, rows_in_all),
            (whole, whole, shaped(8, EXTRA, dtype=F32)),
            [VMEM] * 4,
            (VMEM, VMEM, VMEM),
            [],
            10**6,
            2**22,
            "key_end",
        )(dkv_keep, dkv_recv, *counts)

    with jax.named_scope("query_grad_end"):
        half = shaped(dec_local, HALF)
        dq_send, dq_keep = kernel_call(
            query_end_kernel,
            (half, half),
            [VMEM] * (chips + 1),
            (VMEM, VMEM),
            [],
            10**5,
            10**6,
            "query_end",
        )(factor, *parts)
        grad_queries = in_order(dq_keep, to_sibling(dq_send), core, 1)

    return grad_queries[None], grad_keys[None], grad_values[None]


def solution(mesh):
    return jax.shard_map(
        local,
        mesh=mesh,
        in_specs=(
            P("dp", "seq", None),
            P("dp", "seq", None),
            P("dp", "seq", None),
            P("dp", "seq", None),
            P("dp", "seq", None),
            P("dp", "seq"),
            P("dp", None, None),
            P("dp", None, None),
        ),
        out_specs=(P("dp", "seq", None), P("dp", "seq", None), P("dp", "seq", None)),
        check_vma=False,
    )
```

```python
import functools
import jax
import jax.numpy as jnp
from jax import lax
from jax.experimental import pallas as pl
from jax.experimental.pallas import tpu as pltpu
from jax.sharding import PartitionSpec as P

HEADS = 8
HEAD_SIZE = 256
HALF_HEADS = HEADS // 2
HALF = HALF_HEADS * HEAD_SIZE
EXTRA = 128
ROOT = HEAD_SIZE**-0.5
NEVER = -1e30
VMEM_LIMIT = 24 * 1024 * 1024
F32 = jnp.float32
BF16 = jnp.bfloat16
ANY = pl.BlockSpec(memory_space=pl.ANY)
VMEM = pl.BlockSpec(memory_space=pltpu.VMEM)
SMEM = pl.BlockSpec(memory_space=pltpu.SMEM)
NT = (((1,), (1,)), ((), ()))
TN = (((0,), (0,)), ((), ()))
NN = (((1,), (0,)), ((), ()))


def dot(a, b, dims):
    return lax.dot_general(a, b, dims, preferred_element_type=F32)


def position():
    me = lax.axis_index("seq")
    return me >> 1, me & 1


def to_sibling(block):
    count = lax.axis_size("seq")
    return lax.ppermute(block, "seq", [(i, i ^ 1) for i in range(count)])


def across(block, apart):
    count = lax.axis_size("seq")
    return lax.ppermute(block, "seq", [(i, i ^ (2 * apart)) for i in range(count)])


def after(block, *others):
    return lax.optimization_barrier((block, *others))


def kernel_call(
    body, out_shape, in_specs, out_specs, scratch, flops, moved, name, vmem_limit=VMEM_LIMIT
):
    return pl.pallas_call(
        body,
        out_shape=out_shape,
        in_specs=in_specs,
        out_specs=out_specs,
        scratch_shapes=scratch,
        compiler_params=pltpu.CompilerParams(vmem_limit_bytes=vmem_limit),
        cost_estimate=pl.CostEstimate(flops=flops, bytes_accessed=moved, transcendentals=0),
        name=name,
    )


def prepare_kernel(
    grad_ref, out_ref, mask_ref, send_ref, keep_ref, grad_held, out_held, mask_held, sems
):
    _, core = position()
    rows = grad_ref.shape[0]
    copies = start_all(
        [(mask_ref, mask_held), (grad_ref, grad_held), (out_ref, out_held)], sems
    )
    copies[0].wait()
    mask_row = mask_held[...].astype(F32)
    here = lax.broadcasted_iota(jnp.int32, (rows, rows), 0) == lax.broadcasted_iota(
        jnp.int32, (rows, rows), 1
    )
    mask = jnp.sum(jnp.where(here, mask_row, 0.0), axis=1, keepdims=True)
    lane = lax.broadcasted_iota(jnp.int32, (rows, EXTRA), 1)
    for copy in copies[1:]:
        copy.wait()
    masked = grad_held[...].astype(F32) * mask
    products = masked * out_held[...].astype(F32)
    grad_held[...] = masked.astype(BF16)
    halves = []
    for half in range(2):
        extra = jnp.where(lane == HALF_HEADS, mask, 0.0)
        for head in range(HALF_HEADS):
            first = half * HALF + head * HEAD_SIZE
            delta = jnp.sum(products[:, first : first + HEAD_SIZE], axis=1, keepdims=True)
            extra = jnp.where(lane == head, delta, extra)
        halves.append(extra)
    for ref, half in ((send_ref, 1 - core), (keep_ref, core)):
        ref[:, :HALF] = grad_held[:, pl.ds(pl.multiple_of(half * HALF, HALF), HALF)]
        ref[:, HALF:] = jnp.where(half == 0, halves[0], halves[1]).astype(BF16)


def in_core_order(own, other, core):
    own, other = own.astype(F32), other.astype(F32)
    joined = jnp.where(
        core == 0, jnp.concatenate([own, other], 0), jnp.concatenate([other, own], 0)
    )
    return joined.astype(BF16)


def join_queries_kernel(own_ref, other_ref, joined_ref):
    _, core = position()
    mine = pl.ds(pl.multiple_of(core * HALF, HALF), HALF)
    joined_ref[...] = in_core_order(own_ref[:, mine], other_ref[:, mine], core)


def join_cotangents_kernel(own_ref, other_ref, joined_ref, delta_ref, count_ref):
    _, core = position()
    joined_ref[...] = in_core_order(own_ref[:, :HALF], other_ref[:, :HALF], core)
    extra = jnp.transpose(in_core_order(own_ref[:, HALF:], other_ref[:, HALF:], core).astype(F32))
    delta_ref[...] = extra[: delta_ref.shape[0]]
    count = jnp.sum(extra[HALF_HEADS : HALF_HEADS + 1], axis=1, keepdims=True)
    count_ref[...] = jnp.broadcast_to(count, count_ref.shape)


def split_kernel(rows_ref, own_ref, send_ref):
    _, core = position()
    for ref, half in ((own_ref, core), (send_ref, 1 - core)):
        ref[...] = rows_ref[:, pl.ds(pl.multiple_of(half * HALF, HALF), HALF)]


def document_of(positions, lengths_ref):
    end = 0
    document = jnp.zeros_like(positions)
    for i in range(lengths_ref.shape[1]):
        end = end + lengths_ref[0, i]
        document += (positions >= end).astype(jnp.int32)
    return document


def setup_kernel(offsets, in_ref, target_ref, key_ref, k_ref, send_ref, bias_own, bias_other):
    chip, core = position()
    split_kernel(key_ref, k_ref, send_ref)
    enc_rows, dec_rows = bias_own.shape
    block = dec_rows // len(offsets)
    lane = lax.broadcasted_iota(jnp.int32, (1, dec_rows), 1)
    dec = lane + chip * block
    for j, offset in enumerate(offsets[1:], 1):
        dec = jnp.where(lane >= j * block, lane + ((chip ^ offset) - j) * block, dec)
    dec = document_of(dec, target_ref)
    for ref, side in ((bias_own, core), (bias_other, 1 - core)):
        enc = lax.broadcasted_iota(jnp.int32, (enc_rows, 1), 0) + (2 * chip + side) * enc_rows
        ref[...] = jnp.where(document_of(enc, in_ref) == dec, 0.0, NEVER)


def start_all(pairs, sems):
    copies = [pltpu.make_async_copy(a, b, sems.at[i]) for i, (a, b) in enumerate(pairs)]
    for copy in copies:
        copy.start()
    return copies


def rows_of(blocks, head):
    columns = slice(head * HEAD_SIZE, (head + 1) * HEAD_SIZE)
    return jnp.concatenate([block[:, columns] for block in blocks], 0)


def value_columns_of(head):
    _, core = position()
    first = core * HALF + head * HEAD_SIZE
    return pl.ds(pl.multiple_of(first, HEAD_SIZE), HEAD_SIZE)


def columns_of(head):
    return slice(head * HEAD_SIZE, (head + 1) * HEAD_SIZE)


def scores_kernel(offsets, delta_ref, bias_own, bias_other, key_ref, other_ref, *refs):
    count_ref, refs = refs[0], refs[1:]
    blocks, (stats_ref,) = refs[: len(offsets)], refs[len(offsets) :]
    rows = blocks[0].shape[0]
    dec_rows = rows * len(offsets)
    stats_ref[...] = jnp.broadcast_to(count_ref[0:1, 0:1], stats_ref.shape)
    stats_ref[HALF_HEADS:, :rows] = delta_ref[:HALF_HEADS]
    for head in range(HALF_HEADS):
        q = rows_of(blocks, head)
        scores = [
            dot(k[:, columns_of(head)], q, NT) * ROOT + bias[...]
            for k, bias in ((key_ref, bias_own), (other_ref, bias_other))
        ]
        top = functools.reduce(jnp.maximum, [jnp.max(s, axis=0, keepdims=True) for s in scores])
        top = jnp.maximum(top, -1e20)
        total = sum(jnp.sum(jnp.exp(s - top), axis=0, keepdims=True) for s in scores)
        stats_ref[head : head + 1, :dec_rows] = jnp.where(
            total > 0, top + jnp.log(jnp.maximum(total, 1e-30)), NEVER
        )


def gathered_stats(offsets, stats, rows):
    logs = []
    for sender, ref in zip(offsets, stats):
        order = [offsets.index(offset ^ sender) for offset in offsets]
        logs.append(
            jnp.concatenate([ref[:HALF_HEADS, j * rows : (j + 1) * rows] for j in order], 1)
        )
    top = functools.reduce(jnp.maximum, logs)
    log_total = top + jnp.log(sum(jnp.exp(log - top) for log in logs))
    delta = jnp.concatenate([ref[HALF_HEADS:, :rows] for ref in stats], 1)
    last = stats[0].shape[1] - 1
    return log_total, delta, sum(ref[0:1, last:] for ref in stats)


def grads_kernel(offsets, bias_own, bias_other, *refs):
    chips = len(offsets)
    stats, refs = refs[:chips], refs[chips:]
    q_blocks, refs = refs[:chips], refs[chips:]
    g_blocks, refs = refs[:chips], refs[chips:]
    (key_ref, key_other, value_ref, value_other), refs = refs[:4], refs[4:]
    dq_blocks, (keep_ref, send_ref, count_ref) = refs[:chips], refs[chips:]
    rows = q_blocks[0].shape[0]
    log_total, delta, count = gathered_stats(offsets, stats, rows)
    count_ref[...] = jnp.broadcast_to(count, count_ref.shape)
    for head in range(HALF_HEADS):
        columns = slice(head * HEAD_SIZE, (head + 1) * HEAD_SIZE)
        value_columns = slice(HALF + columns.start, HALF + columns.stop)
        line = slice(head, head + 1)
        q, g = rows_of(q_blocks, head), rows_of(g_blocks, head)
        dq = 0.0
        for key, value, bias, out_ref in (
            (key_ref, value_ref, bias_own, keep_ref),
            (key_other, value_other, bias_other, send_ref),
        ):
            k, v = key[:, columns], value[:, value_columns_of(head)]
            probs = jnp.exp(dot(k, q, NT) * ROOT + bias[...] - log_total[line])
            dscore = (probs * (dot(v, g, NT) - delta[line])).astype(BF16)
            dq += dot(dscore, k, TN)
            out_ref[:, columns] = (dot(dscore, q, NN) * ROOT).astype(BF16)
            out_ref[:, value_columns] = dot(probs.astype(BF16), g, NN).astype(BF16)
        dq = (dq * ROOT).astype(BF16)
        for j, block in enumerate(dq_blocks):
            block[:, columns] = dq[j * rows : (j + 1) * rows]


def key_end_kernel(rows_in_all, keep_ref, other_ref, *refs):
    counts, (dk_ref, dv_ref, factor_ref) = refs[:2], refs[2:]
    _, core = position()
    factor = rows_in_all / (counts[0][0:1, 0:1] + counts[1][0:1, 0:1])
    factor_ref[...] = jnp.broadcast_to(factor, factor_ref.shape)
    for ref, side in ((keep_ref, core), (other_ref, 1 - core)):
        columns = pl.ds(pl.multiple_of(side * HALF, HALF), HALF)
        dk_ref[:, columns] = (ref[:, :HALF].astype(F32) * factor).astype(BF16)
        dv_ref[:, columns] = (ref[:, HALF:].astype(F32) * factor).astype(BF16)


def query_end_kernel(factor_ref, *refs):
    parts, (send_ref, keep_ref) = refs[:-2], refs[-2:]
    _, core = position()
    summed = factor_ref[0:1, 0:1] * sum(part[...].astype(F32) for part in parts)
    half = summed.shape[0] // 2
    low, high = summed[:half], summed[half:]
    send_ref[...] = jnp.where(core == 0, high, low).astype(BF16)
    keep_ref[...] = jnp.where(core == 0, low, high).astype(BF16)


def in_order(own, other, core, axis):
    return jnp.where(
        core == 0, jnp.concatenate([own, other], axis), jnp.concatenate([other, own], axis)
    )


def local(queries, keys, values, attn_out, out_grad, loss_mask, input_lengths, target_lengths):
    query_rows, key_rows, value_rows = queries[0], keys[0], values[0]
    dec_local, enc_local = query_rows.shape[0], key_rows.shape[0]
    chips = lax.axis_size("seq") // 2
    data_groups = lax.axis_size("dp")
    _, core = position()
    dec_rows = 2 * chips * dec_local
    enc_rows = 2 * enc_local
    block = (2 * dec_local, HALF)
    lengths = (input_lengths[0], target_lengths[0])

    def shaped(*shape, dtype=BF16):
        return jax.ShapeDtypeStruct(shape, dtype)

    def gather(block):
        blocks = [block]
        apart = chips // 2
        while apart > 1:
            blocks += [across(one, apart) for one in blocks]
            apart //= 2
        return blocks, across(block, 1)

    def forwarded(blocks):
        return [across(one, 1) for one in blocks[1:]]

    offsets = [0]
    apart = chips // 2
    while apart:
        offsets += [offset ^ apart for offset in offsets]
        apart //= 2

    features = HEADS * HEAD_SIZE
    sent = shaped(dec_local, HALF + EXTRA)
    block = shaped(2 * dec_local, HALF)

    with jax.named_scope("sibling_exchange"):
        q_recv = to_sibling(query_rows)
        g_send, g_keep = kernel_call(
            prepare_kernel,
            (sent, sent),
            [ANY] * 3,
            (VMEM, VMEM),
            [
                pltpu.VMEM((dec_local, features), BF16),
                pltpu.VMEM((dec_local, features), BF16),
                pltpu.VMEM((1, dec_local), jnp.int32),
                pltpu.SemaphoreType.DMA((3,)),
            ],
            10**5,
            10**6,
            "prepare",
            60 * 1024 * 1024,
        )(out_grad[0], attn_out[0], loss_mask)
        g_recv = to_sibling(g_send)

    with jax.named_scope("query_gather"):
        q_recv, _ = after(q_recv, g_keep)
        q_block = kernel_call(
            join_queries_kernel, block, [VMEM, VMEM], VMEM, [], 10**5, 10**5, "join_queries"
        )(query_rows, q_recv)
        q_far, q_near = gather(q_block)

    with jax.named_scope("setup"):
        half_rows = shaped(enc_local, HALF)
        bias = shaped(enc_local, dec_rows, dtype=F32)
        k_own, k_send, bias_own, bias_other = kernel_call(
            functools.partial(setup_kernel, offsets),
            (half_rows, half_rows, bias, bias),
            [SMEM] * 2 + [VMEM],
            (VMEM,) * 4,
            [],
            10**6,
            2**22,
            "setup",
        )(*lengths, after(key_rows, q_block)[0])

    with jax.named_scope("cotangent_gather"):
        small = shaped(8, 2 * dec_local, dtype=F32)
        g_block, delta, count = kernel_call(
            join_cotangents_kernel,
            (block, small, shaped(8, EXTRA, dtype=F32)),
            [VMEM, VMEM],
            (VMEM,) * 3,
            [],
            10**5,
            10**5,
            "join_cotangents",
        )(g_keep, g_recv)

    def over_groups(count, apart):
        return lax.ppermute(count, "dp", [(i, i ^ apart) for i in range(data_groups)])

    with jax.named_scope("mask_count"):
        apart = 1
        while apart < data_groups // 2:
            count = count + after(over_groups(count, apart), bias_own)[0]
            apart *= 2
        rows_in_all = float(data_groups * dec_rows)

    with jax.named_scope("query_forward"):
        q_far = [q_far[0], *(after(one, bias_own, count)[0] for one in q_far[1:])]
        q_blocks = [*q_far, q_near, *forwarded(q_far)]

    with jax.named_scope("cotangent_gather"):
        g_far, g_near = gather(after(g_block, *q_far, q_near)[0])

    with jax.named_scope("key_exchange"):
        v_recv = to_sibling(value_rows)
        k_send, v_recv, *_ = after(k_send, v_recv, *q_far, q_near)
        k_recv = to_sibling(k_send)

    with jax.named_scope("scores"):
        width = (dec_rows // 128 + 1) * 128
        stats = kernel_call(
            functools.partial(scores_kernel, offsets),
            shaped(2 * HALF_HEADS, width, dtype=F32),
            [VMEM] * (chips + 6),
            VMEM,
            [],
            2 * dec_rows * enc_rows * HALF,
            2 * (dec_rows + enc_rows) * HALF,
            "scores",
        )(delta, bias_own, bias_other, k_own, k_recv, count, *q_blocks)

    with jax.named_scope("stats_exchange"):
        all_stats = [stats] + [across(stats, offset) for offset in offsets[1:]]
        near_stats = all_stats[offsets.index(1)]

    with jax.named_scope("cotangent_forward"):
        g_far = [g_far[0], *(after(one, near_stats)[0] for one in g_far[1:])]
        g_blocks = [*g_far, g_near, *forwarded(g_far)]

    with jax.named_scope("grads"):
        both = shaped(enc_local, 2 * HALF)
        *dq_blocks, dkv_keep, dkv_send, count = kernel_call(
            functools.partial(grads_kernel, offsets),
            (block,) * chips + (both, both, shaped(8, EXTRA, dtype=F32)),
            [VMEM] * (3 * chips + 6),
            (VMEM,) * (chips + 3),
            [],
            10 * dec_rows * enc_rows * HALF,
            4 * (dec_rows + 2 * enc_rows) * HALF,
            "grads",
        )(bias_own, bias_other, *all_stats, *q_blocks, *g_blocks, k_own, k_recv, value_rows, v_recv)

    with jax.named_scope("query_grad_sum"):
        parts = [dq_blocks[0]]
        for j in sorted(range(1, chips), key=lambda j: -offsets[j]):
            parts.append(across(dq_blocks[j], offsets[j]))

    with jax.named_scope("key_grad_end"):
        dkv_recv = to_sibling(dkv_send)
        counts = (count, over_groups(count, data_groups // 2))
        whole = shaped(enc_local, features)
        grad_keys, grad_values, factor = kernel_call(
            functools.partial(key_end_kernel, rows_in_all),
            (whole, whole, shaped(8, EXTRA, dtype=F32)),
            [VMEM] * 4,
            (VMEM, VMEM, VMEM),
            [],
            10**6,
            2**22,
            "key_end",
        )(dkv_keep, dkv_recv, *counts)

    with jax.named_scope("query_grad_end"):
        half = shaped(dec_local, HALF)
        dq_send, dq_keep = kernel_call(
            query_end_kernel,
            (half, half),
            [VMEM] * (chips + 1),
            (VMEM, VMEM),
            [],
            10**5,
            10**6,
            "query_end",
        )(factor, *parts)
        grad_queries = in_order(dq_keep, to_sibling(dq_send), core, 1)

    return grad_queries[None], grad_keys[None], grad_values[None]


def solution(mesh):
    return jax.shard_map(
        local,
        mesh=mesh,
        in_specs=(
            P("dp", "seq", None),
            P("dp", "seq", None),
            P("dp", "seq", None),
            P("dp", "seq", None),
            P("dp", "seq", None),
            P("dp", "seq"),
            P("dp", None, None),
            P("dp", None, None),
        ),
        out_specs=(P("dp", "seq", None), P("dp", "seq", None), P("dp", "seq", None)),
        check_vma=False,
    )
```

```python
import functools
import jax
import jax.numpy as jnp
from jax import lax
from jax.experimental import pallas as pl
from jax.experimental.pallas import tpu as pltpu
from jax.sharding import PartitionSpec as P

HEADS = 8
HEAD_SIZE = 256
HALF_HEADS = HEADS // 2
HALF = HALF_HEADS * HEAD_SIZE
EXTRA = 128
ROOT = HEAD_SIZE**-0.5
NEVER = -1e30
VMEM_LIMIT = 24 * 1024 * 1024
F32 = jnp.float32
BF16 = jnp.bfloat16
ANY = pl.BlockSpec(memory_space=pl.ANY)
VMEM = pl.BlockSpec(memory_space=pltpu.VMEM)
SMEM = pl.BlockSpec(memory_space=pltpu.SMEM)
NT = (((1,), (1,)), ((), ()))
TN = (((0,), (0,)), ((), ()))
NN = (((1,), (0,)), ((), ()))


def dot(a, b, dims):
    return lax.dot_general(a, b, dims, preferred_element_type=F32)


def position():
    me = lax.axis_index("seq")
    return me >> 1, me & 1


def to_sibling(block):
    count = lax.axis_size("seq")
    return lax.ppermute(block, "seq", [(i, i ^ 1) for i in range(count)])


def across(block, apart):
    count = lax.axis_size("seq")
    return lax.ppermute(block, "seq", [(i, i ^ (2 * apart)) for i in range(count)])


def after(block, *others):
    return lax.optimization_barrier((block, *others))


def kernel_call(
    body, out_shape, in_specs, out_specs, scratch, flops, moved, name, vmem_limit=VMEM_LIMIT
):
    return pl.pallas_call(
        body,
        out_shape=out_shape,
        in_specs=in_specs,
        out_specs=out_specs,
        scratch_shapes=scratch,
        compiler_params=pltpu.CompilerParams(vmem_limit_bytes=vmem_limit),
        cost_estimate=pl.CostEstimate(flops=flops, bytes_accessed=moved, transcendentals=0),
        name=name,
    )


def prepare_kernel(
    grad_ref, out_ref, mask_ref, send_ref, keep_ref, grad_held, out_held, mask_held, sems
):
    _, core = position()
    rows = grad_ref.shape[0]
    copies = start_all(
        [(mask_ref, mask_held), (grad_ref, grad_held), (out_ref, out_held)], sems
    )
    copies[0].wait()
    mask_row = mask_held[...].astype(F32)
    here = lax.broadcasted_iota(jnp.int32, (rows, rows), 0) == lax.broadcasted_iota(
        jnp.int32, (rows, rows), 1
    )
    mask = jnp.sum(jnp.where(here, mask_row, 0.0), axis=1, keepdims=True)
    lane = lax.broadcasted_iota(jnp.int32, (rows, EXTRA), 1)
    for copy in copies[1:]:
        copy.wait()
    masked = grad_held[...].astype(F32) * mask
    products = masked * out_held[...].astype(F32)
    grad_held[...] = masked.astype(BF16)
    halves = []
    for half in range(2):
        extra = jnp.where(lane == HALF_HEADS, mask, 0.0)
        for head in range(HALF_HEADS):
            first = half * HALF + head * HEAD_SIZE
            delta = jnp.sum(products[:, first : first + HEAD_SIZE], axis=1, keepdims=True)
            extra = jnp.where(lane == head, delta, extra)
        halves.append(extra)
    for ref, half in ((send_ref, 1 - core), (keep_ref, core)):
        ref[:, :HALF] = grad_held[:, pl.ds(pl.multiple_of(half * HALF, HALF), HALF)]
        ref[:, HALF:] = jnp.where(half == 0, halves[0], halves[1]).astype(BF16)


def in_core_order(own, other, core):
    own, other = own.astype(F32), other.astype(F32)
    joined = jnp.where(
        core == 0, jnp.concatenate([own, other], 0), jnp.concatenate([other, own], 0)
    )
    return joined.astype(BF16)


def join_queries_kernel(own_ref, other_ref, joined_ref):
    _, core = position()
    mine = pl.ds(pl.multiple_of(core * HALF, HALF), HALF)
    joined_ref[...] = in_core_order(own_ref[:, mine], other_ref[:, mine], core)


def join_cotangents_kernel(own_ref, other_ref, joined_ref, delta_ref, count_ref):
    _, core = position()
    joined_ref[...] = in_core_order(own_ref[:, :HALF], other_ref[:, :HALF], core)
    extra = jnp.transpose(in_core_order(own_ref[:, HALF:], other_ref[:, HALF:], core).astype(F32))
    delta_ref[...] = extra[: delta_ref.shape[0]]
    count = jnp.sum(extra[HALF_HEADS : HALF_HEADS + 1], axis=1, keepdims=True)
    count_ref[...] = jnp.broadcast_to(count, count_ref.shape)


def split_kernel(rows_ref, own_ref, send_ref):
    _, core = position()
    for ref, half in ((own_ref, core), (send_ref, 1 - core)):
        ref[...] = rows_ref[:, pl.ds(pl.multiple_of(half * HALF, HALF), HALF)]


def document_of(positions, lengths_ref):
    end = 0
    document = jnp.zeros_like(positions)
    for i in range(lengths_ref.shape[1]):
        end = end + lengths_ref[0, i]
        document += (positions >= end).astype(jnp.int32)
    return document


def setup_kernel(offsets, in_ref, target_ref, key_ref, k_ref, send_ref, bias_own, bias_other):
    chip, core = position()
    split_kernel(key_ref, k_ref, send_ref)
    enc_rows, dec_rows = bias_own.shape
    block = dec_rows // len(offsets)
    lane = lax.broadcasted_iota(jnp.int32, (1, dec_rows), 1)
    dec = lane + chip * block
    for j, offset in enumerate(offsets[1:], 1):
        dec = jnp.where(lane >= j * block, lane + ((chip ^ offset) - j) * block, dec)
    dec = document_of(dec, target_ref)
    for ref, side in ((bias_own, core), (bias_other, 1 - core)):
        enc = lax.broadcasted_iota(jnp.int32, (enc_rows, 1), 0) + (2 * chip + side) * enc_rows
        ref[...] = jnp.where(document_of(enc, in_ref) == dec, 0.0, NEVER)


def start_all(pairs, sems):
    copies = [pltpu.make_async_copy(a, b, sems.at[i]) for i, (a, b) in enumerate(pairs)]
    for copy in copies:
        copy.start()
    return copies


def rows_of(blocks, head):
    columns = slice(head * HEAD_SIZE, (head + 1) * HEAD_SIZE)
    return jnp.concatenate([block[:, columns] for block in blocks], 0)


def value_columns_of(head):
    _, core = position()
    first = core * HALF + head * HEAD_SIZE
    return pl.ds(pl.multiple_of(first, HEAD_SIZE), HEAD_SIZE)


def columns_of(head):
    return slice(head * HEAD_SIZE, (head + 1) * HEAD_SIZE)


def scores_kernel(offsets, delta_ref, bias_own, bias_other, key_ref, other_ref, *refs):
    count_ref, refs = refs[0], refs[1:]
    blocks, (stats_ref,) = refs[: len(offsets)], refs[len(offsets) :]
    rows = blocks[0].shape[0]
    dec_rows = rows * len(offsets)
    stats_ref[...] = jnp.broadcast_to(count_ref[0:1, 0:1], stats_ref.shape)
    stats_ref[HALF_HEADS:, :dec_rows] = jnp.zeros((HALF_HEADS, dec_rows), F32)
    stats_ref[HALF_HEADS:, :rows] = delta_ref[:HALF_HEADS]
    for head in range(HALF_HEADS):
        q = rows_of(blocks, head)
        scores = [
            dot(k[:, columns_of(head)], q, NT) * ROOT + bias[...]
            for k, bias in ((key_ref, bias_own), (other_ref, bias_other))
        ]
        top = functools.reduce(jnp.maximum, [jnp.max(s, axis=0, keepdims=True) for s in scores])
        top = jnp.maximum(top, -1e20)
        total = sum(jnp.sum(jnp.exp(s - top), axis=0, keepdims=True) for s in scores)
        stats_ref[head : head + 1, :dec_rows] = jnp.where(
            total > 0, top + jnp.log(jnp.maximum(total, 1e-30)), NEVER
        )


def merged_stats(offsets, apart, own_ref, other_ref, dec_rows):
    rows = dec_rows // len(offsets)
    order = [offsets.index(offset ^ apart) for offset in offsets]
    own = own_ref[:, :dec_rows]
    other = jnp.concatenate([other_ref[:, j * rows : (j + 1) * rows] for j in order], 1)
    logs = own[:HALF_HEADS], other[:HALF_HEADS]
    top = jnp.maximum(jnp.maximum(*logs), -1e20)
    total = sum(jnp.exp(log - top) for log in logs)
    log_total = jnp.where(total > 0, top + jnp.log(jnp.maximum(total, 1e-30)), NEVER)
    last = own_ref.shape[1] - 1
    count = own_ref[0:1, last:] + other_ref[0:1, last:]
    return log_total, own[HALF_HEADS:] + other[HALF_HEADS:], count


def merge_kernel(offsets, apart, dec_rows, own_ref, other_ref, stats_ref):
    log_total, delta, count = merged_stats(offsets, apart, own_ref, other_ref, dec_rows)
    stats_ref[...] = jnp.broadcast_to(count, stats_ref.shape)
    stats_ref[:HALF_HEADS, :dec_rows] = log_total
    stats_ref[HALF_HEADS:, :dec_rows] = delta


def grads_kernel(offsets, bias_own, bias_other, *refs):
    chips = len(offsets)
    stats, refs = refs[:2], refs[2:]
    q_blocks, refs = refs[:chips], refs[chips:]
    g_blocks, refs = refs[:chips], refs[chips:]
    (key_ref, key_other, value_ref, value_other), refs = refs[:4], refs[4:]
    dq_blocks, (keep_ref, send_ref, count_ref) = refs[:chips], refs[chips:]
    rows = q_blocks[0].shape[0]
    log_total, delta, count = merged_stats(offsets, chips // 2, *stats, rows * chips)
    count_ref[...] = jnp.broadcast_to(count, count_ref.shape)
    for head in range(HALF_HEADS):
        columns = slice(head * HEAD_SIZE, (head + 1) * HEAD_SIZE)
        value_columns = slice(HALF + columns.start, HALF + columns.stop)
        line = slice(head, head + 1)
        q, g = rows_of(q_blocks, head), rows_of(g_blocks, head)
        dq = 0.0
        for key, value, bias, out_ref in (
            (key_ref, value_ref, bias_own, keep_ref),
            (key_other, value_other, bias_other, send_ref),
        ):
            k, v = key[:, columns], value[:, value_columns_of(head)]
            probs = jnp.exp(dot(k, q, NT) * ROOT + bias[...] - log_total[line])
            dscore = (probs * (dot(v, g, NT) - delta[line])).astype(BF16)
            dq += dot(dscore, k, TN)
            out_ref[:, columns] = (dot(dscore, q, NN) * ROOT).astype(BF16)
            out_ref[:, value_columns] = dot(probs.astype(BF16), g, NN).astype(BF16)
        dq = (dq * ROOT).astype(BF16)
        for j, block in enumerate(dq_blocks):
            block[:, columns] = dq[j * rows : (j + 1) * rows]


def key_end_kernel(rows_in_all, keep_ref, other_ref, *refs):
    counts, (dk_ref, dv_ref, factor_ref) = refs[:2], refs[2:]
    _, core = position()
    factor = rows_in_all / (counts[0][0:1, 0:1] + counts[1][0:1, 0:1])
    factor_ref[...] = jnp.broadcast_to(factor, factor_ref.shape)
    for ref, side in ((keep_ref, core), (other_ref, 1 - core)):
        columns = pl.ds(pl.multiple_of(side * HALF, HALF), HALF)
        dk_ref[:, columns] = (ref[:, :HALF].astype(F32) * factor).astype(BF16)
        dv_ref[:, columns] = (ref[:, HALF:].astype(F32) * factor).astype(BF16)


def query_end_kernel(factor_ref, *refs):
    parts, (send_ref, keep_ref) = refs[:-2], refs[-2:]
    _, core = position()
    summed = factor_ref[0:1, 0:1] * sum(part[...].astype(F32) for part in parts)
    half = summed.shape[0] // 2
    low, high = summed[:half], summed[half:]
    send_ref[...] = jnp.where(core == 0, high, low).astype(BF16)
    keep_ref[...] = jnp.where(core == 0, low, high).astype(BF16)


def in_order(own, other, core, axis):
    return jnp.where(
        core == 0, jnp.concatenate([own, other], axis), jnp.concatenate([other, own], axis)
    )


def local(queries, keys, values, attn_out, out_grad, loss_mask, input_lengths, target_lengths):
    query_rows, key_rows, value_rows = queries[0], keys[0], values[0]
    dec_local, enc_local = query_rows.shape[0], key_rows.shape[0]
    chips = lax.axis_size("seq") // 2
    data_groups = lax.axis_size("dp")
    _, core = position()
    dec_rows = 2 * chips * dec_local
    enc_rows = 2 * enc_local
    block = (2 * dec_local, HALF)
    lengths = (input_lengths[0], target_lengths[0])

    def shaped(*shape, dtype=BF16):
        return jax.ShapeDtypeStruct(shape, dtype)

    def gather(block):
        blocks = [block]
        apart = chips // 2
        while apart > 1:
            blocks += [across(one, apart) for one in blocks]
            apart //= 2
        return blocks, across(block, 1)

    def forwarded(blocks):
        return [across(one, 1) for one in blocks[1:]]

    offsets = [0]
    apart = chips // 2
    while apart:
        offsets += [offset ^ apart for offset in offsets]
        apart //= 2

    features = HEADS * HEAD_SIZE
    sent = shaped(dec_local, HALF + EXTRA)
    block = shaped(2 * dec_local, HALF)

    with jax.named_scope("sibling_exchange"):
        q_recv = to_sibling(query_rows)
        g_send, g_keep = kernel_call(
            prepare_kernel,
            (sent, sent),
            [ANY] * 3,
            (VMEM, VMEM),
            [
                pltpu.VMEM((dec_local, features), BF16),
                pltpu.VMEM((dec_local, features), BF16),
                pltpu.VMEM((1, dec_local), jnp.int32),
                pltpu.SemaphoreType.DMA((3,)),
            ],
            10**5,
            10**6,
            "prepare",
            60 * 1024 * 1024,
        )(out_grad[0], attn_out[0], loss_mask)
        g_recv = to_sibling(g_send)

    with jax.named_scope("query_gather"):
        q_recv, _ = after(q_recv, g_keep)
        q_block = kernel_call(
            join_queries_kernel, block, [VMEM, VMEM], VMEM, [], 10**5, 10**5, "join_queries"
        )(query_rows, q_recv)
        q_far, q_near = gather(q_block)

    with jax.named_scope("setup"):
        half_rows = shaped(enc_local, HALF)
        bias = shaped(enc_local, dec_rows, dtype=F32)
        k_own, k_send, bias_own, bias_other = kernel_call(
            functools.partial(setup_kernel, offsets),
            (half_rows, half_rows, bias, bias),
            [SMEM] * 2 + [VMEM],
            (VMEM,) * 4,
            [],
            10**6,
            2**22,
            "setup",
        )(*lengths, after(key_rows, q_block)[0])

    with jax.named_scope("cotangent_gather"):
        small = shaped(8, 2 * dec_local, dtype=F32)
        g_block, delta, count = kernel_call(
            join_cotangents_kernel,
            (block, small, shaped(8, EXTRA, dtype=F32)),
            [VMEM, VMEM],
            (VMEM,) * 3,
            [],
            10**5,
            10**5,
            "join_cotangents",
        )(g_keep, g_recv)

    def over_groups(count, apart):
        return lax.ppermute(count, "dp", [(i, i ^ apart) for i in range(data_groups)])

    with jax.named_scope("mask_count"):
        apart = 1
        while apart < data_groups // 2:
            count = count + after(over_groups(count, apart), bias_own)[0]
            apart *= 2
        rows_in_all = float(data_groups * dec_rows)

    with jax.named_scope("query_forward"):
        q_far = [q_far[0], *(after(one, bias_own, count, q_near)[0] for one in q_far[1:])]
        q_blocks = [*q_far, q_near, *forwarded(q_far)]

    with jax.named_scope("cotangent_gather"):
        sent = after(g_block, *q_far, q_near)[0]
        g_blocks = [g_block] + [across(sent, offset) for offset in offsets[1:]]

    with jax.named_scope("key_exchange"):
        v_recv = to_sibling(value_rows)
        k_send, v_recv, *_ = after(k_send, v_recv, *q_far, q_near)
        k_recv = to_sibling(k_send)

    with jax.named_scope("scores"):
        width = (dec_rows // 128 + 1) * 128
        stats = kernel_call(
            functools.partial(scores_kernel, offsets),
            shaped(2 * HALF_HEADS, width, dtype=F32),
            [VMEM] * (chips + 6),
            VMEM,
            [],
            2 * dec_rows * enc_rows * HALF,
            2 * (dec_rows + enc_rows) * HALF,
            "scores",
        )(delta, bias_own, bias_other, k_own, k_recv, count, *q_blocks)

    with jax.named_scope("stats_exchange"):
        apart = 1
        while apart < chips // 2:
            stats = kernel_call(
                functools.partial(merge_kernel, offsets, apart, dec_rows),
                shaped(2 * HALF_HEADS, width, dtype=F32),
                [VMEM] * 2,
                VMEM,
                [],
                1,
                1,
                "merge_stats",
            )(stats, across(stats, apart))
            apart *= 2
        all_stats = stats, across(stats, apart)

    with jax.named_scope("grads"):
        both = shaped(enc_local, 2 * HALF)
        *dq_blocks, dkv_keep, dkv_send, count = kernel_call(
            functools.partial(grads_kernel, offsets),
            (block,) * chips + (both, both, shaped(8, EXTRA, dtype=F32)),
            [VMEM] * (2 * chips + 8),
            (VMEM,) * (chips + 3),
            [],
            10 * dec_rows * enc_rows * HALF,
            4 * (dec_rows + 2 * enc_rows) * HALF,
            "grads",
        )(bias_own, bias_other, *all_stats, *q_blocks, *g_blocks, k_own, k_recv, value_rows, v_recv)

    with jax.named_scope("query_grad_sum"):
        parts = [dq_blocks[0]]
        for j in sorted(range(1, chips), key=lambda j: -offsets[j]):
            parts.append(across(dq_blocks[j], offsets[j]))

    with jax.named_scope("key_grad_end"):
        dkv_recv = to_sibling(dkv_send)
        counts = (count, over_groups(count, data_groups // 2))
        whole = shaped(enc_local, features)
        grad_keys, grad_values, factor = kernel_call(
            functools.partial(key_end_kernel, rows_in_all),
            (whole, whole, shaped(8, EXTRA, dtype=F32)),
            [VMEM] * 4,
            (VMEM, VMEM, VMEM),
            [],
            10**6,
            2**22,
            "key_end",
        )(dkv_keep, dkv_recv, *counts)

    with jax.named_scope("query_grad_end"):
        half = shaped(dec_local, HALF)
        dq_send, dq_keep = kernel_call(
            query_end_kernel,
            (half, half),
            [VMEM] * (chips + 1),
            (VMEM, VMEM),
            [],
            10**5,
            10**6,
            "query_end",
        )(factor, *parts)
        grad_queries = in_order(dq_keep, to_sibling(dq_send), core, 1)

    return grad_queries[None], grad_keys[None], grad_values[None]


def solution(mesh):
    return jax.shard_map(
        local,
        mesh=mesh,
        in_specs=(
            P("dp", "seq", None),
            P("dp", "seq", None),
            P("dp", "seq", None),
            P("dp", "seq", None),
            P("dp", "seq", None),
            P("dp", "seq"),
            P("dp", None, None),
            P("dp", None, None),
        ),
        out_specs=(P("dp", "seq", None), P("dp", "seq", None), P("dp", "seq", None)),
        check_vma=False,
    )
```

```python
import functools
import jax
import jax.numpy as jnp
from jax import lax
from jax.experimental import pallas as pl
from jax.experimental.pallas import tpu as pltpu
from jax.sharding import PartitionSpec as P

HEADS = 8
HEAD_SIZE = 256
HALF_HEADS = HEADS // 2
HALF = HALF_HEADS * HEAD_SIZE
EXTRA = 128
ROOT = HEAD_SIZE**-0.5
NEVER = -1e30
VMEM_LIMIT = 24 * 1024 * 1024
F32 = jnp.float32
BF16 = jnp.bfloat16
ANY = pl.BlockSpec(memory_space=pl.ANY)
VMEM = pl.BlockSpec(memory_space=pltpu.VMEM)
SMEM = pl.BlockSpec(memory_space=pltpu.SMEM)
NT = (((1,), (1,)), ((), ()))
TN = (((0,), (0,)), ((), ()))
NN = (((1,), (0,)), ((), ()))


def dot(a, b, dims):
    return lax.dot_general(a, b, dims, preferred_element_type=F32)


def position():
    me = lax.axis_index("seq")
    return me >> 1, me & 1


def to_sibling(block):
    count = lax.axis_size("seq")
    return lax.ppermute(block, "seq", [(i, i ^ 1) for i in range(count)])


def across(block, apart):
    count = lax.axis_size("seq")
    return lax.ppermute(block, "seq", [(i, i ^ (2 * apart)) for i in range(count)])


def after(block, *others):
    return lax.optimization_barrier((block, *others))


def kernel_call(
    body, out_shape, in_specs, out_specs, scratch, flops, moved, name, vmem_limit=VMEM_LIMIT
):
    return pl.pallas_call(
        body,
        out_shape=out_shape,
        in_specs=in_specs,
        out_specs=out_specs,
        scratch_shapes=scratch,
        compiler_params=pltpu.CompilerParams(vmem_limit_bytes=vmem_limit),
        cost_estimate=pl.CostEstimate(flops=flops, bytes_accessed=moved, transcendentals=0),
        name=name,
    )


def prepare_kernel(
    grad_ref, out_ref, mask_ref, send_ref, keep_ref, grad_held, out_held, mask_held, sems
):
    _, core = position()
    rows = grad_ref.shape[0]
    copies = start_all(
        [(mask_ref, mask_held), (grad_ref, grad_held), (out_ref, out_held)], sems
    )
    copies[0].wait()
    mask_row = mask_held[...].astype(F32)
    here = lax.broadcasted_iota(jnp.int32, (rows, rows), 0) == lax.broadcasted_iota(
        jnp.int32, (rows, rows), 1
    )
    mask = jnp.sum(jnp.where(here, mask_row, 0.0), axis=1, keepdims=True)
    lane = lax.broadcasted_iota(jnp.int32, (rows, EXTRA), 1)
    for copy in copies[1:]:
        copy.wait()
    masked = grad_held[...].astype(F32) * mask
    products = masked * out_held[...].astype(F32)
    grad_held[...] = masked.astype(BF16)
    halves = []
    for half in range(2):
        extra = jnp.where(lane == HALF_HEADS, mask, 0.0)
        for head in range(HALF_HEADS):
            first = half * HALF + head * HEAD_SIZE
            delta = jnp.sum(products[:, first : first + HEAD_SIZE], axis=1, keepdims=True)
            extra = jnp.where(lane == head, delta, extra)
        halves.append(extra)
    for ref, half in ((send_ref, 1 - core), (keep_ref, core)):
        ref[:, :HALF] = grad_held[:, pl.ds(pl.multiple_of(half * HALF, HALF), HALF)]
        ref[:, HALF:] = jnp.where(half == 0, halves[0], halves[1]).astype(BF16)


def in_core_order(own, other, core):
    own, other = own.astype(F32), other.astype(F32)
    joined = jnp.where(
        core == 0, jnp.concatenate([own, other], 0), jnp.concatenate([other, own], 0)
    )
    return joined.astype(BF16)


def join_queries_kernel(own_ref, other_ref, joined_ref):
    _, core = position()
    mine = pl.ds(pl.multiple_of(core * HALF, HALF), HALF)
    joined = in_core_order(own_ref[:, mine], other_ref[:, mine], core)
    joined_ref[...] = (joined.astype(F32) * ROOT).astype(BF16)


def join_cotangents_kernel(own_ref, other_ref, joined_ref, delta_ref, count_ref):
    _, core = position()
    joined_ref[...] = in_core_order(own_ref[:, :HALF], other_ref[:, :HALF], core)
    extra = jnp.transpose(in_core_order(own_ref[:, HALF:], other_ref[:, HALF:], core).astype(F32))
    delta_ref[...] = extra[: delta_ref.shape[0]]
    count = jnp.sum(extra[HALF_HEADS : HALF_HEADS + 1], axis=1, keepdims=True)
    count_ref[...] = jnp.broadcast_to(count, count_ref.shape)


def split_kernel(rows_ref, own_ref, send_ref):
    _, core = position()
    for ref, half in ((own_ref, core), (send_ref, 1 - core)):
        ref[...] = rows_ref[:, pl.ds(pl.multiple_of(half * HALF, HALF), HALF)]


def document_of(positions, lengths_ref):
    end = 0
    document = jnp.zeros_like(positions)
    for i in range(lengths_ref.shape[1]):
        end = end + lengths_ref[0, i]
        document += (positions >= end).astype(jnp.int32)
    return document


def setup_kernel(offsets, in_ref, target_ref, key_ref, k_ref, send_ref, bias_own, bias_other):
    chip, core = position()
    split_kernel(key_ref, k_ref, send_ref)
    enc_rows, dec_rows = bias_own.shape
    block = dec_rows // len(offsets)
    lane = lax.broadcasted_iota(jnp.int32, (1, dec_rows), 1)
    dec = lane + chip * block
    for j, offset in enumerate(offsets[1:], 1):
        dec = jnp.where(lane >= j * block, lane + ((chip ^ offset) - j) * block, dec)
    dec = document_of(dec, target_ref)
    for ref, side in ((bias_own, core), (bias_other, 1 - core)):
        enc = lax.broadcasted_iota(jnp.int32, (enc_rows, 1), 0) + (2 * chip + side) * enc_rows
        ref[...] = jnp.where(document_of(enc, in_ref) == dec, 0.0, NEVER)


def start_all(pairs, sems):
    copies = [pltpu.make_async_copy(a, b, sems.at[i]) for i, (a, b) in enumerate(pairs)]
    for copy in copies:
        copy.start()
    return copies


def rows_of(blocks, head):
    columns = slice(head * HEAD_SIZE, (head + 1) * HEAD_SIZE)
    return jnp.concatenate([block[:, columns] for block in blocks], 0)


def value_columns_of(head):
    _, core = position()
    first = core * HALF + head * HEAD_SIZE
    return pl.ds(pl.multiple_of(first, HEAD_SIZE), HEAD_SIZE)


def columns_of(head):
    return slice(head * HEAD_SIZE, (head + 1) * HEAD_SIZE)


def scores_kernel(offsets, delta_ref, bias_own, bias_other, key_ref, other_ref, *refs):
    count_ref, refs = refs[0], refs[1:]
    blocks, (stats_ref,) = refs[: len(offsets)], refs[len(offsets) :]
    rows = blocks[0].shape[0]
    dec_rows = rows * len(offsets)
    stats_ref[...] = jnp.broadcast_to(count_ref[0:1, 0:1], stats_ref.shape)
    stats_ref[HALF_HEADS:, :rows] = delta_ref[:HALF_HEADS]
    for head in range(HALF_HEADS):
        q = rows_of(blocks, head)
        scores = [
            dot(k[:, columns_of(head)], q, NT) + bias[...]
            for k, bias in ((key_ref, bias_own), (other_ref, bias_other))
        ]
        top = functools.reduce(jnp.maximum, [jnp.max(s, axis=0, keepdims=True) for s in scores])
        top = jnp.maximum(top, -1e20)
        total = sum(jnp.sum(jnp.exp(s - top), axis=0, keepdims=True) for s in scores)
        stats_ref[head : head + 1, :dec_rows] = jnp.where(
            total > 0, top + jnp.log(jnp.maximum(total, 1e-30)), NEVER
        )


def gathered_stats(offsets, stats, rows):
    logs = []
    for sender, ref in zip(offsets, stats):
        order = [offsets.index(offset ^ sender) for offset in offsets]
        logs.append(
            jnp.concatenate([ref[:HALF_HEADS, j * rows : (j + 1) * rows] for j in order], 1)
        )
    top = functools.reduce(jnp.maximum, logs)
    log_total = top + jnp.log(sum(jnp.exp(log - top) for log in logs))
    delta = jnp.concatenate([ref[HALF_HEADS:, :rows] for ref in stats], 1)
    last = stats[0].shape[1] - 1
    return log_total, delta, sum(ref[0:1, last:] for ref in stats)


def grads_kernel(offsets, bias_own, bias_other, *refs):
    chips = len(offsets)
    stats, refs = refs[:chips], refs[chips:]
    q_blocks, refs = refs[:chips], refs[chips:]
    g_blocks, refs = refs[:chips], refs[chips:]
    (key_ref, key_other, value_ref, value_other), refs = refs[:4], refs[4:]
    dq_blocks, (keep_ref, send_ref, count_ref) = refs[:chips], refs[chips:]
    rows = q_blocks[0].shape[0]
    log_total, delta, count = gathered_stats(offsets, stats, rows)
    count_ref[...] = jnp.broadcast_to(count, count_ref.shape)
    for head in range(HALF_HEADS):
        columns = slice(head * HEAD_SIZE, (head + 1) * HEAD_SIZE)
        value_columns = slice(HALF + columns.start, HALF + columns.stop)
        line = slice(head, head + 1)
        q, g = rows_of(q_blocks, head), rows_of(g_blocks, head)
        dq = 0.0
        for key, value, bias, out_ref in (
            (key_ref, value_ref, bias_own, keep_ref),
            (key_other, value_other, bias_other, send_ref),
        ):
            k, v = key[:, columns], value[:, value_columns_of(head)]
            probs = jnp.exp(dot(k, q, NT) + bias[...] - log_total[line])
            dscore = (probs * (dot(v, g, NT) - delta[line])).astype(BF16)
            dq += dot(dscore, k, TN)
            out_ref[:, columns] = dot(dscore, q, NN).astype(BF16)
            out_ref[:, value_columns] = dot(probs.astype(BF16), g, NN).astype(BF16)
        dq = dq.astype(BF16)
        for j, block in enumerate(dq_blocks):
            block[:, columns] = dq[j * rows : (j + 1) * rows]


def key_end_kernel(rows_in_all, keep_ref, other_ref, *refs):
    counts, (dk_ref, dv_ref, factor_ref) = refs[:2], refs[2:]
    _, core = position()
    factor = rows_in_all / (counts[0][0:1, 0:1] + counts[1][0:1, 0:1])
    factor_ref[...] = jnp.broadcast_to(factor, factor_ref.shape)
    for ref, side in ((keep_ref, core), (other_ref, 1 - core)):
        columns = pl.ds(pl.multiple_of(side * HALF, HALF), HALF)
        dk_ref[:, columns] = (ref[:, :HALF].astype(F32) * factor).astype(BF16)
        dv_ref[:, columns] = (ref[:, HALF:].astype(F32) * factor).astype(BF16)


def query_end_kernel(factor_ref, *refs):
    parts, (send_ref, keep_ref) = refs[:-2], refs[-2:]
    _, core = position()
    summed = (factor_ref[0:1, 0:1] * ROOT) * sum(part[...].astype(F32) for part in parts)
    half = summed.shape[0] // 2
    low, high = summed[:half], summed[half:]
    send_ref[...] = jnp.where(core == 0, high, low).astype(BF16)
    keep_ref[...] = jnp.where(core == 0, low, high).astype(BF16)


def in_order(own, other, core, axis):
    return jnp.where(
        core == 0, jnp.concatenate([own, other], axis), jnp.concatenate([other, own], axis)
    )


def local(queries, keys, values, attn_out, out_grad, loss_mask, input_lengths, target_lengths):
    query_rows, key_rows, value_rows = queries[0], keys[0], values[0]
    dec_local, enc_local = query_rows.shape[0], key_rows.shape[0]
    chips = lax.axis_size("seq") // 2
    data_groups = lax.axis_size("dp")
    _, core = position()
    dec_rows = 2 * chips * dec_local
    enc_rows = 2 * enc_local
    block = (2 * dec_local, HALF)
    lengths = (input_lengths[0], target_lengths[0])

    def shaped(*shape, dtype=BF16):
        return jax.ShapeDtypeStruct(shape, dtype)

    def gather(block):
        blocks = [block]
        apart = chips // 2
        while apart > 1:
            blocks += [across(one, apart) for one in blocks]
            apart //= 2
        return blocks, across(after(block, g_recv)[0], 1)

    def forwarded(blocks):
        return [across(one, 1) for one in blocks[1:]]

    offsets = [0]
    apart = chips // 2
    while apart:
        offsets += [offset ^ apart for offset in offsets]
        apart //= 2

    features = HEADS * HEAD_SIZE
    sent = shaped(dec_local, HALF + EXTRA)
    block = shaped(2 * dec_local, HALF)

    with jax.named_scope("sibling_exchange"):
        q_recv = to_sibling(query_rows)
        g_send, g_keep = kernel_call(
            prepare_kernel,
            (sent, sent),
            [ANY] * 3,
            (VMEM, VMEM),
            [
                pltpu.VMEM((dec_local, features), BF16),
                pltpu.VMEM((dec_local, features), BF16),
                pltpu.VMEM((1, dec_local), jnp.int32),
                pltpu.SemaphoreType.DMA((3,)),
            ],
            10**5,
            10**6,
            "prepare",
            60 * 1024 * 1024,
        )(out_grad[0], attn_out[0], loss_mask)
        g_recv = to_sibling(g_send)

    with jax.named_scope("query_gather"):
        q_recv, _ = after(q_recv, g_keep)
        q_block = kernel_call(
            join_queries_kernel, block, [VMEM, VMEM], VMEM, [], 10**5, 10**5, "join_queries"
        )(query_rows, q_recv)
        q_far, q_near = gather(q_block)

    with jax.named_scope("setup"):
        half_rows = shaped(enc_local, HALF)
        bias = shaped(enc_local, dec_rows, dtype=F32)
        k_own, k_send, bias_own, bias_other = kernel_call(
            functools.partial(setup_kernel, offsets),
            (half_rows, half_rows, bias, bias),
            [SMEM] * 2 + [VMEM],
            (VMEM,) * 4,
            [],
            10**6,
            2**22,
            "setup",
        )(*lengths, after(key_rows, q_block)[0])

    with jax.named_scope("cotangent_gather"):
        small = shaped(8, 2 * dec_local, dtype=F32)
        g_block, delta, count = kernel_call(
            join_cotangents_kernel,
            (block, small, shaped(8, EXTRA, dtype=F32)),
            [VMEM, VMEM],
            (VMEM,) * 3,
            [],
            10**5,
            10**5,
            "join_cotangents",
        )(g_keep, g_recv)

    def over_groups(count, apart):
        return lax.ppermute(count, "dp", [(i, i ^ apart) for i in range(data_groups)])

    with jax.named_scope("mask_count"):
        apart = 1
        while apart < data_groups // 2:
            count = count + after(over_groups(count, apart), bias_own)[0]
            apart *= 2
        rows_in_all = float(data_groups * dec_rows)

    with jax.named_scope("query_forward"):
        q_far = [q_far[0], *(after(one, bias_own, count)[0] for one in q_far[1:])]
        q_blocks = [*q_far, q_near, *forwarded(q_far)]

    with jax.named_scope("cotangent_gather"):
        sent = after(g_block, *q_far)[0]
        g_blocks = [g_block] + [across(sent, offset) for offset in offsets[1:]]

    with jax.named_scope("key_exchange"):
        v_recv = to_sibling(value_rows)
        k_send, v_recv, *_ = after(k_send, v_recv, *q_far)
        k_recv = to_sibling(k_send)

    with jax.named_scope("scores"):
        width = (dec_rows // 128 + 1) * 128
        stats = kernel_call(
            functools.partial(scores_kernel, offsets),
            shaped(2 * HALF_HEADS, width, dtype=F32),
            [VMEM] * (chips + 6),
            VMEM,
            [],
            2 * dec_rows * enc_rows * HALF,
            2 * (dec_rows + enc_rows) * HALF,
            "scores",
        )(delta, bias_own, bias_other, k_own, k_recv, count, *q_blocks)

    with jax.named_scope("stats_exchange"):
        all_stats = [stats] + [across(stats, offset) for offset in offsets[1:]]

    with jax.named_scope("grads"):
        both = shaped(enc_local, 2 * HALF)
        *dq_blocks, dkv_keep, dkv_send, count = kernel_call(
            functools.partial(grads_kernel, offsets),
            (block,) * chips + (both, both, shaped(8, EXTRA, dtype=F32)),
            [VMEM] * (3 * chips + 6),
            (VMEM,) * (chips + 3),
            [],
            10 * dec_rows * enc_rows * HALF,
            4 * (dec_rows + 2 * enc_rows) * HALF,
            "grads",
        )(bias_own, bias_other, *all_stats, *q_blocks, *g_blocks, k_own, k_recv, value_rows, v_recv)

    with jax.named_scope("query_grad_sum"):
        parts = [dq_blocks[0]]
        for j in sorted(range(1, chips), key=lambda j: -offsets[j]):
            parts.append(across(dq_blocks[j], offsets[j]))

    with jax.named_scope("key_grad_end"):
        dkv_recv = to_sibling(dkv_send)
        counts = (count, over_groups(count, data_groups // 2))
        whole = shaped(enc_local, features)
        grad_keys, grad_values, factor = kernel_call(
            functools.partial(key_end_kernel, rows_in_all),
            (whole, whole, shaped(8, EXTRA, dtype=F32)),
            [VMEM] * 4,
            (VMEM, VMEM, VMEM),
            [],
            10**6,
            2**22,
            "key_end",
        )(dkv_keep, dkv_recv, *counts)

    with jax.named_scope("query_grad_end"):
        half = shaped(dec_local, HALF)
        dq_send, dq_keep = kernel_call(
            query_end_kernel,
            (half, half),
            [VMEM] * (chips + 1),
            (VMEM, VMEM),
            [],
            10**5,
            10**6,
            "query_end",
        )(factor, *parts)
        grad_queries = in_order(dq_keep, to_sibling(dq_send), core, 1)

    return grad_queries[None], grad_keys[None], grad_values[None]


def solution(mesh):
    return jax.shard_map(
        local,
        mesh=mesh,
        in_specs=(
            P("dp", "seq", None),
            P("dp", "seq", None),
            P("dp", "seq", None),
            P("dp", "seq", None),
            P("dp", "seq", None),
            P("dp", "seq"),
            P("dp", None, None),
            P("dp", None, None),
        ),
        out_specs=(P("dp", "seq", None), P("dp", "seq", None), P("dp", "seq", None)),
        check_vma=False,
    )
```

```python
import functools
import jax
import jax.numpy as jnp
from jax import lax
from jax.experimental import pallas as pl
from jax.experimental.pallas import tpu as pltpu
from jax.sharding import PartitionSpec as P

HEADS = 8
HEAD_SIZE = 256
HALF_HEADS = HEADS // 2
HALF = HALF_HEADS * HEAD_SIZE
EXTRA = 128
ROOT = HEAD_SIZE**-0.5
NEVER = -1e30
VMEM_LIMIT = 24 * 1024 * 1024
F32 = jnp.float32
BF16 = jnp.bfloat16
ANY = pl.BlockSpec(memory_space=pl.ANY)
VMEM = pl.BlockSpec(memory_space=pltpu.VMEM)
SMEM = pl.BlockSpec(memory_space=pltpu.SMEM)
NT = (((1,), (1,)), ((), ()))
TN = (((0,), (0,)), ((), ()))
NN = (((1,), (0,)), ((), ()))


def dot(a, b, dims):
    return lax.dot_general(a, b, dims, preferred_element_type=F32)


def position():
    me = lax.axis_index("seq")
    return me >> 1, me & 1


def to_sibling(block):
    count = lax.axis_size("seq")
    return lax.ppermute(block, "seq", [(i, i ^ 1) for i in range(count)])


def across(block, apart):
    count = lax.axis_size("seq")
    return lax.ppermute(block, "seq", [(i, i ^ (2 * apart)) for i in range(count)])


def after(block, *others):
    return lax.optimization_barrier((block, *others))


def kernel_call(
    body, out_shape, in_specs, out_specs, scratch, flops, moved, name, vmem_limit=VMEM_LIMIT
):
    return pl.pallas_call(
        body,
        out_shape=out_shape,
        in_specs=in_specs,
        out_specs=out_specs,
        scratch_shapes=scratch,
        compiler_params=pltpu.CompilerParams(vmem_limit_bytes=vmem_limit),
        cost_estimate=pl.CostEstimate(flops=flops, bytes_accessed=moved, transcendentals=0),
        name=name,
    )


def prepare_kernel(
    grad_ref, out_ref, mask_ref, send_ref, keep_ref, grad_held, out_held, mask_held, sems
):
    _, core = position()
    rows = grad_ref.shape[0]
    copies = start_all(
        [(mask_ref, mask_held), (grad_ref, grad_held), (out_ref, out_held)], sems
    )
    copies[0].wait()
    mask_row = mask_held[...].astype(F32)
    here = lax.broadcasted_iota(jnp.int32, (rows, rows), 0) == lax.broadcasted_iota(
        jnp.int32, (rows, rows), 1
    )
    mask = jnp.sum(jnp.where(here, mask_row, 0.0), axis=1, keepdims=True)
    lane = lax.broadcasted_iota(jnp.int32, (rows, EXTRA), 1)
    for copy in copies[1:]:
        copy.wait()
    masked = grad_held[...].astype(F32) * mask
    products = masked * out_held[...].astype(F32)
    grad_held[...] = masked.astype(BF16)
    halves = []
    for half in range(2):
        extra = jnp.where(lane == HALF_HEADS, mask, 0.0)
        for head in range(HALF_HEADS):
            first = half * HALF + head * HEAD_SIZE
            delta = jnp.sum(products[:, first : first + HEAD_SIZE], axis=1, keepdims=True)
            extra = jnp.where(lane == head, delta, extra)
        halves.append(extra)
    for ref, half in ((send_ref, 1 - core), (keep_ref, core)):
        ref[:, :HALF] = grad_held[:, pl.ds(pl.multiple_of(half * HALF, HALF), HALF)]
        ref[:, HALF:] = jnp.where(half == 0, halves[0], halves[1]).astype(BF16)


def in_core_order(own, other, core):
    own, other = own.astype(F32), other.astype(F32)
    joined = jnp.where(
        core == 0, jnp.concatenate([own, other], 0), jnp.concatenate([other, own], 0)
    )
    return joined.astype(BF16)


def join_queries_kernel(own_ref, other_ref, joined_ref):
    _, core = position()
    mine = pl.ds(pl.multiple_of(core * HALF, HALF), HALF)
    joined_ref[...] = in_core_order(own_ref[:, mine], other_ref[:, mine], core)


def join_cotangents_kernel(own_ref, other_ref, joined_ref, delta_ref, count_ref):
    _, core = position()
    joined_ref[...] = in_core_order(own_ref[:, :HALF], other_ref[:, :HALF], core)
    extra = jnp.transpose(in_core_order(own_ref[:, HALF:], other_ref[:, HALF:], core).astype(F32))
    delta_ref[...] = extra[: delta_ref.shape[0]]
    count = jnp.sum(extra[HALF_HEADS : HALF_HEADS + 1], axis=1, keepdims=True)
    count_ref[...] = jnp.broadcast_to(count, count_ref.shape)


def split_kernel(rows_ref, own_ref, send_ref):
    _, core = position()
    for ref, half in ((own_ref, core), (send_ref, 1 - core)):
        ref[...] = rows_ref[:, pl.ds(pl.multiple_of(half * HALF, HALF), HALF)]


def document_of(positions, lengths_ref):
    end = 0
    document = jnp.zeros_like(positions)
    for i in range(lengths_ref.shape[1]):
        end = end + lengths_ref[0, i]
        document += (positions >= end).astype(jnp.int32)
    return document


def setup_kernel(offsets, in_ref, target_ref, key_ref, k_ref, send_ref, bias_own, bias_other):
    chip, core = position()
    split_kernel(key_ref, k_ref, send_ref)
    enc_rows, dec_rows = bias_own.shape
    block = dec_rows // len(offsets)
    lane = lax.broadcasted_iota(jnp.int32, (1, dec_rows), 1)
    dec = lane + chip * block
    for j, offset in enumerate(offsets[1:], 1):
        dec = jnp.where(lane >= j * block, lane + ((chip ^ offset) - j) * block, dec)
    dec = document_of(dec, target_ref)
    for ref, side in ((bias_own, core), (bias_other, 1 - core)):
        enc = lax.broadcasted_iota(jnp.int32, (enc_rows, 1), 0) + (2 * chip + side) * enc_rows
        ref[...] = jnp.where(document_of(enc, in_ref) == dec, 0.0, NEVER)


def start_all(pairs, sems):
    copies = [pltpu.make_async_copy(a, b, sems.at[i]) for i, (a, b) in enumerate(pairs)]
    for copy in copies:
        copy.start()
    return copies


def rows_of(blocks, head):
    columns = slice(head * HEAD_SIZE, (head + 1) * HEAD_SIZE)
    return jnp.concatenate([block[:, columns] for block in blocks], 0)


def value_columns_of(head):
    _, core = position()
    first = core * HALF + head * HEAD_SIZE
    return pl.ds(pl.multiple_of(first, HEAD_SIZE), HEAD_SIZE)


def columns_of(head):
    return slice(head * HEAD_SIZE, (head + 1) * HEAD_SIZE)


def scores_kernel(offsets, delta_ref, bias_own, bias_other, key_ref, other_ref, *refs):
    count_ref, refs = refs[0], refs[1:]
    blocks, (stats_ref,) = refs[: len(offsets)], refs[len(offsets) :]
    rows = blocks[0].shape[0]
    dec_rows = rows * len(offsets)
    stats_ref[...] = jnp.broadcast_to(count_ref[0:1, 0:1], stats_ref.shape)
    stats_ref[HALF_HEADS:, :rows] = delta_ref[:HALF_HEADS]
    for head in range(HALF_HEADS):
        q = rows_of(blocks, head)
        scores = [
            dot(k[:, columns_of(head)], q, NT) * ROOT + bias[...]
            for k, bias in ((key_ref, bias_own), (other_ref, bias_other))
        ]
        top = functools.reduce(jnp.maximum, [jnp.max(s, axis=0, keepdims=True) for s in scores])
        top = jnp.maximum(top, -1e20)
        total = sum(jnp.sum(jnp.exp(s - top), axis=0, keepdims=True) for s in scores)
        stats_ref[head : head + 1, :dec_rows] = jnp.where(
            total > 0, top + jnp.log(jnp.maximum(total, 1e-30)), NEVER
        )


def gathered_stats(offsets, stats, rows):
    logs = []
    for sender, ref in zip(offsets, stats):
        order = [offsets.index(offset ^ sender) for offset in offsets]
        logs.append(
            jnp.concatenate([ref[:HALF_HEADS, j * rows : (j + 1) * rows] for j in order], 1)
        )
    top = functools.reduce(jnp.maximum, logs)
    log_total = top + jnp.log(sum(jnp.exp(log - top) for log in logs))
    delta = jnp.concatenate([ref[HALF_HEADS:, :rows] for ref in stats], 1)
    last = stats[0].shape[1] - 1
    return log_total, delta, sum(ref[0:1, last:] for ref in stats)


def grads_kernel(offsets, bias_own, bias_other, *refs):
    chips = len(offsets)
    order = [0, *sorted(offsets[1:], reverse=True)]
    stats, refs = [refs[order.index(offset)] for offset in offsets], refs[chips:]
    q_blocks, refs = refs[:chips], refs[chips:]
    g_blocks, refs = refs[:chips], refs[chips:]
    (key_ref, key_other, value_ref, value_other), refs = refs[:4], refs[4:]
    dq_blocks, (keep_ref, send_ref, count_ref) = refs[:chips], refs[chips:]
    rows = q_blocks[0].shape[0]
    log_total, delta, count = gathered_stats(offsets, stats, rows)
    count_ref[...] = jnp.broadcast_to(count, count_ref.shape)
    for head in range(HALF_HEADS):
        columns = slice(head * HEAD_SIZE, (head + 1) * HEAD_SIZE)
        value_columns = slice(HALF + columns.start, HALF + columns.stop)
        line = slice(head, head + 1)
        q, g = rows_of(q_blocks, head), rows_of(g_blocks, head)
        dq = 0.0
        for key, value, bias, out_ref in (
            (key_ref, value_ref, bias_own, keep_ref),
            (key_other, value_other, bias_other, send_ref),
        ):
            k, v = key[:, columns], value[:, value_columns_of(head)]
            probs = jnp.exp(dot(k, q, NT) * ROOT + bias[...] - log_total[line])
            dscore = (probs * (dot(v, g, NT) - delta[line])).astype(BF16)
            dq += dot(dscore, k, TN)
            out_ref[:, columns] = (dot(dscore, q, NN) * ROOT).astype(BF16)
            out_ref[:, value_columns] = dot(probs.astype(BF16), g, NN).astype(BF16)
        dq = (dq * ROOT).astype(BF16)
        for j, block in enumerate(dq_blocks):
            block[:, columns] = dq[j * rows : (j + 1) * rows]


def key_end_kernel(rows_in_all, keep_ref, other_ref, *refs):
    counts, (dk_ref, dv_ref, factor_ref) = refs[:2], refs[2:]
    _, core = position()
    factor = rows_in_all / (counts[0][0:1, 0:1] + counts[1][0:1, 0:1])
    factor_ref[...] = jnp.broadcast_to(factor, factor_ref.shape)
    for ref, side in ((keep_ref, core), (other_ref, 1 - core)):
        columns = pl.ds(pl.multiple_of(side * HALF, HALF), HALF)
        dk_ref[:, columns] = (ref[:, :HALF].astype(F32) * factor).astype(BF16)
        dv_ref[:, columns] = (ref[:, HALF:].astype(F32) * factor).astype(BF16)


def query_end_kernel(factor_ref, *refs):
    parts, (send_ref, keep_ref) = refs[:-2], refs[-2:]
    _, core = position()
    summed = factor_ref[0:1, 0:1] * sum(part[...].astype(F32) for part in parts)
    half = summed.shape[0] // 2
    low, high = summed[:half], summed[half:]
    send_ref[...] = jnp.where(core == 0, high, low).astype(BF16)
    keep_ref[...] = jnp.where(core == 0, low, high).astype(BF16)


def in_order(own, other, core, axis):
    return jnp.where(
        core == 0, jnp.concatenate([own, other], axis), jnp.concatenate([other, own], axis)
    )


def local(queries, keys, values, attn_out, out_grad, loss_mask, input_lengths, target_lengths):
    query_rows, key_rows, value_rows = queries[0], keys[0], values[0]
    dec_local, enc_local = query_rows.shape[0], key_rows.shape[0]
    chips = lax.axis_size("seq") // 2
    data_groups = lax.axis_size("dp")
    _, core = position()
    dec_rows = 2 * chips * dec_local
    enc_rows = 2 * enc_local
    block = (2 * dec_local, HALF)
    lengths = (input_lengths[0], target_lengths[0])

    def shaped(*shape, dtype=BF16):
        return jax.ShapeDtypeStruct(shape, dtype)

    def gather(block):
        blocks = [block]
        apart = chips // 2
        while apart > 1:
            blocks += [across(one, apart) for one in blocks]
            apart //= 2
        return blocks, across(block, 1)

    def forwarded(blocks):
        return [across(one, 1) for one in blocks[1:]]

    offsets = [0]
    apart = chips // 2
    while apart:
        offsets += [offset ^ apart for offset in offsets]
        apart //= 2

    features = HEADS * HEAD_SIZE
    sent = shaped(dec_local, HALF + EXTRA)
    block = shaped(2 * dec_local, HALF)

    with jax.named_scope("sibling_exchange"):
        q_recv = to_sibling(query_rows)
        g_send, g_keep = kernel_call(
            prepare_kernel,
            (sent, sent),
            [ANY] * 3,
            (VMEM, VMEM),
            [
                pltpu.VMEM((dec_local, features), BF16),
                pltpu.VMEM((dec_local, features), BF16),
                pltpu.VMEM((1, dec_local), jnp.int32),
                pltpu.SemaphoreType.DMA((3,)),
            ],
            10**5,
            10**6,
            "prepare",
            60 * 1024 * 1024,
        )(out_grad[0], attn_out[0], loss_mask)
        g_recv = to_sibling(g_send)

    with jax.named_scope("query_gather"):
        q_recv, _ = after(q_recv, g_keep)
        q_block = kernel_call(
            join_queries_kernel, block, [VMEM, VMEM], VMEM, [], 10**5, 10**5, "join_queries"
        )(query_rows, q_recv)
        q_far, q_near = gather(q_block)

    with jax.named_scope("setup"):
        half_rows = shaped(enc_local, HALF)
        bias = shaped(enc_local, dec_rows, dtype=F32)
        k_own, k_send, bias_own, bias_other = kernel_call(
            functools.partial(setup_kernel, offsets),
            (half_rows, half_rows, bias, bias),
            [SMEM] * 2 + [VMEM],
            (VMEM,) * 4,
            [],
            10**6,
            2**22,
            "setup",
        )(*lengths, after(key_rows, q_block)[0])

    with jax.named_scope("cotangent_gather"):
        small = shaped(8, 2 * dec_local, dtype=F32)
        g_block, delta, count = kernel_call(
            join_cotangents_kernel,
            (block, small, shaped(8, EXTRA, dtype=F32)),
            [VMEM, VMEM],
            (VMEM,) * 3,
            [],
            10**5,
            10**5,
            "join_cotangents",
        )(g_keep, g_recv)

    def over_groups(count, apart):
        return lax.ppermute(count, "dp", [(i, i ^ apart) for i in range(data_groups)])

    with jax.named_scope("mask_count"):
        apart = 1
        while apart < data_groups // 2:
            count = count + after(over_groups(count, apart), bias_own)[0]
            apart *= 2
        rows_in_all = float(data_groups * dec_rows)

    with jax.named_scope("query_forward"):
        q_far = [q_far[0], *(after(one, bias_own, count, q_near)[0] for one in q_far[1:])]
        q_blocks = [*q_far, q_near, *forwarded(q_far)]

    with jax.named_scope("cotangent_gather"):
        sent = after(g_block, *q_far, q_near)[0]
        g_blocks = [g_block] + [across(sent, offset) for offset in offsets[1:]]

    with jax.named_scope("key_exchange"):
        v_recv = to_sibling(value_rows)
        k_send, v_recv, *_ = after(k_send, v_recv, *q_far, q_near)
        k_recv = to_sibling(k_send)

    with jax.named_scope("scores"):
        width = (dec_rows // 128 + 1) * 128
        stats = kernel_call(
            functools.partial(scores_kernel, offsets),
            shaped(2 * HALF_HEADS, width, dtype=F32),
            [VMEM] * (chips + 6),
            VMEM,
            [],
            2 * dec_rows * enc_rows * HALF,
            2 * (dec_rows + enc_rows) * HALF,
            "scores",
        )(delta, bias_own, bias_other, k_own, k_recv, count, *q_blocks)

    with jax.named_scope("stats_exchange"):
        order = [0, *sorted(offsets[1:], reverse=True)]
        all_stats = [stats] + [across(stats, offset) for offset in order[1:]]

    with jax.named_scope("grads"):
        both = shaped(enc_local, 2 * HALF)
        *dq_blocks, dkv_keep, dkv_send, count = kernel_call(
            functools.partial(grads_kernel, offsets),
            (block,) * chips + (both, both, shaped(8, EXTRA, dtype=F32)),
            [VMEM] * (3 * chips + 6),
            (VMEM,) * (chips + 3),
            [],
            10 * dec_rows * enc_rows * HALF,
            4 * (dec_rows + 2 * enc_rows) * HALF,
            "grads",
        )(bias_own, bias_other, *all_stats, *q_blocks, *g_blocks, k_own, k_recv, value_rows, v_recv)

    with jax.named_scope("query_grad_sum"):
        parts = [dq_blocks[0]]
        for j in sorted(range(1, chips), key=lambda j: -offsets[j]):
            parts.append(across(dq_blocks[j], offsets[j]))

    with jax.named_scope("key_grad_end"):
        dkv_recv = to_sibling(dkv_send)
        counts = (count, over_groups(count, data_groups // 2))
        whole = shaped(enc_local, features)
        grad_keys, grad_values, factor = kernel_call(
            functools.partial(key_end_kernel, rows_in_all),
            (whole, whole, shaped(8, EXTRA, dtype=F32)),
            [VMEM] * 4,
            (VMEM, VMEM, VMEM),
            [],
            10**6,
            2**22,
            "key_end",
        )(dkv_keep, dkv_recv, *counts)

    with jax.named_scope("query_grad_end"):
        half = shaped(dec_local, HALF)
        dq_send, dq_keep = kernel_call(
            query_end_kernel,
            (half, half),
            [VMEM] * (chips + 1),
            (VMEM, VMEM),
            [],
            10**5,
            10**6,
            "query_end",
        )(factor, *parts)
        grad_queries = in_order(dq_keep, to_sibling(dq_send), core, 1)

    return grad_queries[None], grad_keys[None], grad_values[None]


def solution(mesh):
    return jax.shard_map(
        local,
        mesh=mesh,
        in_specs=(
            P("dp", "seq", None),
            P("dp", "seq", None),
            P("dp", "seq", None),
            P("dp", "seq", None),
            P("dp", "seq", None),
            P("dp", "seq"),
            P("dp", None, None),
            P("dp", None, None),
        ),
        out_specs=(P("dp", "seq", None), P("dp", "seq", None), P("dp", "seq", None)),
        check_vma=False,
    )
```

```python
import functools
import jax
import jax.numpy as jnp
from jax import lax
from jax.experimental import pallas as pl
from jax.experimental.pallas import tpu as pltpu
from jax.sharding import PartitionSpec as P

HEADS = 8
HEAD_SIZE = 256
HALF_HEADS = HEADS // 2
HALF = HALF_HEADS * HEAD_SIZE
EXTRA = 128
ROOT = HEAD_SIZE**-0.5
NEVER = -1e30
VMEM_LIMIT = 24 * 1024 * 1024
F32 = jnp.float32
BF16 = jnp.bfloat16
ANY = pl.BlockSpec(memory_space=pl.ANY)
VMEM = pl.BlockSpec(memory_space=pltpu.VMEM)
SMEM = pl.BlockSpec(memory_space=pltpu.SMEM)
NT = (((1,), (1,)), ((), ()))
TN = (((0,), (0,)), ((), ()))
NN = (((1,), (0,)), ((), ()))


def dot(a, b, dims):
    return lax.dot_general(a, b, dims, preferred_element_type=F32)


def position():
    me = lax.axis_index("seq")
    return me >> 1, me & 1


def to_sibling(block):
    count = lax.axis_size("seq")
    return lax.ppermute(block, "seq", [(i, i ^ 1) for i in range(count)])


def across(block, apart):
    count = lax.axis_size("seq")
    return lax.ppermute(block, "seq", [(i, i ^ (2 * apart)) for i in range(count)])


def after(block, *others):
    return lax.optimization_barrier((block, *others))


def kernel_call(
    body, out_shape, in_specs, out_specs, scratch, flops, moved, name, vmem_limit=VMEM_LIMIT
):
    return pl.pallas_call(
        body,
        out_shape=out_shape,
        in_specs=in_specs,
        out_specs=out_specs,
        scratch_shapes=scratch,
        compiler_params=pltpu.CompilerParams(vmem_limit_bytes=vmem_limit),
        cost_estimate=pl.CostEstimate(flops=flops, bytes_accessed=moved, transcendentals=0),
        name=name,
    )


def document_of(positions, lengths_ref):
    end = 0
    document = jnp.zeros_like(positions)
    for i in range(lengths_ref.shape[1]):
        end = end + lengths_ref[0, i]
        document += (positions >= end).astype(jnp.int32)
    return document


def prepare_kernel(
    offsets,
    dec_rows,
    enc_rows,
    in_ref,
    target_ref,
    grad_ref,
    out_ref,
    mask_ref,
    send_ref,
    keep_ref,
    docs_ref,
    grad_held, out_held, mask_held, sems
):
    chip, core = position()
    rows = grad_ref.shape[0]
    copies = start_all(
        [(mask_ref, mask_held), (grad_ref, grad_held), (out_ref, out_held)], sems
    )
    lane = lax.broadcasted_iota(jnp.int32, (1, docs_ref.shape[1]), 1)
    block = dec_rows // len(offsets)
    dec = lane + chip * block
    for j, offset in enumerate(offsets[1:], 1):
        dec = jnp.where(lane >= j * block, lane + ((chip ^ offset) - j) * block, dec)
    docs = [document_of(dec, target_ref)]
    for side in (core, 1 - core):
        docs.append(document_of(lane + (2 * chip + side) * enc_rows, in_ref))
    docs_ref[...] = jnp.concatenate(docs + docs + docs[:2], 0).astype(F32)
    copies[0].wait()
    mask_row = mask_held[...].astype(F32)
    here = lax.broadcasted_iota(jnp.int32, (rows, rows), 0) == lax.broadcasted_iota(
        jnp.int32, (rows, rows), 1
    )
    mask = jnp.sum(jnp.where(here, mask_row, 0.0), axis=1, keepdims=True)
    lane = lax.broadcasted_iota(jnp.int32, (rows, EXTRA), 1)
    for copy in copies[1:]:
        copy.wait()
    masked = grad_held[...].astype(F32) * mask
    products = masked * out_held[...].astype(F32)
    grad_held[...] = masked.astype(BF16)
    halves = []
    for half in range(2):
        extra = jnp.where(lane == HALF_HEADS, mask, 0.0)
        for head in range(HALF_HEADS):
            first = half * HALF + head * HEAD_SIZE
            delta = jnp.sum(products[:, first : first + HEAD_SIZE], axis=1, keepdims=True)
            extra = jnp.where(lane == head, delta, extra)
        halves.append(extra)
    for ref, half in ((send_ref, 1 - core), (keep_ref, core)):
        ref[:, :HALF] = grad_held[:, pl.ds(pl.multiple_of(half * HALF, HALF), HALF)]
        ref[:, HALF:] = jnp.where(half == 0, halves[0], halves[1]).astype(BF16)


def in_core_order(own, other, core):
    own, other = own.astype(F32), other.astype(F32)
    joined = jnp.where(
        core == 0, jnp.concatenate([own, other], 0), jnp.concatenate([other, own], 0)
    )
    return joined.astype(BF16)


def join_queries_kernel(own_ref, other_ref, joined_ref):
    _, core = position()
    mine = pl.ds(pl.multiple_of(core * HALF, HALF), HALF)
    joined_ref[...] = in_core_order(own_ref[:, mine], other_ref[:, mine], core)


def join_cotangents_kernel(own_ref, other_ref, joined_ref, delta_ref, count_ref):
    _, core = position()
    joined_ref[...] = in_core_order(own_ref[:, :HALF], other_ref[:, :HALF], core)
    extra = jnp.transpose(in_core_order(own_ref[:, HALF:], other_ref[:, HALF:], core).astype(F32))
    delta_ref[...] = extra[: delta_ref.shape[0]]
    count = jnp.sum(extra[HALF_HEADS : HALF_HEADS + 1], axis=1, keepdims=True)
    count_ref[...] = jnp.broadcast_to(count, count_ref.shape)


def split_kernel(rows_ref, own_ref, send_ref):
    _, core = position()
    for ref, half in ((own_ref, core), (send_ref, 1 - core)):
        ref[...] = rows_ref[:, pl.ds(pl.multiple_of(half * HALF, HALF), HALF)]


def setup_kernel(docs_ref, key_ref, k_ref, send_ref, bias_own, bias_other):
    split_kernel(key_ref, k_ref, send_ref)
    enc_rows, dec_rows = bias_own.shape
    dec = docs_ref[0:1, :dec_rows]
    columns = jnp.transpose(docs_ref[:, :enc_rows])
    for ref, column in ((bias_own, 1), (bias_other, 2)):
        ref[...] = jnp.where(columns[:, column : column + 1] == dec, 0.0, NEVER)


def start_all(pairs, sems):
    copies = [pltpu.make_async_copy(a, b, sems.at[i]) for i, (a, b) in enumerate(pairs)]
    for copy in copies:
        copy.start()
    return copies


def rows_of(blocks, head):
    columns = slice(head * HEAD_SIZE, (head + 1) * HEAD_SIZE)
    return jnp.concatenate([block[:, columns] for block in blocks], 0)


def value_columns_of(head):
    _, core = position()
    first = core * HALF + head * HEAD_SIZE
    return pl.ds(pl.multiple_of(first, HEAD_SIZE), HEAD_SIZE)


def columns_of(head):
    return slice(head * HEAD_SIZE, (head + 1) * HEAD_SIZE)


def scores_kernel(offsets, delta_ref, bias_own, bias_other, key_ref, other_ref, *refs):
    count_ref, refs = refs[0], refs[1:]
    blocks, (stats_ref,) = refs[: len(offsets)], refs[len(offsets) :]
    rows = blocks[0].shape[0]
    dec_rows = rows * len(offsets)
    stats_ref[...] = jnp.broadcast_to(count_ref[0:1, 0:1], stats_ref.shape)
    stats_ref[HALF_HEADS:, :rows] = delta_ref[:HALF_HEADS]
    for head in range(HALF_HEADS):
        q = rows_of(blocks, head)
        scores = [
            dot(k[:, columns_of(head)], q, NT) * ROOT + bias[...]
            for k, bias in ((key_ref, bias_own), (other_ref, bias_other))
        ]
        top = functools.reduce(jnp.maximum, [jnp.max(s, axis=0, keepdims=True) for s in scores])
        top = jnp.maximum(top, -1e20)
        total = sum(jnp.sum(jnp.exp(s - top), axis=0, keepdims=True) for s in scores)
        stats_ref[head : head + 1, :dec_rows] = jnp.where(
            total > 0, top + jnp.log(jnp.maximum(total, 1e-30)), NEVER
        )


def gathered_stats(offsets, stats, rows):
    logs = []
    for sender, ref in zip(offsets, stats):
        order = [offsets.index(offset ^ sender) for offset in offsets]
        logs.append(
            jnp.concatenate([ref[:HALF_HEADS, j * rows : (j + 1) * rows] for j in order], 1)
        )
    top = functools.reduce(jnp.maximum, logs)
    log_total = top + jnp.log(sum(jnp.exp(log - top) for log in logs))
    delta = jnp.concatenate([ref[HALF_HEADS:, :rows] for ref in stats], 1)
    last = stats[0].shape[1] - 1
    return log_total, delta, sum(ref[0:1, last:] for ref in stats)


def grads_kernel(offsets, bias_own, bias_other, *refs):
    chips = len(offsets)
    order = [0, *sorted(offsets[1:], reverse=True)]
    stats, refs = [refs[order.index(offset)] for offset in offsets], refs[chips:]
    q_blocks, refs = refs[:chips], refs[chips:]
    g_blocks, refs = refs[:chips], refs[chips:]
    (key_ref, key_other, value_ref, value_other), refs = refs[:4], refs[4:]
    dq_blocks, (keep_ref, send_ref, count_ref) = refs[:chips], refs[chips:]
    rows = q_blocks[0].shape[0]
    log_total, delta, count = gathered_stats(offsets, stats, rows)
    count_ref[...] = jnp.broadcast_to(count, count_ref.shape)
    for head in range(HALF_HEADS):
        columns = slice(head * HEAD_SIZE, (head + 1) * HEAD_SIZE)
        value_columns = slice(HALF + columns.start, HALF + columns.stop)
        line = slice(head, head + 1)
        q, g = rows_of(q_blocks, head), rows_of(g_blocks, head)
        dq = 0.0
        for key, value, bias, out_ref in (
            (key_ref, value_ref, bias_own, keep_ref),
            (key_other, value_other, bias_other, send_ref),
        ):
            k, v = key[:, columns], value[:, value_columns_of(head)]
            probs = jnp.exp(dot(k, q, NT) * ROOT + bias[...] - log_total[line])
            dscore = (probs * (dot(v, g, NT) - delta[line])).astype(BF16)
            dq += dot(dscore, k, TN)
            out_ref[:, columns] = (dot(dscore, q, NN) * ROOT).astype(BF16)
            out_ref[:, value_columns] = dot(probs.astype(BF16), g, NN).astype(BF16)
        dq = (dq * ROOT).astype(BF16)
        for j, block in enumerate(dq_blocks):
            block[:, columns] = dq[j * rows : (j + 1) * rows]


def key_end_kernel(rows_in_all, keep_ref, other_ref, *refs):
    counts, (dk_ref, dv_ref, factor_ref) = refs[:2], refs[2:]
    _, core = position()
    factor = rows_in_all / (counts[0][0:1, 0:1] + counts[1][0:1, 0:1])
    factor_ref[...] = jnp.broadcast_to(factor, factor_ref.shape)
    for ref, side in ((keep_ref, core), (other_ref, 1 - core)):
        columns = pl.ds(pl.multiple_of(side * HALF, HALF), HALF)
        dk_ref[:, columns] = (ref[:, :HALF].astype(F32) * factor).astype(BF16)
        dv_ref[:, columns] = (ref[:, HALF:].astype(F32) * factor).astype(BF16)


def query_end_kernel(factor_ref, *refs):
    parts, (send_ref, keep_ref) = refs[:-2], refs[-2:]
    _, core = position()
    summed = factor_ref[0:1, 0:1] * sum(part[...].astype(F32) for part in parts)
    half = summed.shape[0] // 2
    low, high = summed[:half], summed[half:]
    send_ref[...] = jnp.where(core == 0, high, low).astype(BF16)
    keep_ref[...] = jnp.where(core == 0, low, high).astype(BF16)


def in_order(own, other, core, axis):
    return jnp.where(
        core == 0, jnp.concatenate([own, other], axis), jnp.concatenate([other, own], axis)
    )


def local(queries, keys, values, attn_out, out_grad, loss_mask, input_lengths, target_lengths):
    query_rows, key_rows, value_rows = queries[0], keys[0], values[0]
    dec_local, enc_local = query_rows.shape[0], key_rows.shape[0]
    chips = lax.axis_size("seq") // 2
    data_groups = lax.axis_size("dp")
    _, core = position()
    dec_rows = 2 * chips * dec_local
    enc_rows = 2 * enc_local
    block = (2 * dec_local, HALF)
    lengths = (input_lengths[0], target_lengths[0])

    def shaped(*shape, dtype=BF16):
        return jax.ShapeDtypeStruct(shape, dtype)

    def gather(block):
        blocks = [block]
        apart = chips // 2
        while apart > 1:
            blocks += [across(one, apart) for one in blocks]
            apart //= 2
        return blocks, across(block, 1)

    def forwarded(blocks):
        return [across(one, 1) for one in blocks[1:]]

    offsets = [0]
    apart = chips // 2
    while apart:
        offsets += [offset ^ apart for offset in offsets]
        apart //= 2

    features = HEADS * HEAD_SIZE
    sent = shaped(dec_local, HALF + EXTRA)
    block = shaped(2 * dec_local, HALF)

    with jax.named_scope("sibling_exchange"):
        q_recv = to_sibling(query_rows)
        docs = shaped(8, pl.cdiv(max(dec_rows, enc_local), 128) * 128, dtype=F32)
        g_send, g_keep, docs = kernel_call(
            functools.partial(prepare_kernel, offsets, dec_rows, enc_local),
            (sent, sent, docs),
            [SMEM] * 2 + [ANY] * 3,
            (VMEM, VMEM, VMEM),
            [
                pltpu.VMEM((dec_local, features), BF16),
                pltpu.VMEM((dec_local, features), BF16),
                pltpu.VMEM((1, dec_local), jnp.int32),
                pltpu.SemaphoreType.DMA((3,)),
            ],
            10**5,
            10**6,
            "prepare",
            60 * 1024 * 1024,
        )(*lengths, out_grad[0], attn_out[0], loss_mask)
        g_recv = to_sibling(g_send)

    with jax.named_scope("query_gather"):
        q_recv, _ = after(q_recv, g_keep)
        q_block = kernel_call(
            join_queries_kernel, block, [VMEM, VMEM], VMEM, [], 10**5, 10**5, "join_queries"
        )(query_rows, q_recv)
        q_far, q_near = gather(q_block)

    with jax.named_scope("setup"):
        half_rows = shaped(enc_local, HALF)
        bias = shaped(enc_local, dec_rows, dtype=F32)
        k_own, k_send, bias_own, bias_other = kernel_call(
            setup_kernel,
            (half_rows, half_rows, bias, bias),
            [VMEM] * 2,
            (VMEM,) * 4,
            [],
            10**6,
            2**22,
            "setup",
        )(docs, after(key_rows, q_block)[0])

    with jax.named_scope("cotangent_gather"):
        small = shaped(8, 2 * dec_local, dtype=F32)
        g_block, delta, count = kernel_call(
            join_cotangents_kernel,
            (block, small, shaped(8, EXTRA, dtype=F32)),
            [VMEM, VMEM],
            (VMEM,) * 3,
            [],
            10**5,
            10**5,
            "join_cotangents",
        )(g_keep, g_recv)

    def over_groups(count, apart):
        return lax.ppermute(count, "dp", [(i, i ^ apart) for i in range(data_groups)])

    with jax.named_scope("mask_count"):
        apart = 1
        while apart < data_groups // 2:
            count = count + after(over_groups(count, apart), bias_own)[0]
            apart *= 2
        rows_in_all = float(data_groups * dec_rows)

    with jax.named_scope("query_forward"):
        q_far = [q_far[0], *(after(one, bias_own, count, q_near)[0] for one in q_far[1:])]
        q_blocks = [*q_far, q_near, *forwarded(q_far)]

    with jax.named_scope("cotangent_gather"):
        sent = after(g_block, *q_far, q_near)[0]
        g_blocks = [g_block] + [across(sent, offset) for offset in offsets[1:]]

    with jax.named_scope("key_exchange"):
        v_recv = to_sibling(value_rows)
        k_send, v_recv, *_ = after(k_send, v_recv, *q_far, q_near)
        k_recv = to_sibling(k_send)

    with jax.named_scope("scores"):
        width = (dec_rows // 128 + 1) * 128
        stats = kernel_call(
            functools.partial(scores_kernel, offsets),
            shaped(2 * HALF_HEADS, width, dtype=F32),
            [VMEM] * (chips + 6),
            VMEM,
            [],
            2 * dec_rows * enc_rows * HALF,
            2 * (dec_rows + enc_rows) * HALF,
            "scores",
        )(delta, bias_own, bias_other, k_own, k_recv, count, *q_blocks)

    with jax.named_scope("stats_exchange"):
        order = [0, *sorted(offsets[1:], reverse=True)]
        all_stats = [stats] + [across(stats, offset) for offset in order[1:]]

    with jax.named_scope("grads"):
        both = shaped(enc_local, 2 * HALF)
        *dq_blocks, dkv_keep, dkv_send, count = kernel_call(
            functools.partial(grads_kernel, offsets),
            (block,) * chips + (both, both, shaped(8, EXTRA, dtype=F32)),
            [VMEM] * (3 * chips + 6),
            (VMEM,) * (chips + 3),
            [],
            10 * dec_rows * enc_rows * HALF,
            4 * (dec_rows + 2 * enc_rows) * HALF,
            "grads",
        )(bias_own, bias_other, *all_stats, *q_blocks, *g_blocks, k_own, k_recv, value_rows, v_recv)

    with jax.named_scope("query_grad_sum"):
        parts = [dq_blocks[0]]
        for j in sorted(range(1, chips), key=lambda j: -offsets[j]):
            parts.append(across(dq_blocks[j], offsets[j]))

    with jax.named_scope("key_grad_end"):
        dkv_recv = to_sibling(dkv_send)
        counts = (count, over_groups(count, data_groups // 2))
        whole = shaped(enc_local, features)
        grad_keys, grad_values, factor = kernel_call(
            functools.partial(key_end_kernel, rows_in_all),
            (whole, whole, shaped(8, EXTRA, dtype=F32)),
            [VMEM] * 4,
            (VMEM, VMEM, VMEM),
            [],
            10**6,
            2**22,
            "key_end",
        )(dkv_keep, dkv_recv, *counts)

    with jax.named_scope("query_grad_end"):
        half = shaped(dec_local, HALF)
        dq_send, dq_keep = kernel_call(
            query_end_kernel,
            (half, half),
            [VMEM] * (chips + 1),
            (VMEM, VMEM),
            [],
            10**5,
            10**6,
            "query_end",
        )(factor, *parts)
        grad_queries = in_order(dq_keep, to_sibling(dq_send), core, 1)

    return grad_queries[None], grad_keys[None], grad_values[None]


def solution(mesh):
    return jax.shard_map(
        local,
        mesh=mesh,
        in_specs=(
            P("dp", "seq", None),
            P("dp", "seq", None),
            P("dp", "seq", None),
            P("dp", "seq", None),
            P("dp", "seq", None),
            P("dp", "seq"),
            P("dp", None, None),
            P("dp", None, None),
        ),
        out_specs=(P("dp", "seq", None), P("dp", "seq", None), P("dp", "seq", None)),
        check_vma=False,
    )
```

```python
import functools
import jax
import jax.numpy as jnp
from jax import lax
from jax.experimental import pallas as pl
from jax.experimental.pallas import tpu as pltpu
from jax.sharding import PartitionSpec as P

HEADS = 8
HEAD_SIZE = 256
HALF_HEADS = HEADS // 2
HALF = HALF_HEADS * HEAD_SIZE
EXTRA = 128
ROOT = HEAD_SIZE**-0.5
NEVER = -1e30
VMEM_LIMIT = 24 * 1024 * 1024
F32 = jnp.float32
BF16 = jnp.bfloat16
ANY = pl.BlockSpec(memory_space=pl.ANY)
VMEM = pl.BlockSpec(memory_space=pltpu.VMEM)
NT = (((1,), (1,)), ((), ()))
TN = (((0,), (0,)), ((), ()))
NN = (((1,), (0,)), ((), ()))


def dot(a, b, dims):
    return lax.dot_general(a, b, dims, preferred_element_type=F32)


def position():
    me = lax.axis_index("seq")
    return me >> 1, me & 1


def to_sibling(block):
    count = lax.axis_size("seq")
    return lax.ppermute(block, "seq", [(i, i ^ 1) for i in range(count)])


def across(block, apart):
    count = lax.axis_size("seq")
    return lax.ppermute(block, "seq", [(i, i ^ (2 * apart)) for i in range(count)])


def after(block, *others):
    return lax.optimization_barrier((block, *others))


def kernel_call(
    body, out_shape, in_specs, out_specs, scratch, flops, moved, name, vmem_limit=VMEM_LIMIT
):
    return pl.pallas_call(
        body,
        out_shape=out_shape,
        in_specs=in_specs,
        out_specs=out_specs,
        scratch_shapes=scratch,
        compiler_params=pltpu.CompilerParams(vmem_limit_bytes=vmem_limit),
        cost_estimate=pl.CostEstimate(flops=flops, bytes_accessed=moved, transcendentals=0),
        name=name,
    )


def document_of(positions, lengths_ref):
    end = 0
    document = jnp.zeros_like(positions)
    for i in range(lengths_ref.shape[1]):
        end = end + lengths_ref[0, i]
        document += (positions >= end).astype(jnp.int32)
    return document


def prepare_kernel(
    offsets,
    dec_rows,
    enc_rows,
    in_any,
    target_any,
    grad_ref,
    out_ref,
    mask_ref,
    send_ref,
    keep_ref,
    docs_ref,
    in_ref,
    target_ref,
    grad_held,
    out_held,
    mask_held,
    sems,
):
    chip, core = position()
    rows = grad_ref.shape[0]
    copies = start_all(
        [
            (in_any, in_ref),
            (target_any, target_ref),
            (mask_ref, mask_held),
            (grad_ref, grad_held),
            (out_ref, out_held),
        ],
        sems,
    )
    for copy in copies[:3]:
        copy.wait()
    lane = lax.broadcasted_iota(jnp.int32, (1, docs_ref.shape[1]), 1)
    block = dec_rows // len(offsets)
    dec = lane + chip * block
    for j, offset in enumerate(offsets[1:], 1):
        dec = jnp.where(lane >= j * block, lane + ((chip ^ offset) - j) * block, dec)
    docs = [document_of(dec, target_ref)]
    for side in (core, 1 - core):
        docs.append(document_of(lane + (2 * chip + side) * enc_rows, in_ref))
    docs_ref[...] = jnp.concatenate(docs + docs + docs[:2], 0).astype(F32)
    mask_row = mask_held[...].astype(F32)
    here = lax.broadcasted_iota(jnp.int32, (rows, rows), 0) == lax.broadcasted_iota(
        jnp.int32, (rows, rows), 1
    )
    mask = jnp.sum(jnp.where(here, mask_row, 0.0), axis=1, keepdims=True)
    lane = lax.broadcasted_iota(jnp.int32, (rows, EXTRA), 1)
    for copy in copies[3:]:
        copy.wait()
    masked = grad_held[...].astype(F32) * mask
    products = masked * out_held[...].astype(F32)
    grad_held[...] = masked.astype(BF16)
    halves = []
    for half in range(2):
        extra = jnp.where(lane == HALF_HEADS, mask, 0.0)
        for head in range(HALF_HEADS):
            first = half * HALF + head * HEAD_SIZE
            delta = jnp.sum(products[:, first : first + HEAD_SIZE], axis=1, keepdims=True)
            extra = jnp.where(lane == head, delta, extra)
        halves.append(extra)
    for ref, half in ((send_ref, 1 - core), (keep_ref, core)):
        ref[:, :HALF] = grad_held[:, pl.ds(pl.multiple_of(half * HALF, HALF), HALF)]
        ref[:, HALF:] = jnp.where(half == 0, halves[0], halves[1]).astype(BF16)


def in_core_order(own, other, core):
    own, other = own.astype(F32), other.astype(F32)
    joined = jnp.where(
        core == 0, jnp.concatenate([own, other], 0), jnp.concatenate([other, own], 0)
    )
    return joined.astype(BF16)


def join_queries_kernel(own_ref, other_ref, joined_ref):
    _, core = position()
    mine = pl.ds(pl.multiple_of(core * HALF, HALF), HALF)
    joined_ref[...] = in_core_order(own_ref[:, mine], other_ref[:, mine], core)


def join_cotangents_kernel(own_ref, other_ref, joined_ref, delta_ref, count_ref):
    _, core = position()
    joined_ref[...] = in_core_order(own_ref[:, :HALF], other_ref[:, :HALF], core)
    extra = jnp.transpose(in_core_order(own_ref[:, HALF:], other_ref[:, HALF:], core).astype(F32))
    delta_ref[...] = extra[: delta_ref.shape[0]]
    count = jnp.sum(extra[HALF_HEADS : HALF_HEADS + 1], axis=1, keepdims=True)
    count_ref[...] = jnp.broadcast_to(count, count_ref.shape)


def split_kernel(rows_ref, own_ref, send_ref):
    _, core = position()
    for ref, half in ((own_ref, core), (send_ref, 1 - core)):
        ref[...] = rows_ref[:, pl.ds(pl.multiple_of(half * HALF, HALF), HALF)]


def setup_kernel(docs_ref, key_ref, k_ref, send_ref, bias_own, bias_other):
    split_kernel(key_ref, k_ref, send_ref)
    enc_rows, dec_rows = bias_own.shape
    dec = docs_ref[0:1, :dec_rows]
    columns = jnp.transpose(docs_ref[:, :enc_rows])
    for ref, column in ((bias_own, 1), (bias_other, 2)):
        ref[...] = jnp.where(columns[:, column : column + 1] == dec, 0.0, NEVER)


def start_all(pairs, sems):
    copies = [pltpu.make_async_copy(a, b, sems.at[i]) for i, (a, b) in enumerate(pairs)]
    for copy in copies:
        copy.start()
    return copies


def rows_of(blocks, head):
    columns = slice(head * HEAD_SIZE, (head + 1) * HEAD_SIZE)
    return jnp.concatenate([block[:, columns] for block in blocks], 0)


def value_columns_of(head):
    _, core = position()
    first = core * HALF + head * HEAD_SIZE
    return pl.ds(pl.multiple_of(first, HEAD_SIZE), HEAD_SIZE)


def columns_of(head):
    return slice(head * HEAD_SIZE, (head + 1) * HEAD_SIZE)


def scores_kernel(offsets, delta_ref, bias_own, bias_other, key_ref, other_ref, *refs):
    count_ref, refs = refs[0], refs[1:]
    blocks, (stats_ref,) = refs[: len(offsets)], refs[len(offsets) :]
    rows = blocks[0].shape[0]
    dec_rows = rows * len(offsets)
    stats_ref[...] = jnp.broadcast_to(count_ref[0:1, 0:1], stats_ref.shape)
    stats_ref[HALF_HEADS:, :rows] = delta_ref[:HALF_HEADS]
    for head in range(HALF_HEADS):
        q = rows_of(blocks, head)
        scores = [
            dot(k[:, columns_of(head)], q, NT) * ROOT + bias[...]
            for k, bias in ((key_ref, bias_own), (other_ref, bias_other))
        ]
        top = functools.reduce(jnp.maximum, [jnp.max(s, axis=0, keepdims=True) for s in scores])
        top = jnp.maximum(top, -1e20)
        total = sum(jnp.sum(jnp.exp(s - top), axis=0, keepdims=True) for s in scores)
        stats_ref[head : head + 1, :dec_rows] = jnp.where(
            total > 0, top + jnp.log(jnp.maximum(total, 1e-30)), NEVER
        )


def gathered_stats(offsets, stats, rows):
    logs = []
    for sender, ref in zip(offsets, stats):
        order = [offsets.index(offset ^ sender) for offset in offsets]
        logs.append(
            jnp.concatenate([ref[:HALF_HEADS, j * rows : (j + 1) * rows] for j in order], 1)
        )
    top = functools.reduce(jnp.maximum, logs)
    log_total = top + jnp.log(sum(jnp.exp(log - top) for log in logs))
    delta = jnp.concatenate([ref[HALF_HEADS:, :rows] for ref in stats], 1)
    last = stats[0].shape[1] - 1
    return log_total, delta, sum(ref[0:1, last:] for ref in stats)


def grads_kernel(offsets, bias_own, bias_other, *refs):
    chips = len(offsets)
    order = [0, *sorted(offsets[1:], reverse=True)]
    stats, refs = [refs[order.index(offset)] for offset in offsets], refs[chips:]
    q_blocks, refs = refs[:chips], refs[chips:]
    g_blocks, refs = refs[:chips], refs[chips:]
    (key_ref, key_other, value_ref, value_other), refs = refs[:4], refs[4:]
    dq_blocks, (keep_ref, send_ref, count_ref) = refs[:chips], refs[chips:]
    rows = q_blocks[0].shape[0]
    log_total, delta, count = gathered_stats(offsets, stats, rows)
    count_ref[...] = jnp.broadcast_to(count, count_ref.shape)
    for head in range(HALF_HEADS):
        columns = slice(head * HEAD_SIZE, (head + 1) * HEAD_SIZE)
        value_columns = slice(HALF + columns.start, HALF + columns.stop)
        line = slice(head, head + 1)
        q, g = rows_of(q_blocks, head), rows_of(g_blocks, head)
        dq = 0.0
        for key, value, bias, out_ref in (
            (key_ref, value_ref, bias_own, keep_ref),
            (key_other, value_other, bias_other, send_ref),
        ):
            k, v = key[:, columns], value[:, value_columns_of(head)]
            probs = jnp.exp(dot(k, q, NT) * ROOT + bias[...] - log_total[line])
            dscore = (probs * (dot(v, g, NT) - delta[line])).astype(BF16)
            dq += dot(dscore, k, TN)
            out_ref[:, columns] = (dot(dscore, q, NN) * ROOT).astype(BF16)
            out_ref[:, value_columns] = dot(probs.astype(BF16), g, NN).astype(BF16)
        dq = (dq * ROOT).astype(BF16)
        for j, block in enumerate(dq_blocks):
            block[:, columns] = dq[j * rows : (j + 1) * rows]


def key_end_kernel(rows_in_all, keep_ref, other_ref, *refs):
    counts, (dk_ref, dv_ref, factor_ref) = refs[:2], refs[2:]
    _, core = position()
    factor = rows_in_all / (counts[0][0:1, 0:1] + counts[1][0:1, 0:1])
    factor_ref[...] = jnp.broadcast_to(factor, factor_ref.shape)
    for ref, side in ((keep_ref, core), (other_ref, 1 - core)):
        columns = pl.ds(pl.multiple_of(side * HALF, HALF), HALF)
        dk_ref[:, columns] = (ref[:, :HALF].astype(F32) * factor).astype(BF16)
        dv_ref[:, columns] = (ref[:, HALF:].astype(F32) * factor).astype(BF16)


def query_end_kernel(factor_ref, *refs):
    parts, (send_ref, keep_ref) = refs[:-2], refs[-2:]
    _, core = position()
    summed = factor_ref[0:1, 0:1] * sum(part[...].astype(F32) for part in parts)
    half = summed.shape[0] // 2
    low, high = summed[:half], summed[half:]
    send_ref[...] = jnp.where(core == 0, high, low).astype(BF16)
    keep_ref[...] = jnp.where(core == 0, low, high).astype(BF16)


def in_order(own, other, core, axis):
    return jnp.where(
        core == 0, jnp.concatenate([own, other], axis), jnp.concatenate([other, own], axis)
    )


def local(queries, keys, values, attn_out, out_grad, loss_mask, input_lengths, target_lengths):
    query_rows, key_rows, value_rows = queries[0], keys[0], values[0]
    dec_local, enc_local = query_rows.shape[0], key_rows.shape[0]
    chips = lax.axis_size("seq") // 2
    data_groups = lax.axis_size("dp")
    _, core = position()
    dec_rows = 2 * chips * dec_local
    enc_rows = 2 * enc_local
    block = (2 * dec_local, HALF)
    lengths = (input_lengths[0], target_lengths[0])

    def shaped(*shape, dtype=BF16):
        return jax.ShapeDtypeStruct(shape, dtype)

    def gather(block):
        blocks = [block]
        apart = chips // 2
        while apart > 1:
            blocks += [across(one, apart) for one in blocks]
            apart //= 2
        return blocks, across(block, 1)

    def forwarded(blocks):
        return [across(one, 1) for one in blocks[1:]]

    offsets = [0]
    apart = chips // 2
    while apart:
        offsets += [offset ^ apart for offset in offsets]
        apart //= 2

    features = HEADS * HEAD_SIZE
    sent = shaped(dec_local, HALF + EXTRA)
    block = shaped(2 * dec_local, HALF)

    with jax.named_scope("sibling_exchange"):
        q_recv = to_sibling(query_rows)
        docs = shaped(8, pl.cdiv(max(dec_rows, enc_local), 128) * 128, dtype=F32)
        g_send, g_keep, docs = kernel_call(
            functools.partial(prepare_kernel, offsets, dec_rows, enc_local),
            (sent, sent, docs),
            [ANY] * 5,
            (VMEM, VMEM, VMEM),
            [
                pltpu.SMEM(lengths[0].shape, jnp.int32),
                pltpu.SMEM(lengths[1].shape, jnp.int32),
                pltpu.VMEM((dec_local, features), BF16),
                pltpu.VMEM((dec_local, features), BF16),
                pltpu.VMEM((1, dec_local), jnp.int32),
                pltpu.SemaphoreType.DMA((5,)),
            ],
            10**5,
            10**6,
            "prepare",
            60 * 1024 * 1024,
        )(*lengths, out_grad[0], attn_out[0], loss_mask)
        g_recv = to_sibling(g_send)

    with jax.named_scope("query_gather"):
        q_recv, _ = after(q_recv, g_keep)
        q_block = kernel_call(
            join_queries_kernel, block, [VMEM, VMEM], VMEM, [], 10**5, 10**5, "join_queries"
        )(query_rows, q_recv)
        q_far, q_near = gather(q_block)

    with jax.named_scope("setup"):
        half_rows = shaped(enc_local, HALF)
        bias = shaped(enc_local, dec_rows, dtype=F32)
        k_own, k_send, bias_own, bias_other = kernel_call(
            setup_kernel,
            (half_rows, half_rows, bias, bias),
            [VMEM] * 2,
            (VMEM,) * 4,
            [],
            10**6,
            2**22,
            "setup",
        )(docs, after(key_rows, q_block)[0])

    with jax.named_scope("cotangent_gather"):
        small = shaped(8, 2 * dec_local, dtype=F32)
        g_block, delta, count = kernel_call(
            join_cotangents_kernel,
            (block, small, shaped(8, EXTRA, dtype=F32)),
            [VMEM, VMEM],
            (VMEM,) * 3,
            [],
            10**5,
            10**5,
            "join_cotangents",
        )(g_keep, g_recv)

    def over_groups(count, apart):
        return lax.ppermute(count, "dp", [(i, i ^ apart) for i in range(data_groups)])

    with jax.named_scope("mask_count"):
        apart = 1
        while apart < data_groups // 2:
            count = count + after(over_groups(count, apart), bias_own)[0]
            apart *= 2
        rows_in_all = float(data_groups * dec_rows)

    with jax.named_scope("query_forward"):
        q_far = [q_far[0], *(after(one, bias_own, count, q_near)[0] for one in q_far[1:])]
        q_blocks = [*q_far, q_near, *forwarded(q_far)]

    with jax.named_scope("cotangent_gather"):
        sent = after(g_block, *q_far, q_near)[0]
        g_blocks = [g_block] + [across(sent, offset) for offset in offsets[1:]]

    with jax.named_scope("key_exchange"):
        v_recv = to_sibling(after(value_rows, q_recv)[0])
        k_send, v_recv, *_ = after(k_send, v_recv, *q_far, q_near)
        k_recv = to_sibling(k_send)

    with jax.named_scope("scores"):
        width = (dec_rows // 128 + 1) * 128
        stats = kernel_call(
            functools.partial(scores_kernel, offsets),
            shaped(2 * HALF_HEADS, width, dtype=F32),
            [VMEM] * (chips + 6),
            VMEM,
            [],
            2 * dec_rows * enc_rows * HALF,
            2 * (dec_rows + enc_rows) * HALF,
            "scores",
        )(delta, bias_own, bias_other, k_own, k_recv, count, *q_blocks)

    with jax.named_scope("stats_exchange"):
        order = [0, *sorted(offsets[1:], reverse=True)]
        all_stats = [stats] + [across(stats, offset) for offset in order[1:]]

    with jax.named_scope("grads"):
        both = shaped(enc_local, 2 * HALF)
        *dq_blocks, dkv_keep, dkv_send, count = kernel_call(
            functools.partial(grads_kernel, offsets),
            (block,) * chips + (both, both, shaped(8, EXTRA, dtype=F32)),
            [VMEM] * (3 * chips + 6),
            (VMEM,) * (chips + 3),
            [],
            10 * dec_rows * enc_rows * HALF,
            4 * (dec_rows + 2 * enc_rows) * HALF,
            "grads",
        )(bias_own, bias_other, *all_stats, *q_blocks, *g_blocks, k_own, k_recv, value_rows, v_recv)

    with jax.named_scope("query_grad_sum"):
        parts = [dq_blocks[0]]
        for j in sorted(range(1, chips), key=lambda j: -offsets[j]):
            parts.append(across(dq_blocks[j], offsets[j]))

    with jax.named_scope("key_grad_end"):
        dkv_recv = to_sibling(dkv_send)
        counts = (count, over_groups(count, data_groups // 2))
        whole = shaped(enc_local, features)
        grad_keys, grad_values, factor = kernel_call(
            functools.partial(key_end_kernel, rows_in_all),
            (whole, whole, shaped(8, EXTRA, dtype=F32)),
            [VMEM] * 4,
            (VMEM, VMEM, VMEM),
            [],
            10**6,
            2**22,
            "key_end",
        )(dkv_keep, dkv_recv, *counts)

    with jax.named_scope("query_grad_end"):
        half = shaped(dec_local, HALF)
        dq_send, dq_keep = kernel_call(
            query_end_kernel,
            (half, half),
            [VMEM] * (chips + 1),
            (VMEM, VMEM),
            [],
            10**5,
            10**6,
            "query_end",
        )(factor, *parts)
        grad_queries = in_order(dq_keep, to_sibling(dq_send), core, 1)

    return grad_queries[None], grad_keys[None], grad_values[None]


def solution(mesh):
    return jax.shard_map(
        local,
        mesh=mesh,
        in_specs=(
            P("dp", "seq", None),
            P("dp", "seq", None),
            P("dp", "seq", None),
            P("dp", "seq", None),
            P("dp", "seq", None),
            P("dp", "seq"),
            P("dp", None, None),
            P("dp", None, None),
        ),
        out_specs=(P("dp", "seq", None), P("dp", "seq", None), P("dp", "seq", None)),
        check_vma=False,
    )
```

```python
import functools
import jax
import jax.numpy as jnp
from jax import lax
from jax.experimental import pallas as pl
from jax.experimental.pallas import tpu as pltpu
from jax.sharding import PartitionSpec as P

HEADS = 8
HEAD_SIZE = 256
HALF_HEADS = HEADS // 2
HALF = HALF_HEADS * HEAD_SIZE
EXTRA = 128
ROOT = HEAD_SIZE**-0.5
NEVER = -1e30
VMEM_LIMIT = 24 * 1024 * 1024
F32 = jnp.float32
BF16 = jnp.bfloat16
ANY = pl.BlockSpec(memory_space=pl.ANY)
VMEM = pl.BlockSpec(memory_space=pltpu.VMEM)
NT = (((1,), (1,)), ((), ()))
TN = (((0,), (0,)), ((), ()))
NN = (((1,), (0,)), ((), ()))


def dot(a, b, dims):
    return lax.dot_general(a, b, dims, preferred_element_type=F32)


def position():
    me = lax.axis_index("seq")
    return me >> 1, me & 1


def to_sibling(block):
    count = lax.axis_size("seq")
    return lax.ppermute(block, "seq", [(i, i ^ 1) for i in range(count)])


def across(block, apart):
    count = lax.axis_size("seq")
    return lax.ppermute(block, "seq", [(i, i ^ (2 * apart)) for i in range(count)])


def after(block, *others):
    return lax.optimization_barrier((block, *others))


def kernel_call(
    body, out_shape, in_specs, out_specs, scratch, flops, moved, name, vmem_limit=VMEM_LIMIT
):
    return pl.pallas_call(
        body,
        out_shape=out_shape,
        in_specs=in_specs,
        out_specs=out_specs,
        scratch_shapes=scratch,
        compiler_params=pltpu.CompilerParams(vmem_limit_bytes=vmem_limit),
        cost_estimate=pl.CostEstimate(flops=flops, bytes_accessed=moved, transcendentals=0),
        name=name,
    )


def document_of(positions, lengths_ref):
    end = 0
    document = jnp.zeros_like(positions)
    for i in range(lengths_ref.shape[1]):
        end = end + lengths_ref[0, i]
        document += (positions >= end).astype(jnp.int32)
    return document


def prepare_kernel(
    offsets,
    dec_rows,
    enc_rows,
    in_any,
    target_any,
    grad_ref,
    out_ref,
    mask_ref,
    send_ref,
    keep_ref,
    docs_ref,
    in_ref,
    target_ref,
    grad_held,
    out_held,
    mask_held,
    sems,
):
    chip, core = position()
    rows = grad_ref.shape[0]
    copies = start_all(
        [
            (in_any, in_ref),
            (target_any, target_ref),
            (mask_ref, mask_held),
            (grad_ref, grad_held),
            (out_ref, out_held),
        ],
        sems,
    )
    for copy in copies[:3]:
        copy.wait()
    lane = lax.broadcasted_iota(jnp.int32, (1, docs_ref.shape[1]), 1)
    block = dec_rows // len(offsets)
    dec = lane + chip * block
    for j, offset in enumerate(offsets[1:], 1):
        dec = jnp.where(lane >= j * block, lane + ((chip ^ offset) - j) * block, dec)
    docs = [document_of(dec, target_ref)]
    for side in (core, 1 - core):
        docs.append(document_of(lane + (2 * chip + side) * enc_rows, in_ref))
    docs_ref[...] = jnp.concatenate(docs + docs + docs[:2], 0).astype(F32)
    mask_row = mask_held[...].astype(F32)
    here = lax.broadcasted_iota(jnp.int32, (rows, rows), 0) == lax.broadcasted_iota(
        jnp.int32, (rows, rows), 1
    )
    mask = jnp.sum(jnp.where(here, mask_row, 0.0), axis=1, keepdims=True)
    lane = lax.broadcasted_iota(jnp.int32, (rows, EXTRA), 1)
    for copy in copies[3:]:
        copy.wait()
    masked = grad_held[...].astype(F32) * mask
    products = masked * out_held[...].astype(F32)
    grad_held[...] = masked.astype(BF16)
    halves = []
    for half in range(2):
        extra = jnp.where(lane == HALF_HEADS, mask, 0.0)
        for head in range(HALF_HEADS):
            first = half * HALF + head * HEAD_SIZE
            delta = jnp.sum(products[:, first : first + HEAD_SIZE], axis=1, keepdims=True)
            extra = jnp.where(lane == head, delta, extra)
        halves.append(extra)
    for ref, half in ((send_ref, 1 - core), (keep_ref, core)):
        ref[:, :HALF] = grad_held[:, pl.ds(pl.multiple_of(half * HALF, HALF), HALF)]
        ref[:, HALF:] = jnp.where(half == 0, halves[0], halves[1]).astype(BF16)


def in_core_order(own, other, core):
    own, other = own.astype(F32), other.astype(F32)
    joined = jnp.where(
        core == 0, jnp.concatenate([own, other], 0), jnp.concatenate([other, own], 0)
    )
    return joined.astype(BF16)


def join_queries_kernel(own_ref, other_ref, joined_ref):
    _, core = position()
    mine = pl.ds(pl.multiple_of(core * HALF, HALF), HALF)
    joined_ref[...] = in_core_order(own_ref[:, mine], other_ref[:, mine], core)


def join_cotangents_kernel(own_ref, other_ref, joined_ref, delta_ref, count_ref):
    _, core = position()
    joined_ref[...] = in_core_order(own_ref[:, :HALF], other_ref[:, :HALF], core)
    extra = jnp.transpose(in_core_order(own_ref[:, HALF:], other_ref[:, HALF:], core).astype(F32))
    delta_ref[...] = extra[: delta_ref.shape[0]]
    count = jnp.sum(extra[HALF_HEADS : HALF_HEADS + 1], axis=1, keepdims=True)
    count_ref[...] = jnp.broadcast_to(count, count_ref.shape)


def split_kernel(rows_ref, own_ref, send_ref):
    _, core = position()
    for ref, half in ((own_ref, core), (send_ref, 1 - core)):
        ref[...] = rows_ref[:, pl.ds(pl.multiple_of(half * HALF, HALF), HALF)]


def setup_kernel(docs_ref, key_ref, k_ref, send_ref, bias_own, bias_other):
    split_kernel(key_ref, k_ref, send_ref)
    enc_rows, dec_rows = bias_own.shape
    dec = docs_ref[0:1, :dec_rows]
    columns = jnp.transpose(docs_ref[:, :enc_rows])
    for ref, column in ((bias_own, 1), (bias_other, 2)):
        ref[...] = jnp.where(columns[:, column : column + 1] == dec, 0.0, NEVER)


def start_all(pairs, sems):
    copies = [pltpu.make_async_copy(a, b, sems.at[i]) for i, (a, b) in enumerate(pairs)]
    for copy in copies:
        copy.start()
    return copies


def rows_of(blocks, head):
    columns = slice(head * HEAD_SIZE, (head + 1) * HEAD_SIZE)
    return jnp.concatenate([block[:, columns] for block in blocks], 0)


def value_columns_of(head):
    _, core = position()
    first = core * HALF + head * HEAD_SIZE
    return pl.ds(pl.multiple_of(first, HEAD_SIZE), HEAD_SIZE)


def columns_of(head):
    return slice(head * HEAD_SIZE, (head + 1) * HEAD_SIZE)


def scores_kernel(offsets, delta_ref, bias_own, bias_other, key_ref, other_ref, *refs):
    count_ref, refs = refs[0], refs[1:]
    blocks, (stats_ref,) = refs[: len(offsets)], refs[len(offsets) :]
    rows = blocks[0].shape[0]
    dec_rows = rows * len(offsets)
    stats_ref[...] = jnp.broadcast_to(count_ref[0:1, 0:1], stats_ref.shape)
    stats_ref[HALF_HEADS:, :rows] = delta_ref[:HALF_HEADS]
    for head in range(HALF_HEADS):
        q = rows_of(blocks, head)
        scores = [
            dot(k[:, columns_of(head)], q, NT) * ROOT + bias[...]
            for k, bias in ((key_ref, bias_own), (other_ref, bias_other))
        ]
        top = functools.reduce(jnp.maximum, [jnp.max(s, axis=0, keepdims=True) for s in scores])
        top = jnp.maximum(top, -1e20)
        total = sum(jnp.sum(jnp.exp(s - top), axis=0, keepdims=True) for s in scores)
        stats_ref[head : head + 1, :dec_rows] = jnp.where(
            total > 0, top + jnp.log(jnp.maximum(total, 1e-30)), NEVER
        )


def gathered_stats(offsets, stats, rows):
    logs = []
    for sender, ref in zip(offsets, stats):
        order = [offsets.index(offset ^ sender) for offset in offsets]
        logs.append(
            jnp.concatenate([ref[:HALF_HEADS, j * rows : (j + 1) * rows] for j in order], 1)
        )
    top = functools.reduce(jnp.maximum, logs)
    log_total = top + jnp.log(sum(jnp.exp(log - top) for log in logs))
    delta = jnp.concatenate([ref[HALF_HEADS:, :rows] for ref in stats], 1)
    last = stats[0].shape[1] - 1
    return log_total, delta, sum(ref[0:1, last:] for ref in stats)


def grads_kernel(offsets, bias_own, bias_other, *refs):
    chips = len(offsets)
    order = [0, *sorted(offsets[1:], reverse=True)]
    stats, refs = [refs[order.index(offset)] for offset in offsets], refs[chips:]
    q_blocks, refs = refs[:chips], refs[chips:]
    g_blocks, refs = refs[:chips], refs[chips:]
    (key_ref, key_other, value_ref, value_other), refs = refs[:4], refs[4:]
    dq_blocks, (keep_ref, send_ref, count_ref) = refs[:chips], refs[chips:]
    rows = q_blocks[0].shape[0]
    log_total, delta, count = gathered_stats(offsets, stats, rows)
    count_ref[...] = jnp.broadcast_to(count, count_ref.shape)
    for head in range(HALF_HEADS):
        columns = slice(head * HEAD_SIZE, (head + 1) * HEAD_SIZE)
        value_columns = slice(HALF + columns.start, HALF + columns.stop)
        line = slice(head, head + 1)
        q, g = rows_of(q_blocks, head), rows_of(g_blocks, head)
        dq = 0.0
        for key, value, bias, out_ref in (
            (key_ref, value_ref, bias_own, keep_ref),
            (key_other, value_other, bias_other, send_ref),
        ):
            k, v = key[:, columns], value[:, value_columns_of(head)]
            probs = jnp.exp(dot(k, q, NT) * ROOT + bias[...] - log_total[line])
            dscore = (probs * (dot(v, g, NT) - delta[line])).astype(BF16)
            dq += dot(dscore, k, TN)
            out_ref[:, columns] = (dot(dscore, q, NN) * ROOT).astype(BF16)
            out_ref[:, value_columns] = dot(probs.astype(BF16), g, NN).astype(BF16)
        dq = (dq * ROOT).astype(BF16)
        for j, block in enumerate(dq_blocks):
            block[:, columns] = dq[j * rows : (j + 1) * rows]


def key_end_kernel(rows_in_all, keep_ref, other_ref, *refs):
    counts, (dk_ref, dv_ref, factor_ref) = refs[:2], refs[2:]
    _, core = position()
    factor = rows_in_all / (counts[0][0:1, 0:1] + counts[1][0:1, 0:1])
    factor_ref[...] = jnp.broadcast_to(factor, factor_ref.shape)
    for ref, side in ((keep_ref, core), (other_ref, 1 - core)):
        columns = pl.ds(pl.multiple_of(side * HALF, HALF), HALF)
        dk_ref[:, columns] = (ref[:, :HALF].astype(F32) * factor).astype(BF16)
        dv_ref[:, columns] = (ref[:, HALF:].astype(F32) * factor).astype(BF16)


def query_end_kernel(factor_ref, *refs):
    parts, (send_ref, keep_ref) = refs[:-2], refs[-2:]
    _, core = position()
    summed = factor_ref[0:1, 0:1] * sum(part[...].astype(F32) for part in parts)
    half = summed.shape[0] // 2
    low, high = summed[:half], summed[half:]
    send_ref[...] = jnp.where(core == 0, high, low).astype(BF16)
    keep_ref[...] = jnp.where(core == 0, low, high).astype(BF16)


def in_order(own, other, core, axis):
    return jnp.where(
        core == 0, jnp.concatenate([own, other], axis), jnp.concatenate([other, own], axis)
    )


def local(queries, keys, values, attn_out, out_grad, loss_mask, input_lengths, target_lengths):
    query_rows, key_rows, value_rows = queries[0], keys[0], values[0]
    dec_local, enc_local = query_rows.shape[0], key_rows.shape[0]
    chips = lax.axis_size("seq") // 2
    data_groups = lax.axis_size("dp")
    _, core = position()
    dec_rows = 2 * chips * dec_local
    enc_rows = 2 * enc_local
    block = (2 * dec_local, HALF)
    lengths = (input_lengths[0], target_lengths[0])

    def shaped(*shape, dtype=BF16):
        return jax.ShapeDtypeStruct(shape, dtype)

    def gather(block):
        blocks = [block]
        apart = chips // 2
        while apart > 1:
            blocks += [across(one, apart) for one in blocks]
            apart //= 2
        return blocks, across(block, 1)

    def forwarded(blocks):
        return [across(one, 1) for one in blocks[1:]]

    offsets = [0]
    apart = chips // 2
    while apart:
        offsets += [offset ^ apart for offset in offsets]
        apart //= 2

    features = HEADS * HEAD_SIZE
    sent = shaped(dec_local, HALF + EXTRA)
    block = shaped(2 * dec_local, HALF)

    with jax.named_scope("sibling_exchange"):
        q_recv = to_sibling(query_rows)
        docs = shaped(8, pl.cdiv(max(dec_rows, enc_local), 128) * 128, dtype=F32)
        g_send, g_keep, docs = kernel_call(
            functools.partial(prepare_kernel, offsets, dec_rows, enc_local),
            (sent, sent, docs),
            [ANY] * 5,
            (VMEM, VMEM, VMEM),
            [
                pltpu.SMEM(lengths[0].shape, jnp.int32),
                pltpu.SMEM(lengths[1].shape, jnp.int32),
                pltpu.VMEM((dec_local, features), BF16),
                pltpu.VMEM((dec_local, features), BF16),
                pltpu.VMEM((1, dec_local), jnp.int32),
                pltpu.SemaphoreType.DMA((5,)),
            ],
            10**5,
            10**6,
            "prepare",
            60 * 1024 * 1024,
        )(*lengths, out_grad[0], attn_out[0], loss_mask)
        g_recv = to_sibling(g_send)

    with jax.named_scope("query_gather"):
        q_recv, _ = after(q_recv, g_keep)
        q_block = kernel_call(
            join_queries_kernel, block, [VMEM, VMEM], VMEM, [], 10**5, 10**5, "join_queries"
        )(query_rows, q_recv)
        q_far, q_near = gather(q_block)

    with jax.named_scope("setup"):
        half_rows = shaped(enc_local, HALF)
        bias = shaped(enc_local, dec_rows, dtype=F32)
        k_own, k_send, bias_own, bias_other = kernel_call(
            setup_kernel,
            (half_rows, half_rows, bias, bias),
            [VMEM] * 2,
            (VMEM,) * 4,
            [],
            10**6,
            2**22,
            "setup",
        )(docs, after(key_rows, q_block)[0])

    with jax.named_scope("cotangent_gather"):
        small = shaped(8, 2 * dec_local, dtype=F32)
        g_block, delta, count = kernel_call(
            join_cotangents_kernel,
            (block, small, shaped(8, EXTRA, dtype=F32)),
            [VMEM, VMEM],
            (VMEM,) * 3,
            [],
            10**5,
            10**5,
            "join_cotangents",
        )(g_keep, g_recv)

    def over_groups(count, apart):
        return lax.ppermute(count, "dp", [(i, i ^ apart) for i in range(data_groups)])

    with jax.named_scope("mask_count"):
        apart = 1
        while apart < data_groups // 2:
            count = count + after(over_groups(count, apart), bias_own)[0]
            apart *= 2
        rows_in_all = float(data_groups * dec_rows)

    with jax.named_scope("query_forward"):
        q_far = [q_far[0], *(after(one, bias_own, count)[0] for one in q_far[1:])]
        q_blocks = [*q_far, q_near, *forwarded(q_far)]

    with jax.named_scope("cotangent_gather"):
        sent = after(g_block, *q_far, q_near)[0]
        g_blocks = [g_block] + [across(sent, offset) for offset in offsets[1:]]

    with jax.named_scope("key_exchange"):
        v_recv = to_sibling(after(value_rows, q_recv)[0])
        k_send, v_recv, *_ = after(k_send, v_recv, *q_far, q_near)
        k_recv = to_sibling(k_send)

    with jax.named_scope("scores"):
        width = (dec_rows // 128 + 1) * 128
        stats = kernel_call(
            functools.partial(scores_kernel, offsets),
            shaped(2 * HALF_HEADS, width, dtype=F32),
            [VMEM] * (chips + 6),
            VMEM,
            [],
            2 * dec_rows * enc_rows * HALF,
            2 * (dec_rows + enc_rows) * HALF,
            "scores",
        )(delta, bias_own, bias_other, k_own, k_recv, count, *q_blocks)

    with jax.named_scope("stats_exchange"):
        order = [0, *sorted(offsets[1:], reverse=True)]
        all_stats = [stats] + [across(stats, offset) for offset in order[1:]]

    with jax.named_scope("grads"):
        both = shaped(enc_local, 2 * HALF)
        *dq_blocks, dkv_keep, dkv_send, count = kernel_call(
            functools.partial(grads_kernel, offsets),
            (block,) * chips + (both, both, shaped(8, EXTRA, dtype=F32)),
            [VMEM] * (3 * chips + 6),
            (VMEM,) * (chips + 3),
            [],
            10 * dec_rows * enc_rows * HALF,
            4 * (dec_rows + 2 * enc_rows) * HALF,
            "grads",
        )(bias_own, bias_other, *all_stats, *q_blocks, *g_blocks, k_own, k_recv, value_rows, v_recv)

    with jax.named_scope("query_grad_sum"):
        parts = [dq_blocks[0]]
        for j in sorted(range(1, chips), key=lambda j: -offsets[j]):
            parts.append(across(dq_blocks[j], offsets[j]))

    with jax.named_scope("key_grad_end"):
        dkv_recv = to_sibling(dkv_send)
        counts = (count, over_groups(count, data_groups // 2))
        whole = shaped(enc_local, features)
        grad_keys, grad_values, factor = kernel_call(
            functools.partial(key_end_kernel, rows_in_all),
            (whole, whole, shaped(8, EXTRA, dtype=F32)),
            [VMEM] * 4,
            (VMEM, VMEM, VMEM),
            [],
            10**6,
            2**22,
            "key_end",
        )(dkv_keep, dkv_recv, *counts)

    with jax.named_scope("query_grad_end"):
        half = shaped(dec_local, HALF)
        dq_send, dq_keep = kernel_call(
            query_end_kernel,
            (half, half),
            [VMEM] * (chips + 1),
            (VMEM, VMEM),
            [],
            10**5,
            10**6,
            "query_end",
        )(factor, *parts)
        grad_queries = in_order(dq_keep, to_sibling(dq_send), core, 1)

    return grad_queries[None], grad_keys[None], grad_values[None]


def solution(mesh):
    return jax.shard_map(
        local,
        mesh=mesh,
        in_specs=(
            P("dp", "seq", None),
            P("dp", "seq", None),
            P("dp", "seq", None),
            P("dp", "seq", None),
            P("dp", "seq", None),
            P("dp", "seq"),
            P("dp", None, None),
            P("dp", None, None),
        ),
        out_specs=(P("dp", "seq", None), P("dp", "seq", None), P("dp", "seq", None)),
        check_vma=False,
    )
```

```python
import functools
import jax
import jax.numpy as jnp
from jax import lax
from jax.experimental import pallas as pl
from jax.experimental.pallas import tpu as pltpu
from jax.sharding import PartitionSpec as P

HEADS = 8
HEAD_SIZE = 256
HALF_HEADS = HEADS // 2
HALF = HALF_HEADS * HEAD_SIZE
EXTRA = 128
ROOT = HEAD_SIZE**-0.5
NEVER = -1e30
VMEM_LIMIT = 24 * 1024 * 1024
F32 = jnp.float32
BF16 = jnp.bfloat16
ANY = pl.BlockSpec(memory_space=pl.ANY)
VMEM = pl.BlockSpec(memory_space=pltpu.VMEM)
NT = (((1,), (1,)), ((), ()))
TN = (((0,), (0,)), ((), ()))
NN = (((1,), (0,)), ((), ()))


def dot(a, b, dims):
    return lax.dot_general(a, b, dims, preferred_element_type=F32)


def position():
    me = lax.axis_index("seq")
    return me >> 1, me & 1


def to_sibling(block):
    count = lax.axis_size("seq")
    return lax.ppermute(block, "seq", [(i, i ^ 1) for i in range(count)])


def across(block, apart):
    count = lax.axis_size("seq")
    return lax.ppermute(block, "seq", [(i, i ^ (2 * apart)) for i in range(count)])


def after(block, *others):
    return lax.optimization_barrier((block, *others))


def kernel_call(
    body, out_shape, in_specs, out_specs, scratch, flops, moved, name, vmem_limit=VMEM_LIMIT
):
    return pl.pallas_call(
        body,
        out_shape=out_shape,
        in_specs=in_specs,
        out_specs=out_specs,
        scratch_shapes=scratch,
        compiler_params=pltpu.CompilerParams(vmem_limit_bytes=vmem_limit),
        cost_estimate=pl.CostEstimate(flops=flops, bytes_accessed=moved, transcendentals=0),
        name=name,
    )


def document_of(positions, lengths_ref):
    end = 0
    document = jnp.zeros_like(positions)
    for i in range(lengths_ref.shape[1]):
        end = end + lengths_ref[0, i]
        document += (positions >= end).astype(jnp.int32)
    return document


def prepare_kernel(
    offsets,
    dec_rows,
    enc_rows,
    in_any,
    target_any,
    grad_ref,
    out_ref,
    mask_ref,
    send_ref,
    keep_ref,
    docs_ref,
    in_ref,
    target_ref,
    grad_held,
    out_held,
    mask_held,
    sems,
):
    chip, core = position()
    rows = grad_ref.shape[0]
    copies = start_all(
        [
            (in_any, in_ref),
            (target_any, target_ref),
            (mask_ref, mask_held),
            (grad_ref, grad_held),
            (out_ref, out_held),
        ],
        sems,
    )
    for copy in copies[:3]:
        copy.wait()
    lane = lax.broadcasted_iota(jnp.int32, (1, docs_ref.shape[1]), 1)
    block = dec_rows // len(offsets)
    dec = lane + chip * block
    for j, offset in enumerate(offsets[1:], 1):
        dec = jnp.where(lane >= j * block, lane + ((chip ^ offset) - j) * block, dec)
    docs = [document_of(dec, target_ref)]
    for side in (core, 1 - core):
        docs.append(document_of(lane + (2 * chip + side) * enc_rows, in_ref))
    docs_ref[...] = jnp.concatenate(docs + docs + docs[:2], 0).astype(F32)
    mask_row = mask_held[...].astype(F32)
    here = lax.broadcasted_iota(jnp.int32, (rows, rows), 0) == lax.broadcasted_iota(
        jnp.int32, (rows, rows), 1
    )
    mask = jnp.sum(jnp.where(here, mask_row, 0.0), axis=1, keepdims=True)
    lane = lax.broadcasted_iota(jnp.int32, (rows, EXTRA), 1)
    for copy in copies[3:]:
        copy.wait()
    masked = grad_held[...].astype(F32) * mask
    products = masked * out_held[...].astype(F32)
    grad_held[...] = masked.astype(BF16)
    halves = []
    for half in range(2):
        extra = jnp.where(lane == HALF_HEADS, mask, 0.0)
        for head in range(HALF_HEADS):
            first = half * HALF + head * HEAD_SIZE
            delta = jnp.sum(products[:, first : first + HEAD_SIZE], axis=1, keepdims=True)
            extra = jnp.where(lane == head, delta, extra)
        halves.append(extra)
    for ref, half in ((send_ref, 1 - core), (keep_ref, core)):
        ref[:, :HALF] = grad_held[:, pl.ds(pl.multiple_of(half * HALF, HALF), HALF)]
        ref[:, HALF:] = jnp.where(half == 0, halves[0], halves[1]).astype(BF16)


def in_core_order(own, other, core):
    own, other = own.astype(F32), other.astype(F32)
    joined = jnp.where(
        core == 0, jnp.concatenate([own, other], 0), jnp.concatenate([other, own], 0)
    )
    return joined.astype(BF16)


def join_queries_kernel(own_ref, other_ref, joined_ref):
    _, core = position()
    mine = pl.ds(pl.multiple_of(core * HALF, HALF), HALF)
    joined_ref[...] = in_core_order(own_ref[:, mine], other_ref[:, mine], core)


def join_cotangents_kernel(own_ref, other_ref, joined_ref, delta_ref, count_ref):
    _, core = position()
    joined_ref[...] = in_core_order(own_ref[:, :HALF], other_ref[:, :HALF], core)
    extra = jnp.transpose(in_core_order(own_ref[:, HALF:], other_ref[:, HALF:], core).astype(F32))
    delta_ref[...] = extra[: delta_ref.shape[0]]
    count = jnp.sum(extra[HALF_HEADS : HALF_HEADS + 1], axis=1, keepdims=True)
    count_ref[...] = jnp.broadcast_to(count, count_ref.shape)


def split_kernel(rows_ref, own_ref, send_ref):
    _, core = position()
    for ref, half in ((own_ref, core), (send_ref, 1 - core)):
        ref[...] = rows_ref[:, pl.ds(pl.multiple_of(half * HALF, HALF), HALF)]


def setup_kernel(docs_ref, key_ref, k_ref, send_ref, bias_own, bias_other):
    split_kernel(key_ref, k_ref, send_ref)
    enc_rows, dec_rows = bias_own.shape
    dec = docs_ref[0:1, :dec_rows]
    columns = jnp.transpose(docs_ref[:, :enc_rows])
    for ref, column in ((bias_own, 1), (bias_other, 2)):
        ref[...] = jnp.where(columns[:, column : column + 1] == dec, 0.0, NEVER)


def start_all(pairs, sems):
    copies = [pltpu.make_async_copy(a, b, sems.at[i]) for i, (a, b) in enumerate(pairs)]
    for copy in copies:
        copy.start()
    return copies


def rows_of(blocks, head):
    columns = slice(head * HEAD_SIZE, (head + 1) * HEAD_SIZE)
    return jnp.concatenate([block[:, columns] for block in blocks], 0)


def value_columns_of(head):
    _, core = position()
    first = core * HALF + head * HEAD_SIZE
    return pl.ds(pl.multiple_of(first, HEAD_SIZE), HEAD_SIZE)


def columns_of(head):
    return slice(head * HEAD_SIZE, (head + 1) * HEAD_SIZE)


def scores_kernel(offsets, delta_ref, bias_own, bias_other, key_ref, other_ref, *refs):
    count_ref, refs = refs[0], refs[1:]
    blocks, (stats_ref,) = refs[: len(offsets)], refs[len(offsets) :]
    rows = blocks[0].shape[0]
    dec_rows = rows * len(offsets)
    stats_ref[...] = jnp.broadcast_to(count_ref[0:1, 0:1], stats_ref.shape)
    stats_ref[HALF_HEADS:, :rows] = delta_ref[:HALF_HEADS]
    for head in range(HALF_HEADS):
        q = rows_of(blocks, head)
        scores = [
            dot(k[:, columns_of(head)], q, NT) * ROOT + bias[...]
            for k, bias in ((key_ref, bias_own), (other_ref, bias_other))
        ]
        top = functools.reduce(jnp.maximum, [jnp.max(s, axis=0, keepdims=True) for s in scores])
        top = jnp.maximum(top, -1e20)
        total = sum(jnp.sum(jnp.exp(s - top), axis=0, keepdims=True) for s in scores)
        stats_ref[head : head + 1, :dec_rows] = jnp.where(
            total > 0, top + jnp.log(jnp.maximum(total, 1e-30)), NEVER
        )


def gathered_stats(offsets, stats, rows):
    logs = []
    for sender, ref in zip(offsets, stats):
        order = [offsets.index(offset ^ sender) for offset in offsets]
        logs.append(
            jnp.concatenate([ref[:HALF_HEADS, j * rows : (j + 1) * rows] for j in order], 1)
        )
    top = functools.reduce(jnp.maximum, logs)
    log_total = top + jnp.log(sum(jnp.exp(log - top) for log in logs))
    delta = jnp.concatenate([ref[HALF_HEADS:, :rows] for ref in stats], 1)
    last = stats[0].shape[1] - 1
    return log_total, delta, sum(ref[0:1, last:] for ref in stats)


def grads_kernel(offsets, bias_own, bias_other, *refs):
    chips = len(offsets)
    order = [0, *sorted(offsets[1:], reverse=True)]
    stats, refs = [refs[order.index(offset)] for offset in offsets], refs[chips:]
    q_blocks, refs = refs[:chips], refs[chips:]
    g_blocks, refs = refs[:chips], refs[chips:]
    (key_ref, key_other, value_ref, value_other), refs = refs[:4], refs[4:]
    dq_blocks, (keep_ref, send_ref, count_ref) = refs[:chips], refs[chips:]
    rows = q_blocks[0].shape[0]
    log_total, delta, count = gathered_stats(offsets, stats, rows)
    count_ref[...] = jnp.broadcast_to(count, count_ref.shape)
    for head in range(HALF_HEADS):
        columns = slice(head * HEAD_SIZE, (head + 1) * HEAD_SIZE)
        value_columns = slice(HALF + columns.start, HALF + columns.stop)
        line = slice(head, head + 1)
        q, g = rows_of(q_blocks, head), rows_of(g_blocks, head)
        dq = 0.0
        for key, value, bias, out_ref in (
            (key_ref, value_ref, bias_own, keep_ref),
            (key_other, value_other, bias_other, send_ref),
        ):
            k, v = key[:, columns], value[:, value_columns_of(head)]
            probs = jnp.exp(dot(k, q, NT) * ROOT + bias[...] - log_total[line])
            dscore = (probs * (dot(v, g, NT) - delta[line])).astype(BF16)
            dq += dot(dscore, k, TN)
            out_ref[:, columns] = (dot(dscore, q, NN) * ROOT).astype(BF16)
            out_ref[:, value_columns] = dot(probs.astype(BF16), g, NN).astype(BF16)
        dq = (dq * ROOT).astype(BF16)
        for j, block in enumerate(dq_blocks):
            block[:, columns] = dq[j * rows : (j + 1) * rows]


def key_end_kernel(rows_in_all, keep_ref, other_ref, *refs):
    counts, (dk_ref, dv_ref, factor_ref) = refs[:2], refs[2:]
    _, core = position()
    factor = rows_in_all / (counts[0][0:1, 0:1] + counts[1][0:1, 0:1])
    factor_ref[...] = jnp.broadcast_to(factor, factor_ref.shape)
    for ref, side in ((keep_ref, core), (other_ref, 1 - core)):
        columns = pl.ds(pl.multiple_of(side * HALF, HALF), HALF)
        dk_ref[:, columns] = (ref[:, :HALF].astype(F32) * factor).astype(BF16)
        dv_ref[:, columns] = (ref[:, HALF:].astype(F32) * factor).astype(BF16)


def query_end_kernel(factor_ref, *refs):
    parts, (send_ref, keep_ref) = refs[:-2], refs[-2:]
    _, core = position()
    summed = factor_ref[0:1, 0:1] * sum(part[...].astype(F32) for part in parts)
    half = summed.shape[0] // 2
    low, high = summed[:half], summed[half:]
    send_ref[...] = jnp.where(core == 0, high, low).astype(BF16)
    keep_ref[...] = jnp.where(core == 0, low, high).astype(BF16)


def in_order(own, other, core, axis):
    return jnp.where(
        core == 0, jnp.concatenate([own, other], axis), jnp.concatenate([other, own], axis)
    )


def local(queries, keys, values, attn_out, out_grad, loss_mask, input_lengths, target_lengths):
    query_rows, key_rows, value_rows = queries[0], keys[0], values[0]
    dec_local, enc_local = query_rows.shape[0], key_rows.shape[0]
    chips = lax.axis_size("seq") // 2
    data_groups = lax.axis_size("dp")
    _, core = position()
    dec_rows = 2 * chips * dec_local
    enc_rows = 2 * enc_local
    block = (2 * dec_local, HALF)
    lengths = (input_lengths[0], target_lengths[0])

    def shaped(*shape, dtype=BF16):
        return jax.ShapeDtypeStruct(shape, dtype)

    def gather(block):
        blocks = [block]
        apart = chips // 2
        while apart > 1:
            blocks += [across(one, apart) for one in blocks]
            apart //= 2
        return blocks, across(block, 1)

    def forwarded(blocks):
        return [across(one, 1) for one in blocks[1:]]

    offsets = [0]
    apart = chips // 2
    while apart:
        offsets += [offset ^ apart for offset in offsets]
        apart //= 2

    features = HEADS * HEAD_SIZE
    sent = shaped(dec_local, HALF + EXTRA)
    block = shaped(2 * dec_local, HALF)

    with jax.named_scope("sibling_exchange"):
        q_recv = to_sibling(query_rows)
        docs = shaped(8, pl.cdiv(max(dec_rows, enc_local), 128) * 128, dtype=F32)
        g_send, g_keep, docs = kernel_call(
            functools.partial(prepare_kernel, offsets, dec_rows, enc_local),
            (sent, sent, docs),
            [ANY] * 5,
            (VMEM, VMEM, VMEM),
            [
                pltpu.SMEM(lengths[0].shape, jnp.int32),
                pltpu.SMEM(lengths[1].shape, jnp.int32),
                pltpu.VMEM((dec_local, features), BF16),
                pltpu.VMEM((dec_local, features), BF16),
                pltpu.VMEM((1, dec_local), jnp.int32),
                pltpu.SemaphoreType.DMA((5,)),
            ],
            10**5,
            10**6,
            "prepare",
            60 * 1024 * 1024,
        )(*lengths, out_grad[0], attn_out[0], loss_mask)
        g_recv = to_sibling(g_send)

    with jax.named_scope("query_gather"):
        q_recv, _ = after(q_recv, g_keep)
        q_block = kernel_call(
            join_queries_kernel, block, [VMEM, VMEM], VMEM, [], 10**5, 10**5, "join_queries"
        )(query_rows, q_recv)
        q_far, q_near = gather(q_block)

    with jax.named_scope("setup"):
        half_rows = shaped(enc_local, HALF)
        bias = shaped(enc_local, dec_rows, dtype=F32)
        k_own, k_send, bias_own, bias_other = kernel_call(
            setup_kernel,
            (half_rows, half_rows, bias, bias),
            [VMEM] * 2,
            (VMEM,) * 4,
            [],
            10**6,
            2**22,
            "setup",
        )(docs, after(key_rows, q_block)[0])

    with jax.named_scope("cotangent_gather"):
        small = shaped(8, 2 * dec_local, dtype=F32)
        g_block, delta, count = kernel_call(
            join_cotangents_kernel,
            (block, small, shaped(8, EXTRA, dtype=F32)),
            [VMEM, VMEM],
            (VMEM,) * 3,
            [],
            10**5,
            10**5,
            "join_cotangents",
        )(g_keep, g_recv)

    def over_groups(count, apart):
        return lax.ppermute(count, "dp", [(i, i ^ apart) for i in range(data_groups)])

    with jax.named_scope("mask_count"):
        apart = 1
        while apart < data_groups // 2:
            count = count + after(over_groups(count, apart), bias_own)[0]
            apart *= 2
        rows_in_all = float(data_groups * dec_rows)

    with jax.named_scope("query_forward"):
        q_far = [q_far[0], *(after(one, bias_own, count)[0] for one in q_far[1:])]
        q_blocks = [*q_far, q_near, *forwarded(q_far)]

    with jax.named_scope("cotangent_gather"):
        sent = after(g_block, *q_far, q_near)[0]
        g_blocks = [g_block] + [across(sent, offset) for offset in offsets[1:]]

    with jax.named_scope("key_exchange"):
        v_recv = to_sibling(after(value_rows, q_recv)[0])
        k_send, v_recv, *_ = after(k_send, v_recv, *q_far, q_near)
        k_recv = to_sibling(k_send)

    with jax.named_scope("scores"):
        width = (dec_rows // 128 + 1) * 128
        stats = kernel_call(
            functools.partial(scores_kernel, offsets),
            shaped(2 * HALF_HEADS, width, dtype=F32),
            [VMEM] * (chips + 6),
            VMEM,
            [],
            2 * dec_rows * enc_rows * HALF,
            2 * (dec_rows + enc_rows) * HALF,
            "scores",
        )(delta, bias_own, bias_other, k_own, k_recv, count, *q_blocks)

    with jax.named_scope("stats_exchange"):
        order = [0, *sorted(offsets[1:], reverse=True)]
        all_stats = [stats] + [across(stats, offset) for offset in order[1:]]

    with jax.named_scope("grads"):
        both = shaped(enc_local, 2 * HALF)
        *dq_blocks, dkv_keep, dkv_send, count = kernel_call(
            functools.partial(grads_kernel, offsets),
            (block,) * chips + (both, both, shaped(8, EXTRA, dtype=F32)),
            [VMEM] * (3 * chips + 6),
            (VMEM,) * (chips + 3),
            [],
            10 * dec_rows * enc_rows * HALF,
            4 * (dec_rows + 2 * enc_rows) * HALF,
            "grads",
        )(bias_own, bias_other, *all_stats, *q_blocks, *g_blocks, k_own, k_recv, value_rows, v_recv)

    with jax.named_scope("query_grad_sum"):
        parts = [dq_blocks[0]]
        for j in sorted(range(1, chips), key=lambda j: (offsets[j] == 1, offsets[j])):
            parts.append(across(dq_blocks[j], offsets[j]))

    with jax.named_scope("key_grad_end"):
        dkv_recv = to_sibling(dkv_send)
        counts = (count, over_groups(count, data_groups // 2))
        whole = shaped(enc_local, features)
        grad_keys, grad_values, factor = kernel_call(
            functools.partial(key_end_kernel, rows_in_all),
            (whole, whole, shaped(8, EXTRA, dtype=F32)),
            [VMEM] * 4,
            (VMEM, VMEM, VMEM),
            [],
            10**6,
            2**22,
            "key_end",
        )(dkv_keep, dkv_recv, *counts)

    with jax.named_scope("query_grad_end"):
        half = shaped(dec_local, HALF)
        dq_send, dq_keep = kernel_call(
            query_end_kernel,
            (half, half),
            [VMEM] * (chips + 1),
            (VMEM, VMEM),
            [],
            10**5,
            10**6,
            "query_end",
        )(factor, *parts)
        grad_queries = in_order(dq_keep, to_sibling(dq_send), core, 1)

    return grad_queries[None], grad_keys[None], grad_values[None]


def solution(mesh):
    return jax.shard_map(
        local,
        mesh=mesh,
        in_specs=(
            P("dp", "seq", None),
            P("dp", "seq", None),
            P("dp", "seq", None),
            P("dp", "seq", None),
            P("dp", "seq", None),
            P("dp", "seq"),
            P("dp", None, None),
            P("dp", None, None),
        ),
        out_specs=(P("dp", "seq", None), P("dp", "seq", None), P("dp", "seq", None)),
        check_vma=False,
    )
```
